32 devices in a mesh: ctx: 8 (over y, x, core), fsdp: 4 (over z).
Axes of the slice: x: 2, y: 2, z: 4, core: 2. Of those that a mesh axis runs over, the one named last changes fastest.
Arguments:
- tokens: bfloat16 [4, 1024, 1280], P('fsdp', 'ctx'), may hold values from -6 to 6
- documents: int32 [4, 1024], P('fsdp', 'ctx'), may hold values from 0 to 1, as said below
- routes: int32 [4, 1024, 7], P('fsdp', 'ctx'), may hold values from 0 to 15, all different within a row
- priority: int32 [4, 8, 128], P('fsdp', 'ctx'), may hold values from 0 to 127, each once within a row
- attention_gain: bfloat16 [1280], P('fsdp'), may hold values from 0.5 to 1.5
- query_weight: bfloat16 [1280, 1280], P('fsdp'), may hold values from -0.25 to 0.25
- key_weight: bfloat16 [1280, 1280], P('fsdp'), may hold values from -0.25 to 0.25
- value_weight: bfloat16 [1280, 1280], P('fsdp'), may hold values from -0.15625 to 0.15625
- output_weight: bfloat16 [1280, 1280], P('fsdp'), may hold values from -1.25 to 1.25
- feedforward_gain: bfloat16 [1280], P('fsdp'), may hold values from 0.5 to 1.5
- router_weight: bfloat16 [1280, 16], P('fsdp'), may hold values from -0.078125 to 0.078125
- shared_gate: bfloat16 [1280, 896], P('fsdp'), may hold values from -0.15625 to 0.15625
- shared_up: bfloat16 [1280, 896], P('fsdp'), may hold values from -0.15625 to 0.15625
- shared_down: bfloat16 [896, 1280], P('fsdp'), may hold values from -0.1875 to 0.1875
- expert_gate: bfloat16 [16, 1280, 896], P('ctx', 'fsdp'), may hold values from -0.15625 to 0.15625
- expert_up: bfloat16 [16, 1280, 896], P('ctx', 'fsdp'), may hold values from -0.15625 to 0.15625
- expert_down: bfloat16 [16, 896, 1280], P('ctx', 'fsdp'), may hold values from -2 to 2
- cotangent: bfloat16 [4, 1024, 1280], P('fsdp', 'ctx'), may hold values from -6 to 6
Outputs:
- output: bfloat16 [4, 1024, 1280], P('fsdp', 'ctx')
- grad_tokens: bfloat16 [4, 1024, 1280], P('fsdp', 'ctx')
- grad_attention_gain: float32 [1280], P('fsdp')
- grad_query_weight: float32 [1280, 1280], P('fsdp')
- grad_key_weight: float32 [1280, 1280], P('fsdp')
- grad_value_weight: float32 [1280, 1280], P('fsdp')
- grad_output_weight: float32 [1280, 1280], P('fsdp')
- grad_feedforward_gain: float32 [1280], P('fsdp')
- grad_router_weight: float32 [1280, 16], P('fsdp')
- grad_shared_gate: float32 [1280, 896], P('fsdp')
- grad_shared_up: float32 [1280, 896], P('fsdp')
- grad_shared_down: float32 [896, 1280], P('fsdp')
- grad_expert_gate: float32 [16, 1280, 896], P('ctx', 'fsdp')
- grad_expert_up: float32 [16, 1280, 896], P('ctx', 'fsdp')
- grad_expert_down: float32 [16, 896, 1280], P('ctx', 'fsdp')
The draws below stay inside these ranges and needn't reach their ends.
Inputs may be any that keep to these rules, and one draw needn't show every extreme that they name: In each packed sequence the documents are 0 up to a boundary and 1 after it, both present; one of the two lies within the first or the last 128 positions. `routes`: each token names 7 different experts. `priority`: each block of 128 tokens holds every number once.
All inputs are finite; a program needn't handle non-finite values.
Results may differ from the reference program's by a relative error of at most 0.025.
Values may be sent and summed in bfloat16 or wider, within the bound.
A program may use at most 320 MiB of HBM per device.

```python
import jax
import jax.numpy as jnp
from jax import lax

D = 1280
HEADS = 10
HEAD_DIM = 128
FF = 896
TOPK = 7
SEQ_DEV = 128
AW = 1280
EXPERTS = 16
ROW = 1024
ROWS = 4
CAP = 63
N_CTX = 8


def draw_documents(key, part):
    side_key, cut_key = jax.random.split(key)
    sides = jax.random.randint(side_key, (ROWS, 1), 0, 2)
    cutting = jax.random.randint(cut_key, (ROWS, 1), 1, SEQ_DEV)
    boundary = jnp.where(sides == 0, cutting, ROW - cutting)
    places = jnp.arange(ROW, dtype=jnp.int32)[None, :]
    return (places >= boundary).astype(jnp.int32)


def level_of(own_key, extent, cuts, smallest, largest):
    def one(position, parts):
        steps = jax.random.uniform(jax.random.fold_in(jax.random.fold_in(own_key, 6), position), (parts,), jnp.float32, smallest / len(cuts), largest / len(cuts))
        return jnp.repeat(jnp.exp(steps), extent[position] // parts).reshape((-1,) + (1,) * (len(extent) - position - 1))

    factor_of = one(*cuts[0])
    for cut in cuts[1:]:
        factor_of = factor_of * one(*cut)
    return factor_of


def choose_distinct(own_key, rows, count, top, lift):
    sequence = jax.random.permutation(jax.random.fold_in(own_key, 1), count)
    boost = sequence
    for power in range(3):
        boost = boost * boost // count
    boost = boost * lift // count
    tickets = jax.random.randint(jax.random.fold_in(own_key, 2), (rows, count), 0, 4096) + boost
    sure = jax.random.permutation(jax.random.fold_in(own_key, 3), rows)[jnp.arange(count) % rows]
    tickets = jnp.where(jnp.arange(rows)[:, None] == sure[None, :], 1 << 14, tickets)
    merit = tickets * count + jnp.arange(count)
    return lax.top_k(merit.astype(jnp.int32), top)[1].astype(jnp.int32)


def gaussian(stream_key, extent, deviation, limit, cuts=(), kind=jnp.bfloat16):
    values = jax.random.normal(stream_key, extent, jnp.float32) * deviation
    if len(cuts) > 0:
        values = level_of(stream_key, extent, cuts, -0.22, 0.18) * values
    return jnp.clip(values, min=-limit, max=limit).astype(kind)


def setup_inputs(seed: int = 0) -> dict:
    splits = jax.random.split(jax.random.key(seed), 19)
    return {
        "tokens": gaussian(splits[0], (ROWS, ROW, D), 1.0, 6.0, ((0, 4), (1, 8))),
        "documents": draw_documents(jax.random.fold_in(splits[18], 71), 0),
        "routes": choose_distinct(splits[2], ROWS * ROW, EXPERTS, TOPK, 3584).reshape((ROWS, ROW, TOPK)),
        "priority": jax.vmap(lambda own: jax.random.permutation(own, SEQ_DEV))(jax.random.split(splits[3], ROWS * N_CTX)).reshape((ROWS, N_CTX, SEQ_DEV)).astype(jnp.int32),
        "attention_gain": jnp.clip(1.0 + 0.1 * jax.random.normal(splits[4], (D,), jnp.float32), 0.5, 1.5).astype(jnp.bfloat16),
        "query_weight": gaussian(splits[5], (D, AW), (D // 2) ** -0.5, 0.25, ((0, 4),)),
        "key_weight": gaussian(splits[6], (D, AW), (D // 2) ** -0.5, 0.25, ((0, 4),)),
        "value_weight": gaussian(splits[7], (D, AW), D ** -0.5, 0.15625, ((0, 4),)),
        "output_weight": gaussian(splits[8], (AW, D), (max(AW // 64, 1)) ** -0.5, 1.25, ((0, 4),)),
        "feedforward_gain": jnp.clip(1.0 + 0.1 * jax.random.normal(splits[9], (D,), jnp.float32), 0.5, 1.5).astype(jnp.bfloat16),
        "router_weight": gaussian(splits[10], (D, EXPERTS), (4 * D) ** -0.5, 0.078125, ((0, 4),)),
        "shared_gate": gaussian(splits[11], (D, FF), D ** -0.5, 0.15625, ((0, 4),)),
        "shared_up": gaussian(splits[12], (D, FF), D ** -0.5, 0.15625, ((0, 4),)),
        "shared_down": gaussian(splits[13], (FF, D), FF ** -0.5, 0.1875, ((0, 4),)),
        "expert_gate": gaussian(splits[14], (EXPERTS, D, FF), D ** -0.5, 0.15625, ((0, 8), (1, 4))),
        "expert_up": gaussian(splits[15], (EXPERTS, D, FF), D ** -0.5, 0.15625, ((0, 8), (1, 4))),
        "expert_down": gaussian(splits[16], (EXPERTS, FF, D), (max(FF * 5 // (2 * EXPERTS * EXPERTS), 1)) ** -0.5, 2.0, ((0, 8), (1, 4))),
        "cotangent": gaussian(splits[17], (ROWS, ROW, D), 1.0, 6.0, ((0, 4), (1, 8))),
    }


epsilon = 1e-06
theta_base = 10000.0
negative = -1e+30
highest = lax.Precision.HIGHEST

@jax.custom_vjp
def low(v):
    return lax.optimization_barrier(v.astype(jnp.bfloat16)).astype(jnp.float32)

@jax.custom_vjp
def low_back(v):
    return v

def low_keep(v):
    return (low(v), None)

def low_pass(kept, grad):
    return (grad,)

def back_keep(v):
    return (v, None)

def back_low(kept, grad):
    return (low(grad),)
low.defvjp(low_keep, low_pass)
low_back.defvjp(back_keep, back_low)

def product(left, right):
    return jnp.dot(left, right, precision=highest, preferred_element_type=jnp.float32)

def normalize(values, gain):
    return values * lax.rsqrt(lax.optimization_barrier(jnp.mean(values * values, axis=-1, keepdims=True)) + epsilon) * gain

def silu(values):
    return values * jax.nn.sigmoid(values)

def rotary(values, positions):
    half_dim = HEAD_DIM // 2
    frequency = theta_base ** (-jnp.arange(half_dim, dtype=jnp.float32) / half_dim)
    angles = positions.astype(jnp.float32)[:, None] * frequency[None, :]
    cosine = jnp.cos(angles)[:, None, :]
    sine = jnp.sin(angles)[:, None, :]
    leading = values[..., :half_dim]
    trailing = values[..., half_dim:]
    return jnp.concatenate([leading * cosine - trailing * sine, trailing * cosine + leading * sine], axis=-1)

def sequence_layer(inputs, documents, routes, priority, params):
    attention_gain, query_weight, key_weight, value_weight, output_weight, feedforward_gain, router_weight, shared_gate, shared_up, shared_down, expert_gate, expert_up, expert_down = params
    positions = jnp.arange(ROW, dtype=jnp.int32)
    normed = low(normalize(inputs, attention_gain))
    query_pre = low_back(product(normed, query_weight)).reshape(ROW, HEADS, HEAD_DIM)
    key_pre = low_back(product(normed, key_weight)).reshape(ROW, HEADS, HEAD_DIM)
    queries = low_back(low(rotary(query_pre, positions)))
    key_rows = low_back(low(rotary(key_pre, positions)))
    value_rows = low_back(low(product(normed, value_weight))).reshape(ROW, HEADS, HEAD_DIM)
    block_rows = min(512, ROW)
    score_scale = HEAD_DIM ** (-0.5)

    def attend(number):
        offset = (number * block_rows).astype(jnp.int32)
        query_block = lax.dynamic_slice_in_dim(queries, offset, block_rows, 0)
        query_docs = lax.dynamic_slice_in_dim(documents, offset, block_rows, 0)
        query_pos = offset + jnp.arange(block_rows, dtype=jnp.int32)
        raw_scores = low_back(jnp.einsum('qhd,khd->hqk', query_block, key_rows, precision=highest))
        allowed = (positions[None, :] <= query_pos[:, None]) & (documents[None, :] == query_docs[:, None])
        scores = jnp.where(allowed[None], raw_scores * score_scale, negative)
        shares = low(jax.nn.softmax(scores, axis=-1))
        return jnp.einsum('hqk,khd->qhd', shares, value_rows, precision=highest)
    attended = lax.map(jax.checkpoint(attend), jnp.arange(ROW // block_rows, dtype=jnp.int32)).reshape(ROW, AW)
    mixed_rows = low_back(low(attended))
    hidden = inputs + low_back(product(mixed_rows, output_weight))
    moe_input = low(normalize(hidden, feedforward_gain))
    gate_probs = jax.nn.softmax(product(moe_input, router_weight), axis=-1)
    shared_gate_act = low_back(product(moe_input, shared_gate))
    shared_up_act = low_back(product(moe_input, shared_up))
    shared_out = low_back(product(low(silu(shared_gate_act) * shared_up_act), shared_down))
    blocks = routes.reshape(N_CTX, SEQ_DEV, TOPK)
    onehot = (blocks[..., None] == jnp.arange(EXPERTS, dtype=jnp.int32)).astype(jnp.int32)
    counts = lax.optimization_barrier(jnp.sum(onehot, axis=2))
    earlier = (priority[:, None, :] < priority[:, :, None]).astype(jnp.int32)
    before = jnp.einsum('cts,cse->cte', earlier, counts)
    ranking = lax.optimization_barrier(jnp.sum(onehot * before[:, :, None, :], axis=-1))
    kept_mask = ranking < CAP
    source = jnp.arange(N_CTX, dtype=jnp.int32)[:, None, None]
    inside = source * CAP + ranking
    chosen = lax.optimization_barrier(jnp.sum(onehot.astype(jnp.float32) * gate_probs.reshape(N_CTX, SEQ_DEV, 1, EXPERTS), axis=-1))
    weight = jnp.where(kept_mask, chosen, 0.0)

    def run_expert(item):
        gate_w, up_w, down_w, expert_id = item
        match = (blocks == expert_id) & kept_mask
        found = jnp.any(match, axis=-1)
        located = lax.optimization_barrier(jnp.sum(jnp.where(match, inside, 0), axis=-1))
        target = jnp.where(found, located, N_CTX * CAP).reshape(ROW).astype(jnp.int32)
        rows_in = jnp.zeros((N_CTX * CAP + 1, D), jnp.float32).at[target].set(moe_input)[:N_CTX * CAP]
        rows_in = low_back(rows_in)
        gate_act = low_back(product(rows_in, gate_w))
        up_act = low_back(product(rows_in, up_w))
        expert_hidden = low(silu(gate_act) * up_act)
        return low_back(low(product(expert_hidden, down_w)))
    outputs = lax.map(jax.checkpoint(run_expert), (expert_gate, expert_up, expert_down, jnp.arange(EXPERTS, dtype=jnp.int32)))
    out_table = jnp.concatenate([outputs.reshape(EXPERTS * N_CTX * CAP, D), jnp.zeros((1, D), jnp.float32)], axis=0)
    flat_index = jnp.where(kept_mask, blocks * (N_CTX * CAP) + inside, EXPERTS * N_CTX * CAP).reshape(ROW, TOPK).astype(jnp.int32)
    weight = weight.reshape(ROW, TOPK)
    routed = jnp.zeros((ROW, D), jnp.float32)
    for column in range(TOPK):
        routed = routed + weight[:, column, None] * out_table[flat_index[:, column]]
    return hidden + shared_out + routed

def reference(tokens, documents, routes, priority, attention_gain, query_weight, key_weight, value_weight, output_weight, feedforward_gain, router_weight, shared_gate, shared_up, shared_down, expert_gate, expert_up, expert_down, cotangent):
    params = (attention_gain.astype(jnp.float32), query_weight.astype(jnp.float32), key_weight.astype(jnp.float32), value_weight.astype(jnp.float32), output_weight.astype(jnp.float32), feedforward_gain.astype(jnp.float32), router_weight.astype(jnp.float32), shared_gate.astype(jnp.float32), shared_up.astype(jnp.float32), shared_down.astype(jnp.float32), expert_gate.astype(jnp.float32), expert_up.astype(jnp.float32), expert_down.astype(jnp.float32))

    def forward(inputs, weights):

        def one_row(item):
            return sequence_layer(item[0], item[1], item[2], item[3], weights)
        return lax.map(jax.checkpoint(one_row), (inputs, documents, routes, priority))
    result, pullback = jax.vjp(forward, tokens.astype(jnp.float32), params)
    grad_inputs, grads = pullback(cotangent.astype(jnp.float32))
    return (result.astype(jnp.bfloat16), grad_inputs.astype(jnp.bfloat16), grads[0], grads[1], grads[2], grads[3], grads[4], grads[5], grads[6], grads[7], grads[8], grads[9], grads[10], grads[11], grads[12])
```

```python
import math

import jax
import jax.numpy as jnp
from jax import lax
from jax.experimental import pallas as pl
from jax.experimental.pallas import tpu as pltpu
from jax.sharding import PartitionSpec as P

D = 1280
HEADS = 10
HEAD_DIM = 128
TOPK = 7
EXP_DEV = 2


epsilon = 1e-06
theta_base = 10000.0
negative = -1e30
highest = lax.Precision.HIGHEST


def rotary_tables(positions, half_dim):
    frequency = theta_base ** (-jnp.arange(half_dim, dtype=jnp.float32) / half_dim)
    angles = positions.astype(jnp.float32)[:, None] * frequency[None, :]
    return (jnp.cos(angles)[:, None, :], jnp.sin(angles)[:, None, :])


def rotate(values, cosine, sine):
    half_dim = values.shape[-1] // 2
    leading = values[..., :half_dim]
    trailing = values[..., half_dim:]
    return jnp.concatenate(
        [leading * cosine - trailing * sine, trailing * cosine + leading * sine], axis=-1
    )


def unrotate(values, cosine, sine):
    half_dim = values.shape[-1] // 2
    leading = values[..., :half_dim]
    trailing = values[..., half_dim:]
    return jnp.concatenate(
        [leading * cosine + trailing * sine, trailing * cosine - leading * sine], axis=-1
    )


def blockwise(count, visit, initial):
    rows_each = math.gcd(count, 512)

    def advance(progress, number):
        return (visit(progress, number * rows_each, rows_each), None)

    final, ignored = lax.scan(advance, initial, jnp.arange(count // rows_each, dtype=jnp.int32))
    return final


def allowed_mask(query_pos, query_docs, key_pos, key_docs):
    return (key_pos[None, :] <= query_pos[:, None]) & (key_docs[None, :] == query_docs[:, None])


def rms_factor(values):
    return lax.rsqrt(jnp.mean(values * values, axis=-1, keepdims=True) + epsilon)


def silu_parts(values):
    sigma = jax.nn.sigmoid(values)
    return (values * sigma, sigma * (1.0 + values * (1.0 - sigma)))


def unchanged(progress):
    return progress


NZ = 4
SLOTS = 64
WIDE = 256
MESH = pl.DeviceIdType.MESH
PEERS = ((0, 1), (1, 0), (1, 1))
NN = (((1,), (0,)), ((), ()))
NT = (((1,), (1,)), ((), ()))
TN = (((0,), (0,)), ((), ()))


def dot(left, right, dims=NN):
    return lax.dot_general(left, right, dims, preferred_element_type=jnp.float32)


def flip(c, fy, fx, fk):
    return 4 * ((c // 4 + fy) % 2) + 2 * (((c // 2) % 2 + fx) % 2) + (c % 2 + fk) % 2


def remote(src, dst, send, recv, c, z):
    return pltpu.make_async_remote_copy(
        src_ref=src, dst_ref=dst, send_sem=send, recv_sem=recv, device_id=(c, z), device_id_type=MESH
    )


def greet(c, z):
    barrier = pltpu.get_barrier_semaphore()
    peers = [(c, (z + d) % NZ) for d in range(1, NZ)]
    peers += [(flip(c, fy, fx, 0), z) for fy, fx in PEERS] + [(flip(c, 0, 0, 1), z)]
    for peer in peers:
        pl.semaphore_signal(barrier, inc=1, device_id=peer, device_id_type=MESH)
    pl.semaphore_wait(barrier, len(peers))


class Spread:
    def __init__(self, src, dst, sems, c, z):
        self.src, self.dst, self.c, self.z = src, dst, c, z
        self.local, self.zs, self.zr, self.xs, self.xr, self.ms, self.mr = sems

    def block(self, c, d):
        return self.dst.at[c, (self.z + NZ - d) % NZ]

    def zcopy(self, d):
        return remote(
            self.src, self.dst.at[self.c, self.z], self.zs.at[d - 1], self.zr.at[d - 1], self.c, (self.z + d) % NZ
        )

    def zwait(self, d):
        block = self.block(self.c, d)
        remote(block, block, self.zs.at[d - 1], self.zr.at[d - 1], self.c, self.z).wait_recv()

    def xcopy(self, i, d):
        src = self.src if d == 0 else self.block(self.c, d)
        fy, fx = PEERS[i]
        return remote(
            src, self.block(self.c, d), self.xs.at[i, d], self.xr.at[i, d], flip(self.c, fy, fx, 0), self.z
        )

    def xwait(self, i, d):
        fy, fx = PEERS[i]
        block = self.block(flip(self.c, fy, fx, 0), d)
        remote(block, block, self.xs.at[i, d], self.xr.at[i, d], self.c, self.z).wait_recv()

    def mcopy(self, i, d):
        fy, fx = (((0, 0),) + PEERS)[i]
        block = self.block(flip(self.c, fy, fx, 0), d)
        src = self.src if (i == 0 and d == 0) else block
        return remote(src, block, self.ms.at[i, d], self.mr.at[i, d], flip(self.c, 0, 0, 1), self.z)

    def mwait(self, i, d):
        fy, fx = (((0, 0),) + PEERS)[i]
        block = self.block(flip(self.c, fy, fx, 1), d)
        remote(block, block, self.ms.at[i, d], self.mr.at[i, d], self.c, self.z).wait_recv()

    def start(self):
        self.own = pltpu.make_async_copy(self.src, self.dst.at[self.c, self.z], self.local)
        self.own.start()
        for d in range(1, NZ):
            self.zcopy(d).start()
        for i in range(3):
            self.xcopy(i, 0).start()
        self.mcopy(0, 0).start()

    def relay_z(self):
        for d in range(1, NZ):
            self.zwait(d)
            for i in range(3):
                self.xcopy(i, d).start()
            self.mcopy(0, d).start()

    def relay_x(self):
        for d in range(NZ):
            for i in range(3):
                self.xwait(i, d)
                self.mcopy(i + 1, d).start()

    def finish(self):
        self.own.wait()
        for d in range(NZ):
            for i in range(4):
                self.mwait(i, d)
        for d in range(1, NZ):
            self.zcopy(d).wait_send()
        for d in range(NZ):
            for i in range(3):
                self.xcopy(i, d).wait_send()
            for i in range(4):
                self.mcopy(i, d).wait_send()


def spread_sems():
    dma = pltpu.SemaphoreType.DMA
    return [dma, dma((3,)), dma((3,)), dma((3, NZ)), dma((3, NZ)), dma((4, NZ)), dma((4, NZ))]


def swish(values):
    sigma = 1.0 / (1.0 + jnp.exp(-values))
    return values * sigma, sigma * (1.0 + values * (1.0 - sigma))


def expert_kernel(
    b_ref, t_ref, g_ref, wsend_ref, wdn_ref,
    y_ref, db_ref, dg_ref, dgu_ref, ddn_ref, dsgu_ref, dsdn_ref, ball, tall, gall, mrecv, xrecv,
    wgu, acc, bg, gg, tg, oh, xs, gs, ys, ds, st, ld, zbuf, zrecv, gst,
    sb0, sb1, sb2, sb3, sb4, sb5, sb6, sg0, sg1, sg2, sg3, sg4, sg5, sg6, st0, st1, st2, st3, st4, st5, st6,
    wl, wss, wrs, lsem, ms, mr, xs_s, xs_r, ldsem, zs, zr, gl, gss, grs,
):
    c = lax.axis_index("ctx")
    z = lax.axis_index("fsdp")
    f32, bf16 = jnp.float32, jnp.bfloat16
    mate = flip(c, 0, 0, 1)
    length = b_ref.shape[0]
    group = NZ * length
    rows = wgu.shape[1] // NZ
    greet(c, z)
    spread_b = Spread(b_ref, ball, (sb0, sb1, sb2, sb3, sb4, sb5, sb6), c, z)
    spread_t = Spread(t_ref, tall, (st0, st1, st2, st3, st4, st5, st6), c, z)
    spread_g = Spread(g_ref, gall, (sg0, sg1, sg2, sg3, sg4, sg5, sg6), c, z)

    def wcopy(d):
        there = (z + d) % NZ
        return remote(
            wsend_ref.at[there], wgu.at[:, pl.ds(pl.multiple_of(z * rows, rows), rows), :],
            wss.at[d - 1], wrs.at[d - 1], c, there,
        )

    def wwait(d):
        here = wgu.at[:, pl.ds(pl.multiple_of((z + NZ - d) % NZ * rows, rows), rows), :]
        remote(wsend_ref.at[0], here, wss.at[d - 1], wrs.at[d - 1], c, z).wait_recv()

    wown = pltpu.make_async_copy(wsend_ref.at[z], wgu.at[:, pl.ds(pl.multiple_of(z * rows, rows), rows), :], wl)
    spread_t.start()
    spread_b.start()
    spread_g.start()
    wown.start()
    for d in range(1, NZ):
        wcopy(d).start()
    acc[...] = jnp.zeros_like(acc)
    ddn_ref[...] = jnp.zeros_like(ddn_ref)
    st[...] = jnp.zeros_like(st)
    zbuf[...] = jnp.zeros_like(zbuf)
    spread_t.relay_z()
    spread_b.relay_z()
    spread_t.relay_x()
    spread_b.relay_x()
    spread_g.relay_z()
    spread_g.relay_x()
    spread_t.finish()
    spread_b.finish()
    spread_g.finish()
    wown.wait()
    for d in range(1, NZ):
        wwait(d)

    def target(g):
        left = 3 - g // 2
        return flip(c, left % 2, left // 2, 1 - g % 2)

    def loads(g):
        slot = g % 2
        there = target(g)
        return (
            pltpu.make_async_copy(ball.at[there], bg.at[slot], lsem.at[slot, 0]),
            pltpu.make_async_copy(gall.at[there], gg.at[slot], lsem.at[slot, 1]),
            pltpu.make_async_copy(tall.at[there], tg.at[slot], lsem.at[slot, 2]),
        )

    def to_mate(s):
        return remote(st.at[0], mrecv.at[s], ms.at[s], mr.at[s], mate, z)

    def to_chip(s):
        left = 3 - s
        return remote(st.at[1], xrecv.at[s], xs_s.at[s], xs_r.at[s], flip(c, left % 2, left // 2, 0), z)

    for copy in loads(0):
        copy.start()
    slot_ids = lax.broadcasted_iota(jnp.int32, (SLOTS, length), 0).astype(f32)
    row_ids = lax.broadcasted_iota(jnp.int32, (16, length), 0)
    table_rows = lax.broadcasted_iota(jnp.int32, (16, 2 * length), 0)

    def step(g, carry):
        slot = g % 2
        s = g // 2
        par = g % 2
        for copy in loads(g):
            copy.wait()

        @pl.when(g < 7)
        def _():
            for copy in loads(g + 1):
                copy.start()

        @pl.when((s > 0) & (par == 0))
        def _():
            to_mate(s - 1).wait_send()

        @pl.when((s > 0) & (par == 1))
        def _():
            to_chip(s - 1).wait_send()

        scales = [[], []]
        for q in range(NZ):
            hits = []
            for e in range(2):
                mine = jnp.sum(jnp.where(table_rows == 2 * c + e, tg[slot, q], 0.0), axis=0, keepdims=True)
                rank = mine[:, :length]
                share = mine[:, length:]
                hit = slot_ids == rank
                scales[e].append(jnp.sum(jnp.where(hit, share, 0.0), axis=1, keepdims=True))
                hits.append(jnp.where(hit, 1.0, 0.0))
            hot = jnp.concatenate(hits, axis=0).astype(bf16)
            oh[q] = hot
            part = dot(hot, bg[slot, q]).astype(bf16)
            xs[0, q * SLOTS : (q + 1) * SLOTS] = part[:SLOTS]
            xs[1, q * SLOTS : (q + 1) * SLOTS] = part[SLOTS:]
            part = dot(hot, gg[slot, q]).astype(bf16)
            gs[0, q * SLOTS : (q + 1) * SLOTS] = part[:SLOTS]
            gs[1, q * SLOTS : (q + 1) * SLOTS] = part[SLOTS:]
        back = [0.0] * NZ
        for e in range(2):
            scale = jnp.concatenate(scales[e], axis=0)
            both = dot(xs[e], wgu[e])
            up = both[:, WIDE:]
            silu, slope = swish(both[:, :WIDE])
            inner = (silu * up).astype(bf16)
            scaled = (inner.astype(f32) * scale).astype(bf16)
            out = dot(scaled, wdn_ref[e]).astype(bf16)
            pull = dot(gs[e], wdn_ref[e], NT)
            gain = jnp.sum(inner.astype(f32) * pull, axis=1, keepdims=True)
            pull = pull * scale
            turn = jnp.concatenate([(pull * up * slope).astype(bf16), (pull * silu).astype(bf16)], axis=1)
            ddn_ref[e] += dot(scaled, gs[e], TN)
            acc[e] += dot(xs[e], turn, TN)
            into = dot(turn, wgu[e], NT).astype(bf16)
            for q in range(NZ):
                part = slice(q * SLOTS, (q + 1) * SLOTS)
                ys[q, e * SLOTS : (e + 1) * SLOTS] = out[part]
                ds[q, e * SLOTS : (e + 1) * SLOTS] = into[part]
                hit = oh[q, e * SLOTS : (e + 1) * SLOTS].astype(f32)
                line = jnp.sum(hit * gain[part], axis=0, keepdims=True)
                back[q] = back[q] + jnp.where(row_ids == 2 * c + e, line, 0.0)
        for q in range(NZ):
            st[par, q * length : (q + 1) * length] = dot(oh[q], ds[q], TN).astype(bf16)
            st[par, group + q * length : group + (q + 1) * length] = dot(oh[q], ys[q], TN).astype(bf16)
            st[par, 2 * group :, q * length : (q + 1) * length] = back[q].astype(bf16)

        @pl.when(g == 7)
        def _():
            for h in range(2):
                tokens = bg[slot, 2 * h : 2 * h + 2].reshape(2 * length, bg.shape[3])
                upper = gg[slot, 2 * h : 2 * h + 2].reshape(2 * length, bg.shape[3])
                both = dot(tokens, wgu[2])
                up = both[:, WIDE:]
                silu, slope = swish(both[:, :WIDE])
                inner = (silu * up).astype(bf16)
                part = slice(2 * h * length, 2 * (h + 1) * length)
                more = slice(group + 2 * h * length, group + 2 * (h + 1) * length)
                st[1, more] = (st[1, more].astype(f32) + dot(inner, wdn_ref[2])).astype(bf16)
                pull = dot(upper, wdn_ref[2], NT)
                turn = jnp.concatenate([(pull * up * slope).astype(bf16), (pull * silu).astype(bf16)], axis=1)
                st[1, part] = (st[1, part].astype(f32) + dot(turn, wgu[2], NT)).astype(bf16)
                if h == 0:
                    dsdn_ref[...] = dot(inner, upper, TN)
                    dsgu_ref[...] = dot(tokens, turn, TN)
                else:
                    dsdn_ref[...] += dot(inner, upper, TN)
                    dsgu_ref[...] += dot(tokens, turn, TN)

        @pl.when(par == 0)
        def _():
            to_mate(s).start()

        @pl.when(par == 1)
        def _():
            to_mate(s).wait_recv()
            copy = pltpu.make_async_copy(mrecv.at[s], ld.at[0], ldsem.at[0])
            copy.start()
            copy.wait()

            def add(i, carry):
                part = pl.ds(pl.multiple_of(i * 16, 16), 16)
                st[1, part] = (st[1, part].astype(f32) + ld[0, part].astype(f32)).astype(bf16)
                return carry

            lax.fori_loop(0, st.shape[1] // 16, add, 0)

            @pl.when(s < 3)
            def _():
                to_chip(s).start()

        return carry

    lax.fori_loop(0, 8, step, 0)
    to_mate(3).wait_send()
    for e in range(2):
        gst[e] = acc[e].astype(bf16)

    def gcopy(d):
        there = (z + d) % NZ
        return remote(
            gst.at[:, pl.ds(pl.multiple_of(there * rows, rows), rows), :], dgu_ref.at[z],
            gss.at[d - 1], grs.at[d - 1], c, there,
        )

    gown = pltpu.make_async_copy(gst.at[:, pl.ds(pl.multiple_of(z * rows, rows), rows), :], dgu_ref.at[z], gl)
    gown.start()
    for i in range(3):
        to_chip(i).wait_recv()
        pltpu.make_async_copy(xrecv.at[i], ld.at[i], ldsem.at[i]).start()
    for i in range(3):
        pltpu.make_async_copy(xrecv.at[i], ld.at[i], ldsem.at[i]).wait()

    def total(part, lanes=slice(None)):
        value = st[1, part, lanes].astype(f32)
        for i in range(3):
            value = value + ld[i, part, lanes].astype(f32)
        return value.astype(bf16)

    for q in range(NZ):

        def add(i, carry):
            base = pl.multiple_of(i * 16, 16)
            zbuf[q, pl.ds(base, 16)] = total(pl.ds(pl.multiple_of(base + q * length, 16), 16))
            zbuf[q, pl.ds(pl.multiple_of(base + length, 16), 16)] = total(
                pl.ds(pl.multiple_of(base + group + q * length, 16), 16)
            )
            return carry

        lax.fori_loop(0, length // 16, add, 0)
        zbuf[q, 2 * length : 2 * length + 16, 0:length] = total(
            slice(2 * group, 2 * group + 16), slice(q * length, (q + 1) * length)
        )

    def zcopy(d):
        there = (z + d) % NZ
        return remote(zbuf.at[there], zrecv.at[d - 1], zs.at[d - 1], zr.at[d - 1], c, there)

    for d in range(1, NZ):
        zcopy(d).start()
    for d in range(1, NZ):
        gcopy(d).start()
    for d in range(1, NZ):
        zcopy(d).wait_recv()

    def settle(i, carry):
        base = pl.multiple_of(i * 16, 16)
        for ref, start in ((db_ref, 0), (y_ref, length)):
            part = pl.ds(pl.multiple_of(base + start, 16), 16)
            value = zbuf[z, part].astype(f32)
            for d in range(3):
                value = value + zrecv[d, part].astype(f32)
            ref[pl.ds(base, 16)] = value
        return carry

    lax.fori_loop(0, length // 16, settle, 0)
    last = slice(2 * length, 2 * length + 16)
    value = zbuf[z, last, 0:length].astype(f32)
    for d in range(3):
        value = value + zrecv[d, last, 0:length].astype(f32)
    dg_ref[...] = value
    for d in range(1, NZ):
        zcopy(d).wait_send()
        wcopy(d).wait_send()
        gcopy(d).wait()
    gown.wait()


def expert_stage(moe_input, table, upstream_low, wsend, wdn):
    length, width = moe_input.shape
    dma = pltpu.SemaphoreType.DMA
    hbm = pl.BlockSpec(memory_space=pl.ANY)
    vmem = pl.BlockSpec(memory_space=pltpu.VMEM)
    f32, bf16 = jnp.float32, jnp.bfloat16
    shape = jax.ShapeDtypeStruct
    inner = 2 * WIDE
    group = NZ * length
    rows = width // NZ
    return pl.pallas_call(
        expert_kernel,
        name="experts",
        out_shape=[
            shape((length, width), f32),
            shape((length, width), f32),
            shape((16, length), f32),
            shape((NZ, 2, rows, inner), bf16),
            shape((2, WIDE, width), f32),
            shape((width, inner), f32),
            shape((WIDE, width), f32),
            shape((8, NZ, length, width), bf16),
            shape((8, NZ, 16, 2 * length), f32),
            shape((8, NZ, length, width), bf16),
            shape((4, 2 * group + 16, width), bf16),
            shape((3, 2 * group + 16, width), bf16),
        ],
        in_specs=[hbm, hbm, hbm, hbm, vmem],
        out_specs=[vmem, vmem, vmem, hbm, vmem, vmem, vmem, hbm, hbm, hbm, hbm, hbm],
        scratch_shapes=[
            pltpu.VMEM((3, width, inner), bf16),
            pltpu.VMEM((2, width, inner), f32),
            pltpu.VMEM((2, NZ, length, width), bf16),
            pltpu.VMEM((2, NZ, length, width), bf16),
            pltpu.VMEM((2, NZ, 16, 2 * length), f32),
            pltpu.VMEM((NZ, 2 * SLOTS, length), bf16),
            pltpu.VMEM((2, NZ * SLOTS, width), bf16),
            pltpu.VMEM((2, NZ * SLOTS, width), bf16),
            pltpu.VMEM((NZ, 2 * SLOTS, width), bf16),
            pltpu.VMEM((NZ, 2 * SLOTS, width), bf16),
            pltpu.VMEM((2, 2 * group + 16, width), bf16),
            pltpu.VMEM((3, 2 * group + 16, width), bf16),
            pltpu.VMEM((NZ, 2 * length + 16, width), bf16),
            pltpu.VMEM((3, 2 * length + 16, width), bf16),
            pltpu.VMEM((2, width, inner), bf16),
        ]
        + spread_sems() + spread_sems() + spread_sems()
        + [
            dma, dma((3,)), dma((3,)), dma((2, 3)), dma((4,)), dma((4,)), dma((3,)), dma((3,)), dma((3,)),
            dma((3,)), dma((3,)), dma, dma((3,)), dma((3,)),
        ],
        compiler_params=pltpu.CompilerParams(
            collective_id=1, has_side_effects=True, vmem_limit_bytes=62 * 1024 * 1024
        ),
    )(moe_input, table, upstream_low, wsend, wdn)


def per_device(
    tokens,
    documents,
    routes,
    priority,
    attention_gain,
    query_weight,
    key_weight,
    value_weight,
    output_weight,
    feedforward_gain,
    router_weight,
    shared_gate,
    shared_up,
    shared_down,
    expert_gate,
    expert_up,
    expert_down,
    cotangent,
):
    gathered = (
        lax.all_gather(attention_gain, "fsdp", axis=0, tiled=True),
        lax.all_gather(query_weight, "fsdp", axis=0, tiled=True),
        lax.all_gather(key_weight, "fsdp", axis=0, tiled=True),
        lax.all_gather(value_weight, "fsdp", axis=0, tiled=True),
        lax.all_gather(output_weight, "fsdp", axis=0, tiled=True),
        lax.all_gather(feedforward_gain, "fsdp", axis=0, tiled=True),
        lax.all_gather(router_weight, "fsdp", axis=0, tiled=True),
        lax.all_gather(shared_gate, "fsdp", axis=0, tiled=True),
        lax.all_gather(shared_up, "fsdp", axis=0, tiled=True),
        lax.all_gather(shared_down, "fsdp", axis=0, tiled=True),
        lax.all_gather(expert_gate, "fsdp", axis=1, tiled=True),
        lax.all_gather(expert_up, "fsdp", axis=1, tiled=True),
        lax.all_gather(expert_down, "fsdp", axis=1, tiled=True),
    )
    (
        gain_one,
        w_query,
        w_key,
        w_value,
        w_output,
        gain_two,
        w_router,
        w_shared_gate,
        w_shared_up,
        w_shared_down,
        w_expert_gate,
        w_expert_up,
        w_expert_down,
    ) = gathered
    groups = lax.axis_size("ctx")
    length = tokens.shape[1]
    row_length = length * groups
    experts = EXP_DEV * groups
    capacity = 9 * length * TOPK // (8 * experts)
    inner_width = HEADS * HEAD_DIM
    score_scale = HEAD_DIM ** (-0.5)
    spare_slot = experts * capacity
    first_here = lax.axis_index("ctx") * length
    positions = first_here + jnp.arange(length, dtype=jnp.int32)
    last_here = first_here + length - 1
    doc_here = documents[0].astype(jnp.float32)
    doc_wire = documents[0].astype(jnp.bfloat16)
    inputs = tokens[0].astype(jnp.float32)
    upstream_low = cotangent[0]
    upstream = upstream_low.astype(jnp.float32)
    factor_one = rms_factor(inputs)
    normed_one = inputs * factor_one
    gain_one_wide = gain_one.astype(jnp.float32)
    attn_input = (normed_one * gain_one_wide).astype(jnp.bfloat16)
    query_pre = jnp.dot(attn_input, w_query, preferred_element_type=jnp.float32).reshape(
        length, HEADS, HEAD_DIM
    )
    key_pre = jnp.dot(attn_input, w_key, preferred_element_type=jnp.float32).reshape(
        length, HEADS, HEAD_DIM
    )
    cosine, sine = rotary_tables(positions, HEAD_DIM // 2)
    queries = rotate(query_pre, cosine, sine).astype(jnp.bfloat16)
    key_rows = rotate(key_pre, cosine, sine).astype(jnp.bfloat16)
    value_rows = (
        jnp.dot(attn_input, w_value, preferred_element_type=jnp.float32)
        .astype(jnp.bfloat16)
        .reshape(length, HEADS, HEAD_DIM)
    )
    initial = (
        jnp.zeros((HEADS, length, HEAD_DIM), jnp.float32),
        jnp.full((HEADS, length), negative, jnp.float32),
        jnp.zeros((HEADS, length), jnp.float32),
    )
    key_all = lax.all_gather(key_rows, "ctx", axis=0, tiled=True)
    value_all = lax.all_gather(value_rows, "ctx", axis=0, tiled=True)
    docs_all = lax.all_gather(doc_wire, "ctx", axis=0, tiled=True)

    def visit(progress, within, rows_now):

        def compute(progress):
            accum, highest_seen, totals = progress
            key_block = lax.dynamic_slice_in_dim(key_all, within, rows_now, 0)
            value_block = lax.dynamic_slice_in_dim(value_all, within, rows_now, 0)
            docs_block = lax.dynamic_slice_in_dim(docs_all, within, rows_now, 0).astype(jnp.float32)
            key_pos = within + jnp.arange(rows_now, dtype=jnp.int32)
            allowed = allowed_mask(positions, doc_here, key_pos, docs_block)[None]
            scores = jnp.einsum(
                "qhd,khd->hqk", queries, key_block, preferred_element_type=jnp.float32
            )
            scores = jnp.where(allowed, scores * score_scale, negative)
            newest = jnp.maximum(highest_seen, jnp.max(scores, axis=-1))
            shrink = jnp.exp(highest_seen - newest)
            shares = jnp.exp(scores - newest[..., None]) * allowed
            totals = totals * shrink + jnp.sum(shares, axis=-1)
            accum = accum * shrink[..., None] + jnp.einsum(
                "hqk,khd->hqd",
                shares.astype(jnp.bfloat16),
                value_block,
                preferred_element_type=jnp.float32,
            )
            return (accum, newest, totals)

        return lax.cond(within > last_here, unchanged, compute, progress)

    accum, highest_seen, totals = blockwise(key_all.shape[0], visit, initial)
    attended = accum / totals[..., None]
    log_total = highest_seen + jnp.log(totals)
    mixed_rows = (
        jnp.transpose(attended, (1, 0, 2)).reshape(length, inner_width).astype(jnp.bfloat16)
    )
    hidden = inputs + jnp.dot(mixed_rows, w_output, preferred_element_type=jnp.float32)
    factor_two = rms_factor(hidden)
    normed_two = hidden * factor_two
    gain_two_wide = gain_two.astype(jnp.float32)
    moe_input = (normed_two * gain_two_wide).astype(jnp.bfloat16)
    moe_wide = moe_input.astype(jnp.float32)
    router_wide = w_router.astype(jnp.float32)
    gate_probs = jax.nn.softmax(jnp.dot(moe_wide, router_wide, precision=highest), axis=-1)
    route_now = routes[0]
    order_now = priority[0, 0]
    onehot = (route_now[:, :, None] == jnp.arange(experts, dtype=jnp.int32)).astype(jnp.float32)
    counts = jnp.sum(onehot, axis=1)
    earlier = (order_now[None, :] < order_now[:, None]).astype(jnp.bfloat16)
    before = jnp.dot(earlier, counts.astype(jnp.bfloat16), preferred_element_type=jnp.float32)
    ranking = jnp.sum(onehot * before[:, None, :], axis=-1).astype(jnp.int32)
    kept_mask = ranking < capacity
    slot_index = jnp.where(
        kept_mask,
        route_now % EXP_DEV * (groups * capacity) + route_now // EXP_DEV * capacity + ranking,
        spare_slot,
    )
    chosen = jnp.sum(onehot * gate_probs[:, None, :], axis=-1)
    weight = jnp.where(kept_mask, chosen, 0.0)
    flat_slots = slot_index.reshape(-1)
    copies = jnp.broadcast_to(moe_input[:, None, :], (length, TOPK, D)).reshape(length * TOPK, D)
    outgoing = jnp.zeros((spare_slot + 1, D), jnp.bfloat16).at[flat_slots].set(copies)[:spare_slot]
    arrived = lax.all_to_all(
        outgoing.reshape(EXP_DEV, groups, capacity, D),
        "ctx",
        split_axis=1,
        concat_axis=1,
        tiled=True,
    ).reshape(EXP_DEV, groups * capacity, D)
    gate_act = jnp.einsum(
        "erd,edf->erf", arrived, w_expert_gate, preferred_element_type=jnp.float32
    )
    up_act = jnp.einsum("erd,edf->erf", arrived, w_expert_up, preferred_element_type=jnp.float32)
    silu_gate, slope_gate = silu_parts(gate_act)
    expert_hidden = (silu_gate * up_act).astype(jnp.bfloat16)
    expert_out = jnp.einsum(
        "erf,efd->erd", expert_hidden, w_expert_down, preferred_element_type=jnp.float32
    ).astype(jnp.bfloat16)
    returned = lax.all_to_all(
        expert_out.reshape(EXP_DEV, groups, capacity, D),
        "ctx",
        split_axis=1,
        concat_axis=1,
        tiled=True,
    ).reshape(spare_slot, D)
    returned = jnp.concatenate([returned, jnp.zeros((1, D), jnp.bfloat16)], axis=0)
    picked = returned[slot_index]
    routed = jnp.sum(weight[..., None] * picked, axis=1)
    shared_gate_act = jnp.dot(moe_input, w_shared_gate, preferred_element_type=jnp.float32)
    shared_up_act = jnp.dot(moe_input, w_shared_up, preferred_element_type=jnp.float32)
    silu_shared, slope_shared = silu_parts(shared_gate_act)
    shared_hidden = (silu_shared * shared_up_act).astype(jnp.bfloat16)
    shared_out = jnp.dot(shared_hidden, w_shared_down, preferred_element_type=jnp.float32)
    output_rows = (hidden + shared_out + routed).astype(jnp.bfloat16)
    grad_shared_down = jnp.dot(shared_hidden.T, upstream_low, preferred_element_type=jnp.float32)
    grad_shared_hidden = jnp.dot(upstream_low, w_shared_down.T, preferred_element_type=jnp.float32)
    grad_shared_gate_act = (grad_shared_hidden * shared_up_act * slope_shared).astype(jnp.bfloat16)
    grad_shared_up_act = (grad_shared_hidden * silu_shared).astype(jnp.bfloat16)
    grad_shared_gate = jnp.dot(
        moe_input.T, grad_shared_gate_act, preferred_element_type=jnp.float32
    )
    grad_shared_up = jnp.dot(moe_input.T, grad_shared_up_act, preferred_element_type=jnp.float32)
    grad_moe = jnp.dot(
        grad_shared_gate_act, w_shared_gate.T, preferred_element_type=jnp.float32
    ) + jnp.dot(grad_shared_up_act, w_shared_up.T, preferred_element_type=jnp.float32)
    grad_copies = (
        (weight[..., None] * upstream[:, None, :]).astype(jnp.bfloat16).reshape(length * TOPK, D)
    )
    grad_weight = jnp.sum(picked.astype(jnp.float32) * upstream[:, None, :], axis=-1)
    grad_outgoing = (
        jnp.zeros((spare_slot + 1, D), jnp.bfloat16).at[flat_slots].set(grad_copies)[:spare_slot]
    )
    grad_arrived = lax.all_to_all(
        grad_outgoing.reshape(EXP_DEV, groups, capacity, D),
        "ctx",
        split_axis=1,
        concat_axis=1,
        tiled=True,
    ).reshape(EXP_DEV, groups * capacity, D)
    grad_expert_hidden = jnp.einsum(
        "erd,efd->erf", grad_arrived, w_expert_down, preferred_element_type=jnp.float32
    )
    grad_expert_down = jnp.einsum(
        "erf,erd->efd", expert_hidden, grad_arrived, preferred_element_type=jnp.float32
    )
    grad_gate_act = (grad_expert_hidden * up_act * slope_gate).astype(jnp.bfloat16)
    grad_up_act = (grad_expert_hidden * silu_gate).astype(jnp.bfloat16)
    grad_expert_gate = jnp.einsum(
        "erd,erf->edf", arrived, grad_gate_act, preferred_element_type=jnp.float32
    )
    grad_expert_up = jnp.einsum(
        "erd,erf->edf", arrived, grad_up_act, preferred_element_type=jnp.float32
    )
    grad_arrived_in = (
        jnp.einsum("erf,edf->erd", grad_gate_act, w_expert_gate, preferred_element_type=jnp.float32)
        + jnp.einsum("erf,edf->erd", grad_up_act, w_expert_up, preferred_element_type=jnp.float32)
    ).astype(jnp.bfloat16)
    sent_back = lax.all_to_all(
        grad_arrived_in.reshape(EXP_DEV, groups, capacity, D),
        "ctx",
        split_axis=1,
        concat_axis=1,
        tiled=True,
    ).reshape(spare_slot, D)
    sent_back = jnp.concatenate([sent_back, jnp.zeros((1, D), jnp.bfloat16)], axis=0)
    grad_moe = grad_moe + jnp.sum(sent_back[slot_index].astype(jnp.float32), axis=1)
    grad_chosen = jnp.where(kept_mask, grad_weight, 0.0)
    grad_probs = jnp.sum(onehot * grad_chosen[..., None], axis=1)
    grad_logits = gate_probs * (
        grad_probs - jnp.sum(gate_probs * grad_probs, axis=-1, keepdims=True)
    )
    grad_router = jnp.dot(moe_wide.T, grad_logits, precision=highest)
    grad_moe = grad_moe + jnp.dot(grad_logits, router_wide.T, precision=highest)
    grad_gain_two = jnp.sum(grad_moe * normed_two, axis=0)
    scaled_two = grad_moe * gain_two_wide
    grad_hidden = upstream + factor_two * (
        scaled_two - normed_two * jnp.mean(scaled_two * normed_two, axis=-1, keepdims=True)
    )
    grad_hidden_low = grad_hidden.astype(jnp.bfloat16)
    grad_output = jnp.dot(mixed_rows.T, grad_hidden_low, preferred_element_type=jnp.float32)
    grad_mixed = (
        jnp.dot(grad_hidden_low, w_output.T, preferred_element_type=jnp.float32)
        .astype(jnp.bfloat16)
        .reshape(length, HEADS, HEAD_DIM)
    )
    delta = jnp.einsum("qhd,hqd->hq", grad_mixed.astype(jnp.float32), attended)
    start_state = (
        jnp.zeros((length, HEADS, HEAD_DIM), jnp.float32),
        jnp.zeros((row_length, 2 * inner_width), jnp.float32),
    )
    back_key_all = lax.all_gather(key_rows, "ctx", axis=0, tiled=True)
    back_value_all = lax.all_gather(value_rows, "ctx", axis=0, tiled=True)
    back_docs_all = lax.all_gather(doc_wire, "ctx", axis=0, tiled=True)

    def visit(progress, within, rows_now):
        first_row = within

        def compute(progress):
            grad_query_acc, grad_kv_all = progress
            key_block = lax.dynamic_slice_in_dim(back_key_all, within, rows_now, 0)
            value_block = lax.dynamic_slice_in_dim(back_value_all, within, rows_now, 0)
            docs_block = lax.dynamic_slice_in_dim(back_docs_all, within, rows_now, 0).astype(
                jnp.float32
            )
            key_pos = first_row + jnp.arange(rows_now, dtype=jnp.int32)
            allowed = allowed_mask(positions, doc_here, key_pos, docs_block)[None]
            scores = jnp.einsum(
                "qhd,khd->hqk", queries, key_block, preferred_element_type=jnp.float32
            )
            scores = jnp.where(allowed, scores * score_scale, negative)
            shares = jnp.exp(scores - log_total[..., None]) * allowed
            grad_shares = jnp.einsum(
                "qhd,khd->hqk", grad_mixed, value_block, preferred_element_type=jnp.float32
            )
            grad_scores = (shares * (grad_shares - delta[..., None]) * score_scale).astype(
                jnp.bfloat16
            )
            grad_query_acc = grad_query_acc + jnp.einsum(
                "hqk,khd->qhd", grad_scores, key_block, preferred_element_type=jnp.float32
            )
            grad_key_rows = jnp.einsum(
                "hqk,qhd->khd", grad_scores, queries, preferred_element_type=jnp.float32
            ).reshape(rows_now, inner_width)
            grad_value_rows = jnp.einsum(
                "hqk,qhd->khd",
                shares.astype(jnp.bfloat16),
                grad_mixed,
                preferred_element_type=jnp.float32,
            ).reshape(rows_now, inner_width)
            current = lax.dynamic_slice_in_dim(grad_kv_all, first_row, rows_now, 0)
            grad_kv_all = lax.dynamic_update_slice_in_dim(
                grad_kv_all,
                current + jnp.concatenate([grad_key_rows, grad_value_rows], axis=1),
                first_row,
                0,
            )
            return (grad_query_acc, grad_kv_all)

        return lax.cond(first_row > last_here, unchanged, compute, progress)

    grad_query, grad_kv_all = blockwise(back_key_all.shape[0], visit, start_state)
    grad_kv = lax.psum_scatter(
        grad_kv_all.astype(jnp.bfloat16), "ctx", scatter_dimension=0, tiled=True
    ).astype(jnp.float32)
    grad_query_low = (
        unrotate(grad_query.astype(jnp.bfloat16).astype(jnp.float32), cosine, sine)
        .astype(jnp.bfloat16)
        .reshape(length, inner_width)
    )
    grad_key_turned = (
        grad_kv[:, :inner_width]
        .reshape(length, HEADS, HEAD_DIM)
        .astype(jnp.bfloat16)
        .astype(jnp.float32)
    )
    grad_key_low = (
        unrotate(grad_key_turned, cosine, sine).astype(jnp.bfloat16).reshape(length, inner_width)
    )
    grad_value_low = grad_kv[:, inner_width:].astype(jnp.bfloat16)
    grad_wquery = jnp.dot(attn_input.T, grad_query_low, preferred_element_type=jnp.float32)
    grad_wkey = jnp.dot(attn_input.T, grad_key_low, preferred_element_type=jnp.float32)
    grad_wvalue = jnp.dot(attn_input.T, grad_value_low, preferred_element_type=jnp.float32)
    grad_attn = (
        jnp.dot(grad_query_low, w_query.T, preferred_element_type=jnp.float32)
        + jnp.dot(grad_key_low, w_key.T, preferred_element_type=jnp.float32)
        + jnp.dot(grad_value_low, w_value.T, preferred_element_type=jnp.float32)
    )
    grad_gain_one = jnp.sum(grad_attn * normed_one, axis=0)
    scaled_one = grad_attn * gain_one_wide
    grad_inputs = grad_hidden + factor_one * (
        scaled_one - normed_one * jnp.mean(scaled_one * normed_one, axis=-1, keepdims=True)
    )
    owned = (
        lax.psum_scatter(
            grad_gain_one.astype(jnp.bfloat16), "fsdp", scatter_dimension=0, tiled=True
        ).astype(jnp.float32),
        lax.psum_scatter(
            grad_wquery.astype(jnp.bfloat16), "fsdp", scatter_dimension=0, tiled=True
        ).astype(jnp.float32),
        lax.psum_scatter(
            grad_wkey.astype(jnp.bfloat16), "fsdp", scatter_dimension=0, tiled=True
        ).astype(jnp.float32),
        lax.psum_scatter(
            grad_wvalue.astype(jnp.bfloat16), "fsdp", scatter_dimension=0, tiled=True
        ).astype(jnp.float32),
        lax.psum_scatter(
            grad_output.astype(jnp.bfloat16), "fsdp", scatter_dimension=0, tiled=True
        ).astype(jnp.float32),
        lax.psum_scatter(
            grad_gain_two.astype(jnp.bfloat16), "fsdp", scatter_dimension=0, tiled=True
        ).astype(jnp.float32),
        lax.psum_scatter(
            grad_router.astype(jnp.bfloat16), "fsdp", scatter_dimension=0, tiled=True
        ).astype(jnp.float32),
        lax.psum_scatter(
            grad_shared_gate.astype(jnp.bfloat16), "fsdp", scatter_dimension=0, tiled=True
        ).astype(jnp.float32),
        lax.psum_scatter(
            grad_shared_up.astype(jnp.bfloat16), "fsdp", scatter_dimension=0, tiled=True
        ).astype(jnp.float32),
        lax.psum_scatter(
            grad_shared_down.astype(jnp.bfloat16), "fsdp", scatter_dimension=0, tiled=True
        ).astype(jnp.float32),
        lax.psum_scatter(
            grad_expert_gate.astype(jnp.bfloat16), "fsdp", scatter_dimension=1, tiled=True
        ).astype(jnp.float32),
        lax.psum_scatter(
            grad_expert_up.astype(jnp.bfloat16), "fsdp", scatter_dimension=1, tiled=True
        ).astype(jnp.float32),
        lax.psum_scatter(
            grad_expert_down.astype(jnp.bfloat16), "fsdp", scatter_dimension=1, tiled=True
        ).astype(jnp.float32),
    )
    (
        own_gain_one,
        own_wquery,
        own_wkey,
        own_wvalue,
        own_output,
        own_gain_two,
        own_router,
        own_shared_gate,
        own_shared_up,
        own_shared_down,
        own_expert_gate,
        own_expert_up,
        own_expert_down,
    ) = owned
    dense = (
        lax.psum(own_gain_one.astype(jnp.bfloat16), "ctx").astype(jnp.float32),
        lax.psum(own_wquery.astype(jnp.bfloat16), "ctx").astype(jnp.float32),
        lax.psum(own_wkey.astype(jnp.bfloat16), "ctx").astype(jnp.float32),
        lax.psum(own_wvalue.astype(jnp.bfloat16), "ctx").astype(jnp.float32),
        lax.psum(own_output.astype(jnp.bfloat16), "ctx").astype(jnp.float32),
        lax.psum(own_gain_two.astype(jnp.bfloat16), "ctx").astype(jnp.float32),
        lax.psum(own_router.astype(jnp.bfloat16), "ctx").astype(jnp.float32),
        lax.psum(own_shared_gate.astype(jnp.bfloat16), "ctx").astype(jnp.float32),
        lax.psum(own_shared_up.astype(jnp.bfloat16), "ctx").astype(jnp.float32),
        lax.psum(own_shared_down.astype(jnp.bfloat16), "ctx").astype(jnp.float32),
    )
    return (
        output_rows[None],
        grad_inputs.astype(jnp.bfloat16)[None],
        dense[0],
        dense[1],
        dense[2],
        dense[3],
        dense[4],
        dense[5],
        dense[6],
        dense[7],
        dense[8],
        dense[9],
        own_expert_gate,
        own_expert_up,
        own_expert_down,
    )


def per_device_fast(
    tokens,
    documents,
    routes,
    priority,
    attention_gain,
    query_weight,
    key_weight,
    value_weight,
    output_weight,
    feedforward_gain,
    router_weight,
    shared_gate,
    shared_up,
    shared_down,
    expert_gate,
    expert_up,
    expert_down,
    cotangent,
):
    gathered = (
        lax.all_gather(attention_gain, "fsdp", axis=0, tiled=True),
        lax.all_gather(query_weight, "fsdp", axis=0, tiled=True),
        lax.all_gather(key_weight, "fsdp", axis=0, tiled=True),
        lax.all_gather(value_weight, "fsdp", axis=0, tiled=True),
        lax.all_gather(output_weight, "fsdp", axis=0, tiled=True),
        lax.all_gather(feedforward_gain, "fsdp", axis=0, tiled=True),
        lax.all_gather(router_weight, "fsdp", axis=0, tiled=True),
    )
    (
        gain_one,
        w_query,
        w_key,
        w_value,
        w_output,
        gain_two,
        w_router,
    ) = gathered
    groups = lax.axis_size("ctx")
    length = tokens.shape[1]
    row_length = length * groups
    experts = EXP_DEV * groups
    capacity = 9 * length * TOPK // (8 * experts)
    inner_width = HEADS * HEAD_DIM
    score_scale = HEAD_DIM ** (-0.5)
    spare_slot = experts * capacity
    first_here = lax.axis_index("ctx") * length
    positions = first_here + jnp.arange(length, dtype=jnp.int32)
    last_here = first_here + length - 1
    doc_here = documents[0].astype(jnp.float32)
    doc_wire = documents[0].astype(jnp.bfloat16)
    inputs = tokens[0].astype(jnp.float32)
    upstream_low = cotangent[0]
    upstream = upstream_low.astype(jnp.float32)
    factor_one = rms_factor(inputs)
    normed_one = inputs * factor_one
    gain_one_wide = gain_one.astype(jnp.float32)
    attn_input = (normed_one * gain_one_wide).astype(jnp.bfloat16)
    query_pre = jnp.dot(attn_input, w_query, preferred_element_type=jnp.float32).reshape(
        length, HEADS, HEAD_DIM
    )
    key_pre = jnp.dot(attn_input, w_key, preferred_element_type=jnp.float32).reshape(
        length, HEADS, HEAD_DIM
    )
    cosine, sine = rotary_tables(positions, HEAD_DIM // 2)
    queries = rotate(query_pre, cosine, sine).astype(jnp.bfloat16)
    key_rows = rotate(key_pre, cosine, sine).astype(jnp.bfloat16)
    value_rows = (
        jnp.dot(attn_input, w_value, preferred_element_type=jnp.float32)
        .astype(jnp.bfloat16)
        .reshape(length, HEADS, HEAD_DIM)
    )
    initial = (
        jnp.zeros((HEADS, length, HEAD_DIM), jnp.float32),
        jnp.full((HEADS, length), negative, jnp.float32),
        jnp.zeros((HEADS, length), jnp.float32),
    )
    key_all = lax.all_gather(key_rows, "ctx", axis=0, tiled=True)
    value_all = lax.all_gather(value_rows, "ctx", axis=0, tiled=True)
    docs_all = lax.all_gather(doc_wire, "ctx", axis=0, tiled=True)

    def visit(progress, within, rows_now):

        def compute(progress):
            accum, highest_seen, totals = progress
            key_block = lax.dynamic_slice_in_dim(key_all, within, rows_now, 0)
            value_block = lax.dynamic_slice_in_dim(value_all, within, rows_now, 0)
            docs_block = lax.dynamic_slice_in_dim(docs_all, within, rows_now, 0).astype(jnp.float32)
            key_pos = within + jnp.arange(rows_now, dtype=jnp.int32)
            allowed = allowed_mask(positions, doc_here, key_pos, docs_block)[None]
            scores = jnp.einsum(
                "qhd,khd->hqk", queries, key_block, preferred_element_type=jnp.float32
            )
            scores = jnp.where(allowed, scores * score_scale, negative)
            newest = jnp.maximum(highest_seen, jnp.max(scores, axis=-1))
            shrink = jnp.exp(highest_seen - newest)
            shares = jnp.exp(scores - newest[..., None]) * allowed
            totals = totals * shrink + jnp.sum(shares, axis=-1)
            accum = accum * shrink[..., None] + jnp.einsum(
                "hqk,khd->hqd",
                shares.astype(jnp.bfloat16),
                value_block,
                preferred_element_type=jnp.float32,
            )
            return (accum, newest, totals)

        return lax.cond(within > last_here, unchanged, compute, progress)

    accum, highest_seen, totals = blockwise(key_all.shape[0], visit, initial)
    attended = accum / totals[..., None]
    log_total = highest_seen + jnp.log(totals)
    mixed_rows = (
        jnp.transpose(attended, (1, 0, 2)).reshape(length, inner_width).astype(jnp.bfloat16)
    )
    hidden = inputs + jnp.dot(mixed_rows, w_output, preferred_element_type=jnp.float32)
    factor_two = rms_factor(hidden)
    normed_two = hidden * factor_two
    gain_two_wide = gain_two.astype(jnp.float32)
    moe_input = (normed_two * gain_two_wide).astype(jnp.bfloat16)
    moe_wide = moe_input.astype(jnp.float32)
    router_wide = w_router.astype(jnp.float32)
    gate_probs = jax.nn.softmax(jnp.dot(moe_wide, router_wide, precision=highest), axis=-1)
    route_now = routes[0]
    order_now = priority[0, 0]
    onehot = (route_now[:, :, None] == jnp.arange(experts, dtype=jnp.int32)).astype(jnp.float32)
    counts = jnp.sum(onehot, axis=1)
    earlier = (order_now[None, :] < order_now[:, None]).astype(jnp.bfloat16)
    before = jnp.dot(earlier, counts.astype(jnp.bfloat16), preferred_element_type=jnp.float32)
    kept = (counts > 0) & (before < capacity)
    table = jnp.concatenate(
        [jnp.where(kept, before, -1.0).T, jnp.where(kept, gate_probs, 0.0).T], axis=1
    )
    hidden_dev = expert_gate.shape[2] // NZ

    def slices(weights):
        parts = weights.reshape(weights.shape[0], weights.shape[1], NZ, hidden_dev)
        parts = jnp.pad(parts, ((0, 0), (0, 0), (0, 0), (0, WIDE - hidden_dev)))
        return jnp.transpose(parts, (2, 0, 1, 3))

    wsend = jnp.concatenate(
        [
            jnp.concatenate([slices(expert_gate), slices(shared_gate[None])], axis=1),
            jnp.concatenate([slices(expert_up), slices(shared_up[None])], axis=1),
        ],
        axis=3,
    )
    wdn = jnp.pad(
        jnp.concatenate([expert_down, shared_down[None]], axis=0), ((0, 0), (0, WIDE - hidden_dev), (0, 0))
    )
    (routed, grad_moe, grad_table, gu_back, grad_down, shared_gu, shared_dn) = expert_stage(
        moe_input, table, upstream_low, wsend, wdn
    )[:7]
    output_rows = (hidden + routed).astype(jnp.bfloat16)
    grad_probs = grad_table.T

    def joined(parts, at):
        return jnp.concatenate([parts[i][..., at : at + hidden_dev] for i in range(NZ)], axis=-1).astype(jnp.float32)

    own_expert_gate = joined(gu_back, 0)
    own_expert_up = joined(gu_back, WIDE)
    own_expert_down = grad_down[:, :hidden_dev]
    shared_sum = lax.psum(shared_gu.astype(jnp.bfloat16), "ctx")
    shared_back = lax.all_to_all(
        shared_sum.reshape(NZ, shared_sum.shape[0] // NZ, 2 * WIDE), "fsdp", split_axis=0, concat_axis=0, tiled=True
    )
    own_shared_gate = joined(shared_back, 0)
    own_shared_up = joined(shared_back, WIDE)
    own_shared_down = lax.psum(shared_dn[:hidden_dev].astype(jnp.bfloat16), "ctx").astype(jnp.float32)
    grad_logits = gate_probs * (
        grad_probs - jnp.sum(gate_probs * grad_probs, axis=-1, keepdims=True)
    )
    grad_router = jnp.dot(moe_wide.T, grad_logits, precision=highest)
    grad_moe = grad_moe + jnp.dot(grad_logits, router_wide.T, precision=highest)
    grad_gain_two = jnp.sum(grad_moe * normed_two, axis=0)
    scaled_two = grad_moe * gain_two_wide
    grad_hidden = upstream + factor_two * (
        scaled_two - normed_two * jnp.mean(scaled_two * normed_two, axis=-1, keepdims=True)
    )
    grad_hidden_low = grad_hidden.astype(jnp.bfloat16)
    grad_output = jnp.dot(mixed_rows.T, grad_hidden_low, preferred_element_type=jnp.float32)
    grad_mixed = (
        jnp.dot(grad_hidden_low, w_output.T, preferred_element_type=jnp.float32)
        .astype(jnp.bfloat16)
        .reshape(length, HEADS, HEAD_DIM)
    )
    delta = jnp.einsum("qhd,hqd->hq", grad_mixed.astype(jnp.float32), attended)
    start_state = (
        jnp.zeros((length, HEADS, HEAD_DIM), jnp.float32),
        jnp.zeros((row_length, 2 * inner_width), jnp.float32),
    )
    back_key_all = lax.all_gather(key_rows, "ctx", axis=0, tiled=True)
    back_value_all = lax.all_gather(value_rows, "ctx", axis=0, tiled=True)
    back_docs_all = lax.all_gather(doc_wire, "ctx", axis=0, tiled=True)

    def visit(progress, within, rows_now):
        first_row = within

        def compute(progress):
            grad_query_acc, grad_kv_all = progress
            key_block = lax.dynamic_slice_in_dim(back_key_all, within, rows_now, 0)
            value_block = lax.dynamic_slice_in_dim(back_value_all, within, rows_now, 0)
            docs_block = lax.dynamic_slice_in_dim(back_docs_all, within, rows_now, 0).astype(
                jnp.float32
            )
            key_pos = first_row + jnp.arange(rows_now, dtype=jnp.int32)
            allowed = allowed_mask(positions, doc_here, key_pos, docs_block)[None]
            scores = jnp.einsum(
                "qhd,khd->hqk", queries, key_block, preferred_element_type=jnp.float32
            )
            scores = jnp.where(allowed, scores * score_scale, negative)
            shares = jnp.exp(scores - log_total[..., None]) * allowed
            grad_shares = jnp.einsum(
                "qhd,khd->hqk", grad_mixed, value_block, preferred_element_type=jnp.float32
            )
            grad_scores = (shares * (grad_shares - delta[..., None]) * score_scale).astype(
                jnp.bfloat16
            )
            grad_query_acc = grad_query_acc + jnp.einsum(
                "hqk,khd->qhd", grad_scores, key_block, preferred_element_type=jnp.float32
            )
            grad_key_rows = jnp.einsum(
                "hqk,qhd->khd", grad_scores, queries, preferred_element_type=jnp.float32
            ).reshape(rows_now, inner_width)
            grad_value_rows = jnp.einsum(
                "hqk,qhd->khd",
                shares.astype(jnp.bfloat16),
                grad_mixed,
                preferred_element_type=jnp.float32,
            ).reshape(rows_now, inner_width)
            current = lax.dynamic_slice_in_dim(grad_kv_all, first_row, rows_now, 0)
            grad_kv_all = lax.dynamic_update_slice_in_dim(
                grad_kv_all,
                current + jnp.concatenate([grad_key_rows, grad_value_rows], axis=1),
                first_row,
                0,
            )
            return (grad_query_acc, grad_kv_all)

        return lax.cond(first_row > last_here, unchanged, compute, progress)

    grad_query, grad_kv_all = blockwise(back_key_all.shape[0], visit, start_state)
    grad_kv = lax.psum_scatter(
        grad_kv_all.astype(jnp.bfloat16), "ctx", scatter_dimension=0, tiled=True
    ).astype(jnp.float32)
    grad_query_low = (
        unrotate(grad_query.astype(jnp.bfloat16).astype(jnp.float32), cosine, sine)
        .astype(jnp.bfloat16)
        .reshape(length, inner_width)
    )
    grad_key_turned = (
        grad_kv[:, :inner_width]
        .reshape(length, HEADS, HEAD_DIM)
        .astype(jnp.bfloat16)
        .astype(jnp.float32)
    )
    grad_key_low = (
        unrotate(grad_key_turned, cosine, sine).astype(jnp.bfloat16).reshape(length, inner_width)
    )
    grad_value_low = grad_kv[:, inner_width:].astype(jnp.bfloat16)
    grad_wquery = jnp.dot(attn_input.T, grad_query_low, preferred_element_type=jnp.float32)
    grad_wkey = jnp.dot(attn_input.T, grad_key_low, preferred_element_type=jnp.float32)
    grad_wvalue = jnp.dot(attn_input.T, grad_value_low, preferred_element_type=jnp.float32)
    grad_attn = (
        jnp.dot(grad_query_low, w_query.T, preferred_element_type=jnp.float32)
        + jnp.dot(grad_key_low, w_key.T, preferred_element_type=jnp.float32)
        + jnp.dot(grad_value_low, w_value.T, preferred_element_type=jnp.float32)
    )
    grad_gain_one = jnp.sum(grad_attn * normed_one, axis=0)
    scaled_one = grad_attn * gain_one_wide
    grad_inputs = grad_hidden + factor_one * (
        scaled_one - normed_one * jnp.mean(scaled_one * normed_one, axis=-1, keepdims=True)
    )
    owned = (
        lax.psum_scatter(
            grad_gain_one.astype(jnp.bfloat16), "fsdp", scatter_dimension=0, tiled=True
        ).astype(jnp.float32),
        lax.psum_scatter(
            grad_wquery.astype(jnp.bfloat16), "fsdp", scatter_dimension=0, tiled=True
        ).astype(jnp.float32),
        lax.psum_scatter(
            grad_wkey.astype(jnp.bfloat16), "fsdp", scatter_dimension=0, tiled=True
        ).astype(jnp.float32),
        lax.psum_scatter(
            grad_wvalue.astype(jnp.bfloat16), "fsdp", scatter_dimension=0, tiled=True
        ).astype(jnp.float32),
        lax.psum_scatter(
            grad_output.astype(jnp.bfloat16), "fsdp", scatter_dimension=0, tiled=True
        ).astype(jnp.float32),
        lax.psum_scatter(
            grad_gain_two.astype(jnp.bfloat16), "fsdp", scatter_dimension=0, tiled=True
        ).astype(jnp.float32),
        lax.psum_scatter(
            grad_router.astype(jnp.bfloat16), "fsdp", scatter_dimension=0, tiled=True
        ).astype(jnp.float32),
    )
    (
        own_gain_one,
        own_wquery,
        own_wkey,
        own_wvalue,
        own_output,
        own_gain_two,
        own_router,
    ) = owned
    dense = (
        lax.psum(own_gain_one.astype(jnp.bfloat16), "ctx").astype(jnp.float32),
        lax.psum(own_wquery.astype(jnp.bfloat16), "ctx").astype(jnp.float32),
        lax.psum(own_wkey.astype(jnp.bfloat16), "ctx").astype(jnp.float32),
        lax.psum(own_wvalue.astype(jnp.bfloat16), "ctx").astype(jnp.float32),
        lax.psum(own_output.astype(jnp.bfloat16), "ctx").astype(jnp.float32),
        lax.psum(own_gain_two.astype(jnp.bfloat16), "ctx").astype(jnp.float32),
        lax.psum(own_router.astype(jnp.bfloat16), "ctx").astype(jnp.float32),
    )
    return (
        output_rows[None],
        grad_inputs.astype(jnp.bfloat16)[None],
        dense[0],
        dense[1],
        dense[2],
        dense[3],
        dense[4],
        dense[5],
        dense[6],
        own_shared_gate,
        own_shared_up,
        own_shared_down,
        own_expert_gate,
        own_expert_up,
        own_expert_down,
    )


def solution(mesh):
    fast = mesh.shape['ctx'] == 8 and mesh.shape['fsdp'] == NZ
    body = per_device_fast if fast else per_device
    return jax.shard_map(
        body,
        mesh=mesh,
        in_specs=(
            P("fsdp", "ctx", None),
            P("fsdp", "ctx"),
            P("fsdp", "ctx", None),
            P("fsdp", "ctx", None),
            P("fsdp"),
            P("fsdp", None),
            P("fsdp", None),
            P("fsdp", None),
            P("fsdp", None),
            P("fsdp"),
            P("fsdp", None),
            P("fsdp", None),
            P("fsdp", None),
            P("fsdp", None),
            P("ctx", "fsdp", None),
            P("ctx", "fsdp", None),
            P("ctx", "fsdp", None),
            P("fsdp", "ctx", None),
        ),
        out_specs=(
            P("fsdp", "ctx", None),
            P("fsdp", "ctx", None),
            P("fsdp"),
            P("fsdp", None),
            P("fsdp", None),
            P("fsdp", None),
            P("fsdp", None),
            P("fsdp"),
            P("fsdp", None),
            P("fsdp", None),
            P("fsdp", None),
            P("fsdp", None),
            P("ctx", "fsdp", None),
            P("ctx", "fsdp", None),
            P("ctx", "fsdp", None),
        ),
        check_vma=False,
    )
```

```python
import functools
import math

import jax
import jax.numpy as jnp
from jax import lax
from jax.experimental import pallas as pl
from jax.experimental.pallas import tpu as pltpu
from jax.sharding import PartitionSpec as P

D = 1280
HEADS = 10
HEAD_DIM = 128
TOPK = 7
EXP_DEV = 2


epsilon = 1e-06
theta_base = 10000.0
negative = -1e30
highest = lax.Precision.HIGHEST


def rotary_tables(positions, half_dim):
    frequency = theta_base ** (-jnp.arange(half_dim, dtype=jnp.float32) / half_dim)
    angles = positions.astype(jnp.float32)[:, None] * frequency[None, :]
    return (jnp.cos(angles)[:, None, :], jnp.sin(angles)[:, None, :])


def rotate(values, cosine, sine):
    half_dim = values.shape[-1] // 2
    leading = values[..., :half_dim]
    trailing = values[..., half_dim:]
    return jnp.concatenate(
        [leading * cosine - trailing * sine, trailing * cosine + leading * sine], axis=-1
    )


def unrotate(values, cosine, sine):
    half_dim = values.shape[-1] // 2
    leading = values[..., :half_dim]
    trailing = values[..., half_dim:]
    return jnp.concatenate(
        [leading * cosine + trailing * sine, trailing * cosine - leading * sine], axis=-1
    )


def blockwise(count, visit, initial):
    rows_each = math.gcd(count, 512)

    def advance(progress, number):
        return (visit(progress, number * rows_each, rows_each), None)

    final, ignored = lax.scan(advance, initial, jnp.arange(count // rows_each, dtype=jnp.int32))
    return final


def allowed_mask(query_pos, query_docs, key_pos, key_docs):
    return (key_pos[None, :] <= query_pos[:, None]) & (key_docs[None, :] == query_docs[:, None])


def rms_factor(values):
    return lax.rsqrt(jnp.mean(values * values, axis=-1, keepdims=True) + epsilon)


def silu_parts(values):
    sigma = jax.nn.sigmoid(values)
    return (values * sigma, sigma * (1.0 + values * (1.0 - sigma)))


def unchanged(progress):
    return progress


NZ = 4
SLOTS = 64
WIDE = 256
MESH = pl.DeviceIdType.MESH
PEERS = ((0, 1), (1, 0), (1, 1))
NN = (((1,), (0,)), ((), ()))
NT = (((1,), (1,)), ((), ()))
TN = (((0,), (0,)), ((), ()))
MIB = 1024 * 1024


def dot(left, right, dims=NN):
    return lax.dot_general(left, right, dims, preferred_element_type=jnp.float32)


def split_dot(left, right, dims=NN):
    high = left.astype(jnp.bfloat16)
    low = (left - high.astype(jnp.float32)).astype(jnp.bfloat16)
    return dot(high, right, dims) + dot(low, right, dims)


def flip(c, fy, fx, fk):
    return 4 * ((c // 4 + fy) % 2) + 2 * (((c // 2) % 2 + fx) % 2) + (c % 2 + fk) % 2


def rows_at(start, count):
    return pl.ds(pl.multiple_of(start, 16), count)


def lanes_at(start, count):
    return pl.ds(pl.multiple_of(start, 128), count)


def remote(src, dst, send, recv, c, z):
    return pltpu.make_async_remote_copy(
        src_ref=src, dst_ref=dst, send_sem=send, recv_sem=recv, device_id=(c, z), device_id_type=MESH
    )


def greet(c, z):
    barrier = pltpu.get_barrier_semaphore()
    peers = [(c, (z + d) % NZ) for d in range(1, NZ)]
    peers += [(flip(c, fy, fx, 0), z) for fy, fx in PEERS] + [(flip(c, 0, 0, 1), z)]
    for peer in peers:
        pl.semaphore_signal(barrier, inc=1, device_id=peer, device_id_type=MESH)
    pl.semaphore_wait(barrier, len(peers))


class Spread:
    def __init__(self, src, block, sems, c, z, hops=NZ, peers=PEERS, copy_own=True):
        self.src, self.block, self.c, self.z = src, block, c, z
        self.hops, self.peers, self.all = hops, peers, ((0, 0),) + peers
        self.local, self.zs, self.zr, self.xs, self.xr, self.ms, self.mr = sems
        self.own = pltpu.make_async_copy(src(z), block(c, z), self.local) if copy_own else None

    def at(self, c, d):
        return self.block(c, (self.z + NZ - d) % NZ)

    def mine(self, c, d):
        return self.src(self.z) if d == 0 else self.at(c, d)

    def zcopy(self, d):
        there = (self.z + d) % NZ
        return remote(
            self.src(there), self.block(self.c, self.z), self.zs.at[d - 1], self.zr.at[d - 1], self.c, there
        )

    def zwait(self, d):
        block = self.at(self.c, d)
        remote(block, block, self.zs.at[d - 1], self.zr.at[d - 1], self.c, self.z).wait_recv()

    def xcopy(self, i, d):
        there = flip(self.c, self.peers[i][0], self.peers[i][1], 0)
        return remote(self.mine(self.c, d), self.at(self.c, d), self.xs.at[i, d], self.xr.at[i, d], there, self.z)

    def xwait(self, i, d):
        block = self.at(flip(self.c, self.peers[i][0], self.peers[i][1], 0), d)
        remote(block, block, self.xs.at[i, d], self.xr.at[i, d], self.c, self.z).wait_recv()

    def mcopy(self, i, d):
        origin = flip(self.c, self.all[i][0], self.all[i][1], 0)
        src = self.mine(origin, d) if i == 0 else self.at(origin, d)
        return remote(src, self.at(origin, d), self.ms.at[i, d], self.mr.at[i, d], flip(self.c, 0, 0, 1), self.z)

    def mwait(self, i, d):
        block = self.at(flip(self.c, self.all[i][0], self.all[i][1], 1), d)
        remote(block, block, self.ms.at[i, d], self.mr.at[i, d], self.c, self.z).wait_recv()

    def start_z(self):
        if self.own is not None:
            self.own.start()
        for d in range(1, self.hops):
            self.zcopy(d).start()

    def start_x(self):
        for i in range(len(self.peers)):
            self.xcopy(i, 0).start()
        self.mcopy(0, 0).start()

    def relay_z(self):
        for d in range(1, self.hops):
            self.zwait(d)
            for i in range(len(self.peers)):
                self.xcopy(i, d).start()
            self.mcopy(0, d).start()

    def relay_x(self):
        for d in range(self.hops):
            for i in range(len(self.peers)):
                self.xwait(i, d)
                self.mcopy(i + 1, d).start()

    def arrive(self):
        if self.own is not None:
            self.own.wait()
        for d in range(self.hops):
            for i in range(len(self.all)):
                self.mwait(i, d)

    def drain(self):
        for d in range(1, self.hops):
            self.zcopy(d).wait_send()
        for d in range(self.hops):
            for i in range(len(self.peers)):
                self.xcopy(i, d).wait_send()
            for i in range(len(self.all)):
                self.mcopy(i, d).wait_send()


def spread_sems(hops=NZ, peers=3):
    dma = pltpu.SemaphoreType.DMA
    return [
        dma, dma((3,)), dma((3,)), dma((peers, hops)), dma((peers, hops)), dma((peers + 1, hops)), dma((peers + 1, hops)),
    ]


def plane_reduce(part, c, z, refs):
    out4, in4, out3, in3, ms, mr, xs, xr = refs
    mate = flip(c, 0, 0, 1)
    order = PEERS + ((0, 0),)

    def to_mate(i):
        return remote(out4.at[i], in4.at[i], ms.at[i], mr.at[i], mate, z)

    def to_chip(i):
        return remote(out3.at[i], in3.at[i], xs.at[i], xr.at[i], flip(c, PEERS[i][0], PEERS[i][1], 0), z)

    for i, (fy, fx) in enumerate(order):
        out4[i] = part(flip(c, fy, fx, 1)).astype(jnp.bfloat16)
        to_mate(i).start()
    for i, (fy, fx) in enumerate(order):
        value = part(flip(c, fy, fx, 0))
        to_mate(i).wait_recv()
        value = value + in4[i].astype(jnp.float32)
        if i < 3:
            out3[i] = value.astype(jnp.bfloat16)
            to_chip(i).start()
    for i in range(3):
        to_chip(i).wait_recv()
        value = value + in3[i].astype(jnp.float32)
    for i in range(4):
        to_mate(i).wait_send()
    for i in range(3):
        to_chip(i).wait_send()
    return value


def plane_scratch(length, width):
    dma = pltpu.SemaphoreType.DMA
    block = lambda n: pltpu.VMEM((n, length, width), jnp.bfloat16)
    return [block(4), block(4), block(3), block(3), dma((4,)), dma((4,)), dma((3,)), dma((3,))]


def swish(values):
    sigma = 1.0 / (1.0 + jnp.exp(-values))
    return values * sigma, sigma * (1.0 + values * (1.0 - sigma))


def norm_factor(values):
    return lax.rsqrt(jnp.mean(values * values, axis=1, keepdims=True) + epsilon)


def turned(values, cosine, sine):
    return values * cosine + pltpu.roll(values, 64, 1) * sine


def head_rows(c):
    blocks = [2 * c, 2 * c + 1, 16 + 2 * (c // 4), 17 + 2 * (c // 4)]
    return [(b, b // 5) for b in blocks]


def visible(first, count, keys, boundary):
    query = (lax.broadcasted_iota(jnp.int32, (count, 1), 0) + first).astype(jnp.float32)
    key = lax.broadcasted_iota(jnp.int32, (1, keys), 1).astype(jnp.float32)
    query_doc = jnp.where(query >= boundary, 1.0, 0.0)
    key_doc = jnp.where(key >= boundary, 1.0, 0.0)
    return (key <= query) & (key_doc == query_doc)


def attention_kernel(
    capacity,
    x_ref, p_ref, docs_ref, routes_ref, prio_ref, cos_ref, sin_ref, g_ref, wq_ref, wk_ref, wv_ref, wo_ref, wsend_ref,
    hidden_ref, b_ref, table_ref, gates_ref, psum_ref, bound_ref, aall, wall, woall, q1, k1, v1, q2, k2, v2,
    att1, lse1, att2, lse2, mixed, gall, wgu,
    xall, docs, pall, *sems,
):
    f32, bf16 = jnp.float32, jnp.bfloat16
    c = lax.axis_index("ctx")
    z = lax.axis_index("fsdp")
    length, width = x_ref.shape
    count = aall.shape[0]
    shard = width // NZ
    sub = shard // 4
    quarter = c % 4
    sems = list(sems)

    def take(n):
        taken = sems[:n]
        del sems[:n]
        return taken

    spread_x = Spread(lambda _: x_ref, lambda o, _: xall.at[o], take(7), c, z, 1)
    spread_docs = Spread(lambda _: docs_ref, lambda o, _: docs.at[o], take(7), c, z, 1)
    second = lambda o, s: wall.at[rows_at(s * shard + (o % 4) * sub, sub), 384:768]
    spread_h2 = Spread(lambda _: second(c, z), second, take(7), c, z, NZ, ((0, 1),), False)
    spread_g = Spread(lambda _: g_ref, lambda o, s: gall.at[o, s], take(7), c, z)
    shared_in = lambda s: wsend_ref.at[s, 2, rows_at((c // 2) * sub, sub), lanes_at(c % 2 * WIDE, WIDE)]
    shared_to = lambda o, s: wgu.at[2, rows_at(s * shard + (o // 2) * sub, sub), lanes_at(o % 2 * WIDE, WIDE)]
    spread_s = Spread(shared_in, shared_to, take(7), c, z)
    ps, pr, wl, w1s, w1r, wol, wos, wor, wgl, wgs, wgr = take(11)
    reduce_refs = take(8)
    greet(c, z)
    spread_x.start_z()
    spread_x.start_x()
    spread_docs.start_z()
    spread_docs.start_x()

    def pcopy(d):
        return remote(p_ref, pall.at[d - 1], ps.at[d - 1], pr.at[d - 1], c, (z + d) % NZ)

    for d in range(1, NZ):
        pcopy(d).start()
    own_rows = rows_at(z * shard, shard)
    sub_rows = rows_at(z * shard + quarter * sub, sub)
    copies = []
    for i, ref in enumerate((wq_ref, wk_ref, wv_ref)):
        copies.append(
            pltpu.make_async_copy(
                ref.at[:, lanes_at(c * 128, 128)], wall.at[own_rows, i * 128 : (i + 1) * 128], wl.at[i]
            )
        )
        copies.append(
            pltpu.make_async_copy(
                ref.at[rows_at(quarter * sub, sub), lanes_at((8 + c // 4) * 128, 128)],
                wall.at[sub_rows, 384 + i * 128 : 512 + i * 128],
                wl.at[3 + i],
            )
        )
    for copy in copies:
        copy.start()
    for copy in copies:
        copy.wait()

    def h1copy(d):
        return remote(
            wall.at[own_rows, 0:384], wall.at[own_rows, 0:384], w1s.at[d - 1], w1r.at[d - 1], c, (z + d) % NZ
        )

    def h1wait(d):
        here = wall.at[rows_at((z + NZ - d) % NZ * shard, shard), 0:384]
        remote(here, here, w1s.at[d - 1], w1r.at[d - 1], c, z).wait_recv()

    spread_h2.start_z()
    for d in range(1, NZ):
        h1copy(d).start()
    spread_h2.start_x()

    def wo_local(j):
        b, _ = head_rows(c)[j]
        return pltpu.make_async_copy(wo_ref.at[rows_at(b % 5 * 64, 64)], woall.at[64 * j : 64 * j + 64], wol.at[j])

    def wo_remote(j, d):
        b, _ = head_rows(c)[j]
        return remote(
            wo_ref.at[rows_at(b % 5 * 64, 64)], woall.at[64 * j : 64 * j + 64],
            wos.at[j, d - 1], wor.at[j], c, (z + d) % NZ,
        )

    for j, (_, owner) in enumerate(head_rows(c)):

        @pl.when(owner == z)
        def _(j=j):
            wo_local(j).start()
            for d in range(1, NZ):
                wo_remote(j, d).start()

    spread_x.relay_x()
    spread_docs.relay_x()
    packed = p_ref[...].astype(f32)
    for d in range(1, NZ):
        pcopy(d).wait_recv()
        packed = packed + pall[d - 1].astype(f32)
    psum_ref[...] = packed
    gain_one = packed[17:18]
    gain_two = packed[16:17]
    spread_x.arrive()

    def make_a(i, carry):
        values = xall[i].astype(f32)
        aall[rows_at(i * length, length)] = (values * norm_factor(values) * gain_one).astype(bf16)
        return carry

    lax.fori_loop(0, 8, make_a, 0)
    spread_h2.relay_z()
    spread_h2.relay_x()
    spread_h2.arrive()
    for d in range(1, NZ):
        h1wait(d)

    def wgcopy(d):
        there = (z + d) % NZ
        return remote(
            wsend_ref.at[there, 0:2], wgu.at[0:2, own_rows, :], wgs.at[d - 1], wgr.at[d - 1], c, there
        )

    def wgwait(d):
        here = wgu.at[0:2, rows_at((z + NZ - d) % NZ * shard, shard), :]
        remote(here, here, wgs.at[d - 1], wgr.at[d - 1], c, z).wait_recv()

    wgown = pltpu.make_async_copy(wsend_ref.at[z, 0:2], wgu.at[0:2, own_rows, :], wgl)
    spread_g.start_z()
    spread_g.start_x()
    spread_s.start_z()
    spread_s.start_x()
    wgown.start()
    for d in range(1, NZ):
        wgcopy(d).start()
    step = 2 * length
    for i in range(count // step):
        part = slice(i * step, (i + 1) * step)
        values = dot(aall[part], wall[...])
        cosine, sine = cos_ref[part], sin_ref[part]
        q1[part] = turned(values[:, 0:128], cosine, sine).astype(bf16)
        k1[part] = turned(values[:, 128:256], cosine, sine).astype(bf16)
        v1[part] = values[:, 256:384].astype(bf16)
        q2[part] = turned(values[:, 384:512], cosine, sine).astype(bf16)
        k2[part] = turned(values[:, 512:640], cosine, sine).astype(bf16)
        v2[part] = values[:, 640:768].astype(bf16)
    spread_docs.arrive()
    flags = jnp.where(docs[...] == 0.0, 1.0, 0.0)
    boundary = jnp.sum(jnp.sum(flags, axis=0), axis=(0, 1), keepdims=True)
    bound_ref[...] = jnp.broadcast_to(boundary, bound_ref.shape)
    spread_g.relay_z()
    spread_s.relay_z()

    def attend(queries, first, keys, values, n):
        scores = dot(queries, keys[0:n], NT) * (HEAD_DIM**-0.5)
        scores = jnp.where(visible(first, step, n, boundary), scores, negative)
        top = jnp.max(scores, axis=1, keepdims=True)
        shares = jnp.exp(scores - top)
        total = jnp.sum(shares, axis=1, keepdims=True)
        probs = (shares * (1.0 / total)).astype(bf16)
        return dot(probs, values[0:n]), jnp.broadcast_to(top + jnp.log(total), (step, 128))

    mixed[...] = jnp.zeros_like(mixed)
    for i in range(count // step):
        part = slice(i * step, (i + 1) * step)
        out, lse = attend(q1[part], i * step, k1, v1, (i + 1) * step)
        att1[part] = out
        lse1[part] = lse
        mixed[part, 0:128] = out.astype(bf16)
    mine = rows_at(quarter * step, step)
    out, lse = attend(q2[mine], quarter * step, k2, v2, count)
    att2[...] = out
    lse2[...] = lse
    mixed[mine, 128:256] = out.astype(bf16)
    spread_s.relay_x()
    for j, (_, owner) in enumerate(head_rows(c)):

        @pl.when(owner == z)
        def _(j=j):
            wo_local(j).wait()
            for d in range(1, NZ):
                wo_remote(j, d).wait_send()

        @pl.when(owner != z)
        def _(j=j):
            wo_remote(j, 1).wait_recv()

    value = plane_reduce(lambda o: dot(mixed[rows_at(o * length, length)], woall[...]), c, z, reduce_refs)
    hidden = x_ref[...].astype(f32) + value
    hidden_ref[...] = hidden
    tokens = (hidden * norm_factor(hidden) * gain_two).astype(bf16)
    b_ref[...] = tokens
    logits = dot(packed[0:16].astype(bf16), tokens, NT)
    shifted = jnp.exp(logits - jnp.max(logits, axis=0, keepdims=True))
    gates = shifted / jnp.sum(shifted, axis=0, keepdims=True)
    gates_ref[...] = gates
    lane = lax.broadcasted_iota(jnp.int32, (length, 128), 1)
    named = jnp.zeros((length, 128), f32)
    for k in range(routes_ref.shape[1]):
        named = named + jnp.where(lane == routes_ref[:, k : k + 1], 1.0, 0.0)
    named = named.T[0:16]
    order = jnp.broadcast_to(prio_ref[...].astype(f32), (length, length))
    earlier = jnp.where(order.T < order, 1.0, 0.0).astype(bf16)
    rank = dot(named.astype(bf16), earlier)
    kept = (named > 0.0) & (rank < float(capacity))
    table_ref[:, 0:length] = jnp.where(kept, rank, -1.0)
    table_ref[:, length : 2 * length] = jnp.where(kept, gates, 0.0)
    spread_g.relay_x()
    spread_g.arrive()
    spread_s.arrive()
    wgown.wait()
    for d in range(1, NZ):
        wgwait(d)
        wgcopy(d).wait_send()
        h1copy(d).wait_send()
        pcopy(d).wait_send()
    for spread in (spread_x, spread_docs, spread_h2, spread_g, spread_s):
        spread.drain()


def attention_stage(capacity, x, packed, docs, routes, prio, cosine, sine, upstream, wq, wk, wv, wo, wsend):
    length, width = x.shape
    count = cosine.shape[0]
    dma = pltpu.SemaphoreType.DMA
    hbm = pl.BlockSpec(memory_space=pl.ANY)
    vmem = pl.BlockSpec(memory_space=pltpu.VMEM)
    f32, bf16 = jnp.float32, jnp.bfloat16
    shape = jax.ShapeDtypeStruct
    head = lambda rows, kind: shape((rows, HEAD_DIM), kind)
    return pl.pallas_call(
        functools.partial(attention_kernel, capacity),
        name="attention",
        out_shape=[
            shape((length, width), f32), shape((length, width), bf16), shape((16, 2 * length), f32),
            shape((16, length), f32), shape((32, width), f32), shape((8, 128), f32),
            shape((count, width), bf16), shape((width, 768), bf16), shape((256, width), bf16),
            head(count, bf16), head(count, bf16), head(count, bf16), head(count, bf16), head(count, bf16),
            head(count, bf16), head(count, f32), head(count, f32), head(2 * length, f32), head(2 * length, f32),
            shape((count, 256), bf16), shape((8, NZ, length, width), bf16), shape((3, width, 2 * WIDE), bf16),
        ],
        in_specs=[vmem] * 7 + [hbm] * 6,
        out_specs=[vmem] * 20 + [hbm] * 2,
        scratch_shapes=[
            pltpu.VMEM((8, length, width), bf16), pltpu.VMEM((8, 8, 128), f32), pltpu.VMEM((3, 32, width), bf16),
        ]
        + spread_sems(1) + spread_sems(1) + spread_sems(NZ, 1) + spread_sems() + spread_sems()
        + [
            dma((3,)), dma((3,)), dma((6,)), dma((3,)), dma((3,)), dma((4,)), dma((4, 3)), dma((4,)),
            dma, dma((3,)), dma((3,)),
        ]
        + plane_scratch(length, width),
        compiler_params=pltpu.CompilerParams(
            collective_id=2, has_side_effects=True, vmem_limit_bytes=60 * MIB
        ),
    )(x, packed, docs, routes, prio, cosine, sine, upstream, wq, wk, wv, wo, wsend)


def expert_kernel(
    b_ref, t_ref, gall, wgu, wdn_ref,
    y_ref, db_ref, dg_ref, dgu_ref, ddn_ref, dsgu_ref, dsdn_ref, ball, tall, mrecv, xrecv,
    acc, bg, gg, tg, oh, xs, gs, ys, ds, st, ld, zbuf, zrecv, gst,
    sb0, sb1, sb2, sb3, sb4, sb5, sb6, st0, st1, st2, st3, st4, st5, st6,
    lsem, ms, mr, xs_s, xs_r, ldsem, zs, zr, gl, gss, grs,
):
    c = lax.axis_index("ctx")
    z = lax.axis_index("fsdp")
    f32, bf16 = jnp.float32, jnp.bfloat16
    mate = flip(c, 0, 0, 1)
    length = b_ref.shape[0]
    group = NZ * length
    rows = wgu.shape[1] // NZ
    greet(c, z)
    spread_b = Spread(lambda _: b_ref, lambda o, q: ball.at[o, q], (sb0, sb1, sb2, sb3, sb4, sb5, sb6), c, z)
    spread_t = Spread(lambda _: t_ref, lambda o, q: tall.at[o, q], (st0, st1, st2, st3, st4, st5, st6), c, z)
    for spread in (spread_t, spread_b):
        spread.start_z()
        spread.start_x()
    acc[...] = jnp.zeros_like(acc)
    ddn_ref[...] = jnp.zeros_like(ddn_ref)
    st[...] = jnp.zeros_like(st)
    zbuf[...] = jnp.zeros_like(zbuf)
    spread_t.relay_z()
    spread_b.relay_z()
    spread_t.relay_x()
    spread_b.relay_x()
    spread_t.arrive()
    spread_b.arrive()

    def target(g):
        left = 3 - g // 2
        return flip(c, left % 2, left // 2, 1 - g % 2)

    def loads(g):
        slot = g % 2
        there = target(g)
        return (
            pltpu.make_async_copy(ball.at[there], bg.at[slot], lsem.at[slot, 0]),
            pltpu.make_async_copy(gall.at[there], gg.at[slot], lsem.at[slot, 1]),
            pltpu.make_async_copy(tall.at[there], tg.at[slot], lsem.at[slot, 2]),
        )

    def to_mate(s):
        return remote(st.at[0], mrecv.at[s], ms.at[s], mr.at[s], mate, z)

    def to_chip(s):
        left = 3 - s
        return remote(st.at[1], xrecv.at[s], xs_s.at[s], xs_r.at[s], flip(c, left % 2, left // 2, 0), z)

    for copy in loads(0):
        copy.start()
    slot_ids = lax.broadcasted_iota(jnp.int32, (SLOTS, length), 0).astype(f32)
    row_ids = lax.broadcasted_iota(jnp.int32, (16, length), 0)
    table_rows = lax.broadcasted_iota(jnp.int32, (16, 2 * length), 0)

    def step(g, carry):
        slot = g % 2
        s = g // 2
        par = g % 2
        for copy in loads(g):
            copy.wait()

        @pl.when(g < 7)
        def _():
            for copy in loads(g + 1):
                copy.start()

        @pl.when((s > 0) & (par == 0))
        def _():
            to_mate(s - 1).wait_send()

        @pl.when((s > 0) & (par == 1))
        def _():
            to_chip(s - 1).wait_send()

        scales = [[], []]
        for q in range(NZ):
            hits = []
            for e in range(2):
                mine = jnp.sum(jnp.where(table_rows == 2 * c + e, tg[slot, q], 0.0), axis=0, keepdims=True)
                rank = mine[:, :length]
                share = mine[:, length:]
                hit = slot_ids == rank
                scales[e].append(jnp.sum(jnp.where(hit, share, 0.0), axis=1, keepdims=True))
                hits.append(jnp.where(hit, 1.0, 0.0))
            hot = jnp.concatenate(hits, axis=0).astype(bf16)
            oh[q] = hot
            part = dot(hot, bg[slot, q]).astype(bf16)
            xs[0, q * SLOTS : (q + 1) * SLOTS] = part[:SLOTS]
            xs[1, q * SLOTS : (q + 1) * SLOTS] = part[SLOTS:]
            part = dot(hot, gg[slot, q]).astype(bf16)
            gs[0, q * SLOTS : (q + 1) * SLOTS] = part[:SLOTS]
            gs[1, q * SLOTS : (q + 1) * SLOTS] = part[SLOTS:]
        back = [0.0] * NZ
        for e in range(2):
            scale = jnp.concatenate(scales[e], axis=0)
            both = dot(xs[e], wgu[e])
            up = both[:, WIDE:]
            silu, slope = swish(both[:, :WIDE])
            inner = (silu * up).astype(bf16)
            scaled = (inner.astype(f32) * scale).astype(bf16)
            out = dot(scaled, wdn_ref[e]).astype(bf16)
            pull = dot(gs[e], wdn_ref[e], NT)
            gain = jnp.sum(inner.astype(f32) * pull, axis=1, keepdims=True)
            pull = pull * scale
            turn = jnp.concatenate([(pull * up * slope).astype(bf16), (pull * silu).astype(bf16)], axis=1)
            ddn_ref[e] += dot(scaled, gs[e], TN)
            acc[e] += dot(xs[e], turn, TN)
            into = dot(turn, wgu[e], NT).astype(bf16)
            for q in range(NZ):
                part = slice(q * SLOTS, (q + 1) * SLOTS)
                ys[q, e * SLOTS : (e + 1) * SLOTS] = out[part]
                ds[q, e * SLOTS : (e + 1) * SLOTS] = into[part]
                hit = oh[q, e * SLOTS : (e + 1) * SLOTS].astype(f32)
                line = jnp.sum(hit * gain[part], axis=0, keepdims=True)
                back[q] = back[q] + jnp.where(row_ids == 2 * c + e, line, 0.0)
        for q in range(NZ):
            st[par, q * length : (q + 1) * length] = dot(oh[q], ds[q], TN).astype(bf16)
            st[par, group + q * length : group + (q + 1) * length] = dot(oh[q], ys[q], TN).astype(bf16)
            st[par, 2 * group :, q * length : (q + 1) * length] = back[q].astype(bf16)

        @pl.when(g == 7)
        def _():
            for h in range(2):
                tokens = bg[slot, 2 * h : 2 * h + 2].reshape(2 * length, bg.shape[3])
                upper = gg[slot, 2 * h : 2 * h + 2].reshape(2 * length, bg.shape[3])
                both = dot(tokens, wgu[2])
                up = both[:, WIDE:]
                silu, slope = swish(both[:, :WIDE])
                inner = (silu * up).astype(bf16)
                part = slice(2 * h * length, 2 * (h + 1) * length)
                more = slice(group + 2 * h * length, group + 2 * (h + 1) * length)
                st[1, more] = (st[1, more].astype(f32) + dot(inner, wdn_ref[2])).astype(bf16)
                pull = dot(upper, wdn_ref[2], NT)
                turn = jnp.concatenate([(pull * up * slope).astype(bf16), (pull * silu).astype(bf16)], axis=1)
                st[1, part] = (st[1, part].astype(f32) + dot(turn, wgu[2], NT)).astype(bf16)
                if h == 0:
                    dsdn_ref[...] = dot(inner, upper, TN)
                    dsgu_ref[...] = dot(tokens, turn, TN)
                else:
                    dsdn_ref[...] += dot(inner, upper, TN)
                    dsgu_ref[...] += dot(tokens, turn, TN)

        @pl.when(par == 0)
        def _():
            to_mate(s).start()

        @pl.when(par == 1)
        def _():
            to_mate(s).wait_recv()
            copy = pltpu.make_async_copy(mrecv.at[s], ld.at[0], ldsem.at[0])
            copy.start()
            copy.wait()

            def add(i, carry):
                part = pl.ds(pl.multiple_of(i * 16, 16), 16)
                st[1, part] = (st[1, part].astype(f32) + ld[0, part].astype(f32)).astype(bf16)
                return carry

            lax.fori_loop(0, st.shape[1] // 16, add, 0)

            @pl.when(s < 3)
            def _():
                to_chip(s).start()

        return carry

    lax.fori_loop(0, 8, step, 0)
    to_mate(3).wait_send()
    for e in range(2):
        gst[e] = acc[e].astype(bf16)

    def gcopy(d):
        there = (z + d) % NZ
        return remote(
            gst.at[:, pl.ds(pl.multiple_of(there * rows, rows), rows), :], dgu_ref.at[z],
            gss.at[d - 1], grs.at[d - 1], c, there,
        )

    gown = pltpu.make_async_copy(gst.at[:, pl.ds(pl.multiple_of(z * rows, rows), rows), :], dgu_ref.at[z], gl)
    gown.start()
    for i in range(3):
        to_chip(i).wait_recv()
        pltpu.make_async_copy(xrecv.at[i], ld.at[i], ldsem.at[i]).start()
    for i in range(3):
        pltpu.make_async_copy(xrecv.at[i], ld.at[i], ldsem.at[i]).wait()

    def total(part, lanes=slice(None)):
        value = st[1, part, lanes].astype(f32)
        for i in range(3):
            value = value + ld[i, part, lanes].astype(f32)
        return value.astype(bf16)

    for q in range(NZ):

        def add(i, carry):
            base = pl.multiple_of(i * 16, 16)
            zbuf[q, pl.ds(base, 16)] = total(pl.ds(pl.multiple_of(base + q * length, 16), 16))
            zbuf[q, pl.ds(pl.multiple_of(base + length, 16), 16)] = total(
                pl.ds(pl.multiple_of(base + group + q * length, 16), 16)
            )
            return carry

        lax.fori_loop(0, length // 16, add, 0)
        zbuf[q, 2 * length : 2 * length + 16, 0:length] = total(
            slice(2 * group, 2 * group + 16), slice(q * length, (q + 1) * length)
        )

    def zcopy(d):
        there = (z + d) % NZ
        return remote(zbuf.at[there], zrecv.at[d - 1], zs.at[d - 1], zr.at[d - 1], c, there)

    for d in range(1, NZ):
        zcopy(d).start()
    for d in range(1, NZ):
        gcopy(d).start()
    for d in range(1, NZ):
        zcopy(d).wait_recv()

    def settle(i, carry):
        base = pl.multiple_of(i * 16, 16)
        for ref, start in ((db_ref, 0), (y_ref, length)):
            part = pl.ds(pl.multiple_of(base + start, 16), 16)
            value = zbuf[z, part].astype(f32)
            for d in range(3):
                value = value + zrecv[d, part].astype(f32)
            ref[pl.ds(base, 16)] = value
        return carry

    lax.fori_loop(0, length // 16, settle, 0)
    last = slice(2 * length, 2 * length + 16)
    value = zbuf[z, last, 0:length].astype(f32)
    for d in range(3):
        value = value + zrecv[d, last, 0:length].astype(f32)
    dg_ref[...] = value
    for d in range(1, NZ):
        zcopy(d).wait_send()
        gcopy(d).wait()
    gown.wait()
    spread_t.drain()
    spread_b.drain()


def expert_stage(moe_input, table, gall, wgu, wdn):
    length, width = moe_input.shape
    dma = pltpu.SemaphoreType.DMA
    hbm = pl.BlockSpec(memory_space=pl.ANY)
    vmem = pl.BlockSpec(memory_space=pltpu.VMEM)
    f32, bf16 = jnp.float32, jnp.bfloat16
    shape = jax.ShapeDtypeStruct
    inner = 2 * WIDE
    group = NZ * length
    rows = width // NZ
    return pl.pallas_call(
        expert_kernel,
        name="experts",
        out_shape=[
            shape((length, width), f32),
            shape((length, width), f32),
            shape((16, length), f32),
            shape((NZ, 2, rows, inner), bf16),
            shape((2, WIDE, width), f32),
            shape((width, inner), f32),
            shape((WIDE, width), f32),
            shape((8, NZ, length, width), bf16),
            shape((8, NZ, 16, 2 * length), f32),
            shape((4, 2 * group + 16, width), bf16),
            shape((3, 2 * group + 16, width), bf16),
        ],
        in_specs=[hbm, hbm, hbm, vmem, vmem],
        out_specs=[vmem, vmem, vmem, hbm, vmem, vmem, vmem, hbm, hbm, hbm, hbm],
        scratch_shapes=[
            pltpu.VMEM((2, width, inner), f32),
            pltpu.VMEM((2, NZ, length, width), bf16),
            pltpu.VMEM((2, NZ, length, width), bf16),
            pltpu.VMEM((2, NZ, 16, 2 * length), f32),
            pltpu.VMEM((NZ, 2 * SLOTS, length), bf16),
            pltpu.VMEM((2, NZ * SLOTS, width), bf16),
            pltpu.VMEM((2, NZ * SLOTS, width), bf16),
            pltpu.VMEM((NZ, 2 * SLOTS, width), bf16),
            pltpu.VMEM((NZ, 2 * SLOTS, width), bf16),
            pltpu.VMEM((2, 2 * group + 16, width), bf16),
            pltpu.VMEM((3, 2 * group + 16, width), bf16),
            pltpu.VMEM((NZ, 2 * length + 16, width), bf16),
            pltpu.VMEM((3, 2 * length + 16, width), bf16),
            pltpu.VMEM((2, width, inner), bf16),
        ]
        + spread_sems() + spread_sems()
        + [
            dma((2, 3)), dma((4,)), dma((4,)), dma((3,)), dma((3,)), dma((3,)),
            dma((3,)), dma((3,)), dma, dma((3,)), dma((3,)),
        ],
        compiler_params=pltpu.CompilerParams(
            collective_id=1, has_side_effects=True, vmem_limit_bytes=60 * MIB
        ),
    )(moe_input, table, gall, wgu, wdn)


def backward_kernel(
    db_ref, dg_ref, g_ref, x_ref, hidden_ref, b_ref, gates_ref, psum_ref, bound_ref, cos_ref, sin_ref,
    aall, wall, woall, q1, k1, v1, q2, k2, v2, att1, lse1, att2, lse2, mixed,
    gtok_ref, small_ref, gwq_ref, gwk_ref, gwv_ref, gwo_ref,
    dhb, dhall, dm, dk, dv, cat, wst, wrecv, wsum, wfinal, dwo, worecv, wosum, wofinal, small4, *sems,
):
    f32, bf16 = jnp.float32, jnp.bfloat16
    c = lax.axis_index("ctx")
    z = lax.axis_index("fsdp")
    length, width = x_ref.shape
    count = aall.shape[0]
    shard = width // NZ
    quarter = c % 4
    mate = flip(c, 0, 0, 1)
    scale = HEAD_DIM**-0.5
    sems = list(sems)

    def take(n):
        taken = sems[:n]
        del sems[:n]
        return taken

    spread_h = Spread(lambda _: dhb, lambda o, _: dhall.at[o], take(7), c, z, 1)
    spread_w = Spread(lambda _: wsum, lambda o, _: wfinal.at[o], take(7), c, z, 1)
    wzs, wzr, ozs, ozr, oxs, oxr, oms, omr, ss, sr = take(10)
    reduce_refs = take(8)
    greet(c, z)
    packed = psum_ref[...]
    gain_one = packed[17:18]
    gain_two = packed[16:17]
    router = packed[0:16].astype(bf16)
    hidden = hidden_ref[...]
    factor_two = norm_factor(hidden)
    normed_two = hidden * factor_two
    gates = gates_ref[...]
    d_gates = dg_ref[...]
    d_logits = gates * (d_gates - jnp.sum(gates * d_gates, axis=0, keepdims=True))
    d_b = db_ref[...] + split_dot(d_logits, router, TN)
    small_ref[...] = jnp.zeros_like(small_ref)
    small_ref[0:16] = split_dot(d_logits, b_ref[...])
    small_ref[16:17] = jnp.sum(d_b * normed_two, axis=0, keepdims=True)
    pulled = d_b * gain_two
    d_hidden = g_ref[...].astype(f32) + factor_two * (
        pulled - normed_two * jnp.mean(pulled * normed_two, axis=1, keepdims=True)
    )
    dhb[...] = d_hidden.astype(bf16)
    spread_h.start_z()
    spread_h.start_x()
    dk[...] = jnp.zeros_like(dk)
    dv[...] = jnp.zeros_like(dv)
    cat[:, 384:512] = jnp.zeros((count, 128), bf16)
    spread_h.relay_x()
    spread_h.arrive()
    step = 2 * length
    for i in range(count // step):
        block = dhall[2 * i : 2 * i + 2].reshape(step, width)
        dm[i * step : (i + 1) * step] = dot(block, woall[...], NT).astype(bf16)
        part = dot(mixed[i * step : (i + 1) * step], block, TN)
        if i == 0:
            dwo[...] = part
        else:
            dwo[...] += part
    wosum[...] = dwo[...].astype(bf16).reshape(wosum.shape)

    def oz(j, owner):
        d = (owner + NZ - z) % NZ
        return remote(wosum.at[j], worecv.at[j, d - 1], ozs.at[j], ozr.at[j, d - 1], c, owner)

    def oz_wait(j, d):
        return remote(wosum.at[j], worecv.at[j, d], ozs.at[j], ozr.at[j, d], c, z)

    for j, (_, owner) in enumerate(head_rows(c)):

        @pl.when(owner != z)
        def _(j=j, owner=owner):
            oz(j, owner).start()

    boundary = bound_ref[0:1, 0:1]

    def pull_back(queries, first, keys, values, n, upper, out, lse, which):
        scores = dot(queries, keys[0:n], NT) * scale
        scores = jnp.where(visible(first, step, n, boundary), scores, negative)
        shares = jnp.exp(scores - lse[:, 0:1])
        delta = jnp.sum(upper.astype(f32) * out, axis=1, keepdims=True)
        pulled = (scale * (shares * (dot(upper, values[0:n], NT) - delta))).astype(bf16)
        dk[which, 0:n] += dot(pulled, queries, TN)
        dv[which, 0:n] += dot(shares.astype(bf16), upper, TN)
        return dot(pulled, keys[0:n]).astype(bf16).astype(f32)

    for i in range(count // step):
        part = slice(i * step, (i + 1) * step)
        got = pull_back(q1[part], i * step, k1, v1, (i + 1) * step, dm[part, 0:128], att1[part], lse1[part], 0)
        cat[part, 0:128] = turned(got, cos_ref[part], -sin_ref[part]).astype(bf16)
    mine = rows_at(quarter * step, step)
    got = pull_back(q2[mine], quarter * step, k2, v2, count, dm[mine, 128:256], att2[...], lse2[...], 1)
    cat[mine, 384:512] = turned(got, cos_ref[mine], -sin_ref[mine]).astype(bf16)
    for which in range(2):
        at = 384 * which
        keys = dk[which].astype(bf16).astype(f32)
        cat[:, at + 128 : at + 256] = turned(keys, cos_ref[...], -sin_ref[...]).astype(bf16)
        cat[:, at + 256 : at + 384] = dv[which].astype(bf16)
    for i in range(width // 256):
        wst[256 * i : 256 * i + 256] = dot(aall[:, 256 * i : 256 * i + 256], cat[...], TN).astype(bf16)

    def wz(d):
        there = (z + d) % NZ
        return remote(
            wst.at[rows_at(there * shard, shard)], wrecv.at[d - 1], wzs.at[d - 1], wzr.at[d - 1], c, there
        )

    for d in range(1, NZ):
        wz(d).start()

    def ox(j, i):
        there = flip(c, PEERS[i][0], PEERS[i][1], 0)
        return remote(wosum.at[j], wofinal.at[c, j], oxs.at[j, i], oxr.at[j, i], there, z)

    def om(j, i):
        fy, fx = (((0, 0),) + PEERS)[i]
        origin = flip(c, fy, fx, 0)
        src = wosum.at[j] if i == 0 else wofinal.at[origin, j]
        return remote(src, wofinal.at[origin, j], oms.at[j, i], omr.at[j, i], mate, z)

    for j, (_, owner) in enumerate(head_rows(c)):

        @pl.when(owner == z)
        def _(j=j):
            for d in range(3):
                oz_wait(j, d).wait_recv()
            total = wosum[j].astype(f32)
            for d in range(3):
                total = total + worecv[j, d].astype(f32)
            wosum[j] = total.astype(bf16)
            wofinal[c, j] = total.astype(bf16)
            for i in range(3):
                ox(j, i).start()
            om(j, 0).start()

    value = plane_reduce(
        lambda o: dot(cat[rows_at(o * length, length)], wall[...], NT), c, z, reduce_refs
    )
    x = x_ref[...].astype(f32)
    factor_one = norm_factor(x)
    normed_one = x * factor_one
    small_ref[17:18] = jnp.sum(value * normed_one, axis=0, keepdims=True)
    pulled = value * gain_one
    gtok_ref[...] = (
        d_hidden
        + factor_one * (pulled - normed_one * jnp.mean(pulled * normed_one, axis=1, keepdims=True))
    ).astype(bf16)

    total = wst[rows_at(z * shard, shard)].astype(f32)
    for d in range(1, NZ):
        wz(d).wait_recv()
        total = total + wrecv[d - 1].astype(f32)
    wsum[...] = total.astype(bf16)
    spread_w.start_z()
    spread_w.start_x()

    def exchange(stage, slots, targets):
        copies = [
            remote(small4.at[stage], small4.at[slot], ss.at[slot], sr.at[slot], tc, tz)
            for slot, (tc, tz) in zip(slots, targets)
        ]
        for copy in copies:
            copy.start()
        for copy in copies:
            copy.wait_recv()
        value = small4[stage]
        for slot in slots:
            value = value + small4[slot]
        return value, copies

    small4[0] = small_ref[...]
    value, sent = exchange(0, (1,), ((mate, z),))
    small4[2] = value
    value, more = exchange(2, (3, 4, 5), [(flip(c, fy, fx, 0), z) for fy, fx in PEERS])
    sent += more
    small4[6] = value
    value, more = exchange(6, (7, 8, 9), [(c, (z + d) % NZ) for d in range(1, NZ)])
    sent += more
    small_ref[...] = value
    for i in range(3):
        for j, (_, owner) in enumerate(head_rows(flip(c, PEERS[i][0], PEERS[i][1], 0))):

            @pl.when(owner == z)
            def _(j=j, i=i):
                origin = flip(c, PEERS[i][0], PEERS[i][1], 0)
                block = wofinal.at[origin, j]
                remote(block, block, oxs.at[j, i], oxr.at[j, i], c, z).wait_recv()
                om(j, i + 1).start()

    spread_w.relay_x()
    for i in range(4):
        fy, fx = (((0, 0),) + PEERS)[i]
        for j, (_, owner) in enumerate(head_rows(flip(c, fy, fx, 1))):

            @pl.when(owner == z)
            def _(j=j, i=i, fy=fy, fx=fx):
                block = wofinal.at[flip(c, fy, fx, 1), j]
                remote(block, block, oms.at[j, i], omr.at[j, i], c, z).wait_recv()

    for i in range(5):
        b = 5 * z + i

        @pl.when(b < 16)
        def _(b=b, i=i):
            low = jnp.minimum(b, 15)
            gwo_ref[64 * i : 64 * i + 64] = wofinal[low // 2, low % 2].astype(f32)

        @pl.when(b >= 16)
        def _(b=b, i=i):
            high = jnp.maximum(b, 16) - 16
            gwo_ref[64 * i : 64 * i + 64] = sum(
                wofinal[4 * (high // 2) + k, 2 + high % 2].astype(f32) for k in range(4)
            )

    spread_w.arrive()
    for n, ref in enumerate((gwq_ref, gwk_ref, gwv_ref)):
        for o in range(8):
            ref[:, 128 * o : 128 * o + 128] = wfinal[o, :, 128 * n : 128 * n + 128].astype(f32)
        for y in range(2):
            lanes = slice(384 + 128 * n, 512 + 128 * n)
            ref[:, 1024 + 128 * y : 1152 + 128 * y] = sum(
                wfinal[4 * y + k, :, lanes].astype(f32) for k in range(4)
            )
    for copy in sent:
        copy.wait_send()
    for j, (_, owner) in enumerate(head_rows(c)):

        @pl.when(owner != z)
        def _(j=j, owner=owner):
            oz(j, owner).wait_send()

        @pl.when(owner == z)
        def _(j=j):
            for i in range(3):
                ox(j, i).wait_send()
            om(j, 0).wait_send()

    for i in range(3):
        for j, (_, owner) in enumerate(head_rows(flip(c, PEERS[i][0], PEERS[i][1], 0))):

            @pl.when(owner == z)
            def _(j=j, i=i):
                om(j, i + 1).wait_send()

    for d in range(1, NZ):
        wz(d).wait_send()
    spread_h.drain()
    spread_w.drain()


def backward_stage(*operands):
    x, aall = operands[3], operands[11]
    length, width = x.shape
    count = aall.shape[0]
    shard = width // NZ
    dma = pltpu.SemaphoreType.DMA
    vmem = pl.BlockSpec(memory_space=pltpu.VMEM)
    f32, bf16 = jnp.float32, jnp.bfloat16
    shape = jax.ShapeDtypeStruct
    return pl.pallas_call(
        backward_kernel,
        name="backward",
        out_shape=[
            shape((length, width), bf16), shape((32, width), f32), shape((shard, width), f32),
            shape((shard, width), f32), shape((shard, width), f32), shape((shard, width), f32),
        ],
        in_specs=[vmem] * len(operands),
        out_specs=[vmem] * 6,
        scratch_shapes=[
            pltpu.VMEM((length, width), bf16), pltpu.VMEM((8, length, width), bf16), pltpu.VMEM((count, 256), bf16),
            pltpu.VMEM((2, count, 128), f32), pltpu.VMEM((2, count, 128), f32), pltpu.VMEM((count, 768), bf16),
            pltpu.VMEM((width, 768), bf16), pltpu.VMEM((3, shard, 768), bf16), pltpu.VMEM((shard, 768), bf16),
            pltpu.VMEM((8, shard, 768), bf16), pltpu.VMEM((256, width), f32), pltpu.VMEM((4, 3, 64, width), bf16),
            pltpu.VMEM((4, 64, width), bf16), pltpu.VMEM((8, 4, 64, width), bf16), pltpu.VMEM((10, 32, width), f32),
        ]
        + spread_sems(1) + spread_sems(1)
        + [
            dma((3,)), dma((3,)), dma((4,)), dma((4, 3)), dma((4, 3)), dma((4, 3)), dma((4, 4)), dma((4, 4)),
            dma((10,)), dma((10,)),
        ]
        + plane_scratch(length, width),
        compiler_params=pltpu.CompilerParams(
            collective_id=3, has_side_effects=True, vmem_limit_bytes=60 * MIB
        ),
    )(*operands)


def per_device_fast(
    tokens,
    documents,
    routes,
    priority,
    attention_gain,
    query_weight,
    key_weight,
    value_weight,
    output_weight,
    feedforward_gain,
    router_weight,
    shared_gate,
    shared_up,
    shared_down,
    expert_gate,
    expert_up,
    expert_down,
    cotangent,
):
    f32, bf16 = jnp.float32, jnp.bfloat16
    z = lax.axis_index("fsdp")
    length = tokens.shape[1]
    row_length = length * 8
    experts = EXP_DEV * 8
    capacity = 9 * length * TOPK // (8 * experts)
    shard = query_weight.shape[0]
    hidden_dev = expert_gate.shape[2] // NZ
    cosine, sine = rotary_tables(jnp.arange(row_length, dtype=jnp.int32), HEAD_DIM // 2)
    cosine, sine = cosine[:, 0], sine[:, 0]
    cosine_wide = jnp.concatenate([cosine, cosine], axis=1)
    sine_wide = jnp.concatenate([-sine, sine], axis=1)
    small = jnp.concatenate(
        [router_weight.T, feedforward_gain[None], attention_gain[None], jnp.zeros((14, shard), bf16)], axis=0
    )
    packed = lax.dynamic_update_slice(jnp.zeros((32, NZ * shard), bf16), small, (0, z * shard))
    docs = jnp.concatenate([documents.astype(f32), jnp.ones((7, length), f32)], axis=0)

    def slices(weights):
        parts = weights.reshape(weights.shape[0], weights.shape[1], NZ, hidden_dev)
        parts = jnp.pad(parts, ((0, 0), (0, 0), (0, 0), (0, WIDE - hidden_dev)))
        return jnp.transpose(parts, (2, 0, 1, 3))

    wsend = jnp.concatenate(
        [
            jnp.concatenate([slices(expert_gate), slices(shared_gate[None])], axis=1),
            jnp.concatenate([slices(expert_up), slices(shared_up[None])], axis=1),
        ],
        axis=3,
    )
    wdn = jnp.pad(
        jnp.concatenate([expert_down, shared_down[None]], axis=0), ((0, 0), (0, WIDE - hidden_dev), (0, 0))
    )
    front = attention_stage(
        capacity, tokens[0], packed, docs, routes[0], priority[0], cosine_wide, sine_wide, cotangent[0],
        query_weight, key_weight, value_weight, output_weight, wsend,
    )
    hidden, moe_input, table, gates, packed_sum, bound = front[:6]
    kept = front[6:20]
    (routed, grad_moe, grad_table, gu_back, grad_down, shared_gu, shared_dn) = expert_stage(
        moe_input, table, front[20], front[21], wdn
    )[:7]
    output_rows = (hidden + routed).astype(bf16)

    def joined(parts, at):
        return jnp.concatenate([parts[i][..., at : at + hidden_dev] for i in range(NZ)], axis=-1).astype(f32)

    shared_sum = lax.psum(shared_gu.astype(bf16), "ctx")
    shared_down_sum = lax.psum(shared_dn[:hidden_dev].astype(bf16), "ctx")
    grad_tokens, small, grad_wq, grad_wk, grad_wv, grad_wo = backward_stage(
        grad_moe, grad_table, cotangent[0], tokens[0], hidden, moe_input, gates, packed_sum, bound, cosine_wide,
        sine_wide, *kept
    )
    shared_back = lax.all_to_all(
        shared_sum.reshape(NZ, shard, 2 * WIDE), "fsdp", split_axis=0, concat_axis=0, tiled=True
    )
    mine = lax.dynamic_slice_in_dim(small, z * shard, shard, 1)
    return (
        output_rows[None],
        grad_tokens[None],
        mine[17],
        grad_wq,
        grad_wk,
        grad_wv,
        grad_wo,
        mine[16],
        mine[:16].T,
        joined(shared_back, 0),
        joined(shared_back, WIDE),
        shared_down_sum.astype(f32),
        joined(gu_back, 0),
        joined(gu_back, WIDE),
        grad_down[:, :hidden_dev],
    )


def per_device(
    tokens,
    documents,
    routes,
    priority,
    attention_gain,
    query_weight,
    key_weight,
    value_weight,
    output_weight,
    feedforward_gain,
    router_weight,
    shared_gate,
    shared_up,
    shared_down,
    expert_gate,
    expert_up,
    expert_down,
    cotangent,
):
    gathered = (
        lax.all_gather(attention_gain, "fsdp", axis=0, tiled=True),
        lax.all_gather(query_weight, "fsdp", axis=0, tiled=True),
        lax.all_gather(key_weight, "fsdp", axis=0, tiled=True),
        lax.all_gather(value_weight, "fsdp", axis=0, tiled=True),
        lax.all_gather(output_weight, "fsdp", axis=0, tiled=True),
        lax.all_gather(feedforward_gain, "fsdp", axis=0, tiled=True),
        lax.all_gather(router_weight, "fsdp", axis=0, tiled=True),
        lax.all_gather(shared_gate, "fsdp", axis=0, tiled=True),
        lax.all_gather(shared_up, "fsdp", axis=0, tiled=True),
        lax.all_gather(shared_down, "fsdp", axis=0, tiled=True),
        lax.all_gather(expert_gate, "fsdp", axis=1, tiled=True),
        lax.all_gather(expert_up, "fsdp", axis=1, tiled=True),
        lax.all_gather(expert_down, "fsdp", axis=1, tiled=True),
    )
    (
        gain_one,
        w_query,
        w_key,
        w_value,
        w_output,
        gain_two,
        w_router,
        w_shared_gate,
        w_shared_up,
        w_shared_down,
        w_expert_gate,
        w_expert_up,
        w_expert_down,
    ) = gathered
    groups = lax.axis_size("ctx")
    length = tokens.shape[1]
    row_length = length * groups
    experts = EXP_DEV * groups
    capacity = 9 * length * TOPK // (8 * experts)
    inner_width = HEADS * HEAD_DIM
    score_scale = HEAD_DIM ** (-0.5)
    spare_slot = experts * capacity
    first_here = lax.axis_index("ctx") * length
    positions = first_here + jnp.arange(length, dtype=jnp.int32)
    last_here = first_here + length - 1
    doc_here = documents[0].astype(jnp.float32)
    doc_wire = documents[0].astype(jnp.bfloat16)
    inputs = tokens[0].astype(jnp.float32)
    upstream_low = cotangent[0]
    upstream = upstream_low.astype(jnp.float32)
    factor_one = rms_factor(inputs)
    normed_one = inputs * factor_one
    gain_one_wide = gain_one.astype(jnp.float32)
    attn_input = (normed_one * gain_one_wide).astype(jnp.bfloat16)
    query_pre = jnp.dot(attn_input, w_query, preferred_element_type=jnp.float32).reshape(
        length, HEADS, HEAD_DIM
    )
    key_pre = jnp.dot(attn_input, w_key, preferred_element_type=jnp.float32).reshape(
        length, HEADS, HEAD_DIM
    )
    cosine, sine = rotary_tables(positions, HEAD_DIM // 2)
    queries = rotate(query_pre, cosine, sine).astype(jnp.bfloat16)
    key_rows = rotate(key_pre, cosine, sine).astype(jnp.bfloat16)
    value_rows = (
        jnp.dot(attn_input, w_value, preferred_element_type=jnp.float32)
        .astype(jnp.bfloat16)
        .reshape(length, HEADS, HEAD_DIM)
    )
    initial = (
        jnp.zeros((HEADS, length, HEAD_DIM), jnp.float32),
        jnp.full((HEADS, length), negative, jnp.float32),
        jnp.zeros((HEADS, length), jnp.float32),
    )
    key_all = lax.all_gather(key_rows, "ctx", axis=0, tiled=True)
    value_all = lax.all_gather(value_rows, "ctx", axis=0, tiled=True)
    docs_all = lax.all_gather(doc_wire, "ctx", axis=0, tiled=True)

    def visit(progress, within, rows_now):

        def compute(progress):
            accum, highest_seen, totals = progress
            key_block = lax.dynamic_slice_in_dim(key_all, within, rows_now, 0)
            value_block = lax.dynamic_slice_in_dim(value_all, within, rows_now, 0)
            docs_block = lax.dynamic_slice_in_dim(docs_all, within, rows_now, 0).astype(jnp.float32)
            key_pos = within + jnp.arange(rows_now, dtype=jnp.int32)
            allowed = allowed_mask(positions, doc_here, key_pos, docs_block)[None]
            scores = jnp.einsum(
                "qhd,khd->hqk", queries, key_block, preferred_element_type=jnp.float32
            )
            scores = jnp.where(allowed, scores * score_scale, negative)
            newest = jnp.maximum(highest_seen, jnp.max(scores, axis=-1))
            shrink = jnp.exp(highest_seen - newest)
            shares = jnp.exp(scores - newest[..., None]) * allowed
            totals = totals * shrink + jnp.sum(shares, axis=-1)
            accum = accum * shrink[..., None] + jnp.einsum(
                "hqk,khd->hqd",
                shares.astype(jnp.bfloat16),
                value_block,
                preferred_element_type=jnp.float32,
            )
            return (accum, newest, totals)

        return lax.cond(within > last_here, unchanged, compute, progress)

    accum, highest_seen, totals = blockwise(key_all.shape[0], visit, initial)
    attended = accum / totals[..., None]
    log_total = highest_seen + jnp.log(totals)
    mixed_rows = (
        jnp.transpose(attended, (1, 0, 2)).reshape(length, inner_width).astype(jnp.bfloat16)
    )
    hidden = inputs + jnp.dot(mixed_rows, w_output, preferred_element_type=jnp.float32)
    factor_two = rms_factor(hidden)
    normed_two = hidden * factor_two
    gain_two_wide = gain_two.astype(jnp.float32)
    moe_input = (normed_two * gain_two_wide).astype(jnp.bfloat16)
    moe_wide = moe_input.astype(jnp.float32)
    router_wide = w_router.astype(jnp.float32)
    gate_probs = jax.nn.softmax(jnp.dot(moe_wide, router_wide, precision=highest), axis=-1)
    route_now = routes[0]
    order_now = priority[0, 0]
    onehot = (route_now[:, :, None] == jnp.arange(experts, dtype=jnp.int32)).astype(jnp.float32)
    counts = jnp.sum(onehot, axis=1)
    earlier = (order_now[None, :] < order_now[:, None]).astype(jnp.bfloat16)
    before = jnp.dot(earlier, counts.astype(jnp.bfloat16), preferred_element_type=jnp.float32)
    ranking = jnp.sum(onehot * before[:, None, :], axis=-1).astype(jnp.int32)
    kept_mask = ranking < capacity
    slot_index = jnp.where(
        kept_mask,
        route_now % EXP_DEV * (groups * capacity) + route_now // EXP_DEV * capacity + ranking,
        spare_slot,
    )
    chosen = jnp.sum(onehot * gate_probs[:, None, :], axis=-1)
    weight = jnp.where(kept_mask, chosen, 0.0)
    flat_slots = slot_index.reshape(-1)
    copies = jnp.broadcast_to(moe_input[:, None, :], (length, TOPK, D)).reshape(length * TOPK, D)
    outgoing = jnp.zeros((spare_slot + 1, D), jnp.bfloat16).at[flat_slots].set(copies)[:spare_slot]
    arrived = lax.all_to_all(
        outgoing.reshape(EXP_DEV, groups, capacity, D),
        "ctx",
        split_axis=1,
        concat_axis=1,
        tiled=True,
    ).reshape(EXP_DEV, groups * capacity, D)
    gate_act = jnp.einsum(
        "erd,edf->erf", arrived, w_expert_gate, preferred_element_type=jnp.float32
    )
    up_act = jnp.einsum("erd,edf->erf", arrived, w_expert_up, preferred_element_type=jnp.float32)
    silu_gate, slope_gate = silu_parts(gate_act)
    expert_hidden = (silu_gate * up_act).astype(jnp.bfloat16)
    expert_out = jnp.einsum(
        "erf,efd->erd", expert_hidden, w_expert_down, preferred_element_type=jnp.float32
    ).astype(jnp.bfloat16)
    returned = lax.all_to_all(
        expert_out.reshape(EXP_DEV, groups, capacity, D),
        "ctx",
        split_axis=1,
        concat_axis=1,
        tiled=True,
    ).reshape(spare_slot, D)
    returned = jnp.concatenate([returned, jnp.zeros((1, D), jnp.bfloat16)], axis=0)
    picked = returned[slot_index]
    routed = jnp.sum(weight[..., None] * picked, axis=1)
    shared_gate_act = jnp.dot(moe_input, w_shared_gate, preferred_element_type=jnp.float32)
    shared_up_act = jnp.dot(moe_input, w_shared_up, preferred_element_type=jnp.float32)
    silu_shared, slope_shared = silu_parts(shared_gate_act)
    shared_hidden = (silu_shared * shared_up_act).astype(jnp.bfloat16)
    shared_out = jnp.dot(shared_hidden, w_shared_down, preferred_element_type=jnp.float32)
    output_rows = (hidden + shared_out + routed).astype(jnp.bfloat16)
    grad_shared_down = jnp.dot(shared_hidden.T, upstream_low, preferred_element_type=jnp.float32)
    grad_shared_hidden = jnp.dot(upstream_low, w_shared_down.T, preferred_element_type=jnp.float32)
    grad_shared_gate_act = (grad_shared_hidden * shared_up_act * slope_shared).astype(jnp.bfloat16)
    grad_shared_up_act = (grad_shared_hidden * silu_shared).astype(jnp.bfloat16)
    grad_shared_gate = jnp.dot(
        moe_input.T, grad_shared_gate_act, preferred_element_type=jnp.float32
    )
    grad_shared_up = jnp.dot(moe_input.T, grad_shared_up_act, preferred_element_type=jnp.float32)
    grad_moe = jnp.dot(
        grad_shared_gate_act, w_shared_gate.T, preferred_element_type=jnp.float32
    ) + jnp.dot(grad_shared_up_act, w_shared_up.T, preferred_element_type=jnp.float32)
    grad_copies = (
        (weight[..., None] * upstream[:, None, :]).astype(jnp.bfloat16).reshape(length * TOPK, D)
    )
    grad_weight = jnp.sum(picked.astype(jnp.float32) * upstream[:, None, :], axis=-1)
    grad_outgoing = (
        jnp.zeros((spare_slot + 1, D), jnp.bfloat16).at[flat_slots].set(grad_copies)[:spare_slot]
    )
    grad_arrived = lax.all_to_all(
        grad_outgoing.reshape(EXP_DEV, groups, capacity, D),
        "ctx",
        split_axis=1,
        concat_axis=1,
        tiled=True,
    ).reshape(EXP_DEV, groups * capacity, D)
    grad_expert_hidden = jnp.einsum(
        "erd,efd->erf", grad_arrived, w_expert_down, preferred_element_type=jnp.float32
    )
    grad_expert_down = jnp.einsum(
        "erf,erd->efd", expert_hidden, grad_arrived, preferred_element_type=jnp.float32
    )
    grad_gate_act = (grad_expert_hidden * up_act * slope_gate).astype(jnp.bfloat16)
    grad_up_act = (grad_expert_hidden * silu_gate).astype(jnp.bfloat16)
    grad_expert_gate = jnp.einsum(
        "erd,erf->edf", arrived, grad_gate_act, preferred_element_type=jnp.float32
    )
    grad_expert_up = jnp.einsum(
        "erd,erf->edf", arrived, grad_up_act, preferred_element_type=jnp.float32
    )
    grad_arrived_in = (
        jnp.einsum("erf,edf->erd", grad_gate_act, w_expert_gate, preferred_element_type=jnp.float32)
        + jnp.einsum("erf,edf->erd", grad_up_act, w_expert_up, preferred_element_type=jnp.float32)
    ).astype(jnp.bfloat16)
    sent_back = lax.all_to_all(
        grad_arrived_in.reshape(EXP_DEV, groups, capacity, D),
        "ctx",
        split_axis=1,
        concat_axis=1,
        tiled=True,
    ).reshape(spare_slot, D)
    sent_back = jnp.concatenate([sent_back, jnp.zeros((1, D), jnp.bfloat16)], axis=0)
    grad_moe = grad_moe + jnp.sum(sent_back[slot_index].astype(jnp.float32), axis=1)
    grad_chosen = jnp.where(kept_mask, grad_weight, 0.0)
    grad_probs = jnp.sum(onehot * grad_chosen[..., None], axis=1)
    grad_logits = gate_probs * (
        grad_probs - jnp.sum(gate_probs * grad_probs, axis=-1, keepdims=True)
    )
    grad_router = jnp.dot(moe_wide.T, grad_logits, precision=highest)
    grad_moe = grad_moe + jnp.dot(grad_logits, router_wide.T, precision=highest)
    grad_gain_two = jnp.sum(grad_moe * normed_two, axis=0)
    scaled_two = grad_moe * gain_two_wide
    grad_hidden = upstream + factor_two * (
        scaled_two - normed_two * jnp.mean(scaled_two * normed_two, axis=-1, keepdims=True)
    )
    grad_hidden_low = grad_hidden.astype(jnp.bfloat16)
    grad_output = jnp.dot(mixed_rows.T, grad_hidden_low, preferred_element_type=jnp.float32)
    grad_mixed = (
        jnp.dot(grad_hidden_low, w_output.T, preferred_element_type=jnp.float32)
        .astype(jnp.bfloat16)
        .reshape(length, HEADS, HEAD_DIM)
    )
    delta = jnp.einsum("qhd,hqd->hq", grad_mixed.astype(jnp.float32), attended)
    start_state = (
        jnp.zeros((length, HEADS, HEAD_DIM), jnp.float32),
        jnp.zeros((row_length, 2 * inner_width), jnp.float32),
    )
    back_key_all = lax.all_gather(key_rows, "ctx", axis=0, tiled=True)
    back_value_all = lax.all_gather(value_rows, "ctx", axis=0, tiled=True)
    back_docs_all = lax.all_gather(doc_wire, "ctx", axis=0, tiled=True)

    def visit(progress, within, rows_now):
        first_row = within

        def compute(progress):
            grad_query_acc, grad_kv_all = progress
            key_block = lax.dynamic_slice_in_dim(back_key_all, within, rows_now, 0)
            value_block = lax.dynamic_slice_in_dim(back_value_all, within, rows_now, 0)
            docs_block = lax.dynamic_slice_in_dim(back_docs_all, within, rows_now, 0).astype(
                jnp.float32
            )
            key_pos = first_row + jnp.arange(rows_now, dtype=jnp.int32)
            allowed = allowed_mask(positions, doc_here, key_pos, docs_block)[None]
            scores = jnp.einsum(
                "qhd,khd->hqk", queries, key_block, preferred_element_type=jnp.float32
            )
            scores = jnp.where(allowed, scores * score_scale, negative)
            shares = jnp.exp(scores - log_total[..., None]) * allowed
            grad_shares = jnp.einsum(
                "qhd,khd->hqk", grad_mixed, value_block, preferred_element_type=jnp.float32
            )
            grad_scores = (shares * (grad_shares - delta[..., None]) * score_scale).astype(
                jnp.bfloat16
            )
            grad_query_acc = grad_query_acc + jnp.einsum(
                "hqk,khd->qhd", grad_scores, key_block, preferred_element_type=jnp.float32
            )
            grad_key_rows = jnp.einsum(
                "hqk,qhd->khd", grad_scores, queries, preferred_element_type=jnp.float32
            ).reshape(rows_now, inner_width)
            grad_value_rows = jnp.einsum(
                "hqk,qhd->khd",
                shares.astype(jnp.bfloat16),
                grad_mixed,
                preferred_element_type=jnp.float32,
            ).reshape(rows_now, inner_width)
            current = lax.dynamic_slice_in_dim(grad_kv_all, first_row, rows_now, 0)
            grad_kv_all = lax.dynamic_update_slice_in_dim(
                grad_kv_all,
                current + jnp.concatenate([grad_key_rows, grad_value_rows], axis=1),
                first_row,
                0,
            )
            return (grad_query_acc, grad_kv_all)

        return lax.cond(first_row > last_here, unchanged, compute, progress)

    grad_query, grad_kv_all = blockwise(back_key_all.shape[0], visit, start_state)
    grad_kv = lax.psum_scatter(
        grad_kv_all.astype(jnp.bfloat16), "ctx", scatter_dimension=0, tiled=True
    ).astype(jnp.float32)
    grad_query_low = (
        unrotate(grad_query.astype(jnp.bfloat16).astype(jnp.float32), cosine, sine)
        .astype(jnp.bfloat16)
        .reshape(length, inner_width)
    )
    grad_key_turned = (
        grad_kv[:, :inner_width]
        .reshape(length, HEADS, HEAD_DIM)
        .astype(jnp.bfloat16)
        .astype(jnp.float32)
    )
    grad_key_low = (
        unrotate(grad_key_turned, cosine, sine).astype(jnp.bfloat16).reshape(length, inner_width)
    )
    grad_value_low = grad_kv[:, inner_width:].astype(jnp.bfloat16)
    grad_wquery = jnp.dot(attn_input.T, grad_query_low, preferred_element_type=jnp.float32)
    grad_wkey = jnp.dot(attn_input.T, grad_key_low, preferred_element_type=jnp.float32)
    grad_wvalue = jnp.dot(attn_input.T, grad_value_low, preferred_element_type=jnp.float32)
    grad_attn = (
        jnp.dot(grad_query_low, w_query.T, preferred_element_type=jnp.float32)
        + jnp.dot(grad_key_low, w_key.T, preferred_element_type=jnp.float32)
        + jnp.dot(grad_value_low, w_value.T, preferred_element_type=jnp.float32)
    )
    grad_gain_one = jnp.sum(grad_attn * normed_one, axis=0)
    scaled_one = grad_attn * gain_one_wide
    grad_inputs = grad_hidden + factor_one * (
        scaled_one - normed_one * jnp.mean(scaled_one * normed_one, axis=-1, keepdims=True)
    )
    owned = (
        lax.psum_scatter(
            grad_gain_one.astype(jnp.bfloat16), "fsdp", scatter_dimension=0, tiled=True
        ).astype(jnp.float32),
        lax.psum_scatter(
            grad_wquery.astype(jnp.bfloat16), "fsdp", scatter_dimension=0, tiled=True
        ).astype(jnp.float32),
        lax.psum_scatter(
            grad_wkey.astype(jnp.bfloat16), "fsdp", scatter_dimension=0, tiled=True
        ).astype(jnp.float32),
        lax.psum_scatter(
            grad_wvalue.astype(jnp.bfloat16), "fsdp", scatter_dimension=0, tiled=True
        ).astype(jnp.float32),
        lax.psum_scatter(
            grad_output.astype(jnp.bfloat16), "fsdp", scatter_dimension=0, tiled=True
        ).astype(jnp.float32),
        lax.psum_scatter(
            grad_gain_two.astype(jnp.bfloat16), "fsdp", scatter_dimension=0, tiled=True
        ).astype(jnp.float32),
        lax.psum_scatter(
            grad_router.astype(jnp.bfloat16), "fsdp", scatter_dimension=0, tiled=True
        ).astype(jnp.float32),
        lax.psum_scatter(
            grad_shared_gate.astype(jnp.bfloat16), "fsdp", scatter_dimension=0, tiled=True
        ).astype(jnp.float32),
        lax.psum_scatter(
            grad_shared_up.astype(jnp.bfloat16), "fsdp", scatter_dimension=0, tiled=True
        ).astype(jnp.float32),
        lax.psum_scatter(
            grad_shared_down.astype(jnp.bfloat16), "fsdp", scatter_dimension=0, tiled=True
        ).astype(jnp.float32),
        lax.psum_scatter(
            grad_expert_gate.astype(jnp.bfloat16), "fsdp", scatter_dimension=1, tiled=True
        ).astype(jnp.float32),
        lax.psum_scatter(
            grad_expert_up.astype(jnp.bfloat16), "fsdp", scatter_dimension=1, tiled=True
        ).astype(jnp.float32),
        lax.psum_scatter(
            grad_expert_down.astype(jnp.bfloat16), "fsdp", scatter_dimension=1, tiled=True
        ).astype(jnp.float32),
    )
    (
        own_gain_one,
        own_wquery,
        own_wkey,
        own_wvalue,
        own_output,
        own_gain_two,
        own_router,
        own_shared_gate,
        own_shared_up,
        own_shared_down,
        own_expert_gate,
        own_expert_up,
        own_expert_down,
    ) = owned
    dense = (
        lax.psum(own_gain_one.astype(jnp.bfloat16), "ctx").astype(jnp.float32),
        lax.psum(own_wquery.astype(jnp.bfloat16), "ctx").astype(jnp.float32),
        lax.psum(own_wkey.astype(jnp.bfloat16), "ctx").astype(jnp.float32),
        lax.psum(own_wvalue.astype(jnp.bfloat16), "ctx").astype(jnp.float32),
        lax.psum(own_output.astype(jnp.bfloat16), "ctx").astype(jnp.float32),
        lax.psum(own_gain_two.astype(jnp.bfloat16), "ctx").astype(jnp.float32),
        lax.psum(own_router.astype(jnp.bfloat16), "ctx").astype(jnp.float32),
        lax.psum(own_shared_gate.astype(jnp.bfloat16), "ctx").astype(jnp.float32),
        lax.psum(own_shared_up.astype(jnp.bfloat16), "ctx").astype(jnp.float32),
        lax.psum(own_shared_down.astype(jnp.bfloat16), "ctx").astype(jnp.float32),
    )
    return (
        output_rows[None],
        grad_inputs.astype(jnp.bfloat16)[None],
        dense[0],
        dense[1],
        dense[2],
        dense[3],
        dense[4],
        dense[5],
        dense[6],
        dense[7],
        dense[8],
        dense[9],
        own_expert_gate,
        own_expert_up,
        own_expert_down,
    )


def solution(mesh):
    fast = mesh.shape['ctx'] == 8 and mesh.shape['fsdp'] == NZ
    body = per_device_fast if fast else per_device
    return jax.shard_map(
        body,
        mesh=mesh,
        in_specs=(
            P("fsdp", "ctx", None),
            P("fsdp", "ctx"),
            P("fsdp", "ctx", None),
            P("fsdp", "ctx", None),
            P("fsdp"),
            P("fsdp", None),
            P("fsdp", None),
            P("fsdp", None),
            P("fsdp", None),
            P("fsdp"),
            P("fsdp", None),
            P("fsdp", None),
            P("fsdp", None),
            P("fsdp", None),
            P("ctx", "fsdp", None),
            P("ctx", "fsdp", None),
            P("ctx", "fsdp", None),
            P("fsdp", "ctx", None),
        ),
        out_specs=(
            P("fsdp", "ctx", None),
            P("fsdp", "ctx", None),
            P("fsdp"),
            P("fsdp", None),
            P("fsdp", None),
            P("fsdp", None),
            P("fsdp", None),
            P("fsdp"),
            P("fsdp", None),
            P("fsdp", None),
            P("fsdp", None),
            P("fsdp", None),
            P("ctx", "fsdp", None),
            P("ctx", "fsdp", None),
            P("ctx", "fsdp", None),
        ),
        check_vma=False,
    )
```

```python
import functools
import math
import types

import jax
import jax.numpy as jnp
import numpy as np
from jax import lax
from jax.experimental import pallas as pl
from jax.experimental.pallas import tpu as pltpu
from jax.sharding import PartitionSpec as P

D = 1280
HEADS = 10
HEAD_DIM = 128
TOPK = 7
EXP_DEV = 2


epsilon = 1e-06
theta_base = 10000.0
negative = -1e30
highest = lax.Precision.HIGHEST


def rotary_tables(positions, half_dim):
    frequency = theta_base ** (-jnp.arange(half_dim, dtype=jnp.float32) / half_dim)
    angles = positions.astype(jnp.float32)[:, None] * frequency[None, :]
    return (jnp.cos(angles)[:, None, :], jnp.sin(angles)[:, None, :])


def rotate(values, cosine, sine):
    half_dim = values.shape[-1] // 2
    leading = values[..., :half_dim]
    trailing = values[..., half_dim:]
    return jnp.concatenate(
        [leading * cosine - trailing * sine, trailing * cosine + leading * sine], axis=-1
    )


def unrotate(values, cosine, sine):
    half_dim = values.shape[-1] // 2
    leading = values[..., :half_dim]
    trailing = values[..., half_dim:]
    return jnp.concatenate(
        [leading * cosine + trailing * sine, trailing * cosine - leading * sine], axis=-1
    )


def blockwise(count, visit, initial):
    rows_each = math.gcd(count, 512)

    def advance(progress, number):
        return (visit(progress, number * rows_each, rows_each), None)

    final, ignored = lax.scan(advance, initial, jnp.arange(count // rows_each, dtype=jnp.int32))
    return final


def allowed_mask(query_pos, query_docs, key_pos, key_docs):
    return (key_pos[None, :] <= query_pos[:, None]) & (key_docs[None, :] == query_docs[:, None])


def rms_factor(values):
    return lax.rsqrt(jnp.mean(values * values, axis=-1, keepdims=True) + epsilon)


def silu_parts(values):
    sigma = jax.nn.sigmoid(values)
    return (values * sigma, sigma * (1.0 + values * (1.0 - sigma)))


def unchanged(progress):
    return progress


NZ = 4
SLOTS = 64
WIDE = 256
MESH = pl.DeviceIdType.MESH
PEERS = ((0, 1), (1, 0), (1, 1))
NN = (((1,), (0,)), ((), ()))
NT = (((1,), (1,)), ((), ()))
TN = (((0,), (0,)), ((), ()))
MIB = 1024 * 1024


def dot(left, right, dims=NN):
    return lax.dot_general(left, right, dims, preferred_element_type=jnp.float32)


def split_dot(left, right, dims=NN):
    high = left.astype(jnp.bfloat16)
    low = (left - high.astype(jnp.float32)).astype(jnp.bfloat16)
    return dot(high, right, dims) + dot(low, right, dims)


def flip(c, fy, fx, fk):
    return 4 * ((c // 4 + fy) % 2) + 2 * (((c // 2) % 2 + fx) % 2) + (c % 2 + fk) % 2


def rows_at(start, count):
    return pl.ds(pl.multiple_of(start, 16), count)


def lanes_at(start, count):
    return pl.ds(pl.multiple_of(start, 128), count)


def remote(src, dst, send, recv, c, z):
    return pltpu.make_async_remote_copy(
        src_ref=src, dst_ref=dst, send_sem=send, recv_sem=recv, device_id=(c, z), device_id_type=MESH
    )


def greet(c, z):
    barrier = pltpu.get_barrier_semaphore()
    peers = [(c, (z + d) % NZ) for d in range(1, NZ)]
    peers += [(flip(c, fy, fx, 0), z) for fy, fx in PEERS] + [(flip(c, 0, 0, 1), z)]
    for peer in peers:
        pl.semaphore_signal(barrier, inc=1, device_id=peer, device_id_type=MESH)
    pl.semaphore_wait(barrier, len(peers))


class Spread:
    def __init__(self, src, block, sems, c, z, hops=NZ, peers=PEERS, copy_own=True):
        self.src, self.block, self.c, self.z = src, block, c, z
        self.hops, self.peers, self.all = hops, peers, ((0, 0),) + peers
        self.local, self.zs, self.zr, self.xs, self.xr, self.ms, self.mr = sems
        self.forwards = hops == NZ and len(peers) == 3
        self.direct = 2 if self.forwards else len(peers)
        self.own = pltpu.make_async_copy(src(z), block(c, z), self.local) if copy_own else None

    def at(self, c, d):
        return self.block(c, (self.z + NZ - d) % NZ)

    def mine(self, c, d):
        return self.src(self.z) if d == 0 else self.at(c, d)

    def zcopy(self, d):
        there = (self.z + d) % NZ
        return remote(
            self.src(there), self.block(self.c, self.z), self.zs.at[d - 1], self.zr.at[d - 1], self.c, there
        )

    def zwait(self, d):
        block = self.at(self.c, d)
        remote(block, block, self.zs.at[d - 1], self.zr.at[d - 1], self.c, self.z).wait_recv()

    def xcopy(self, i, d):
        there = flip(self.c, self.peers[i][0], self.peers[i][1], 0)
        return remote(self.mine(self.c, d), self.at(self.c, d), self.xs.at[i, d], self.xr.at[i, d], there, self.z)

    def fcopy(self, i, d):
        origin = flip(self.c, self.peers[i][0], self.peers[i][1], 0)
        there = flip(self.c, self.peers[1 - i][0], self.peers[1 - i][1], 0)
        block = self.at(origin, d)
        return remote(block, block, self.xs.at[2, d], self.xr.at[2, d], there, self.z)

    def xwait(self, i, d):
        block = self.at(flip(self.c, self.peers[i][0], self.peers[i][1], 0), d)
        remote(block, block, self.xs.at[i, d], self.xr.at[i, d], self.c, self.z).wait_recv()

    def mcopy(self, i, d):
        origin = flip(self.c, self.all[i][0], self.all[i][1], 0)
        src = self.mine(origin, d) if i == 0 else self.at(origin, d)
        return remote(src, self.at(origin, d), self.ms.at[i, d], self.mr.at[i, d], flip(self.c, 0, 0, 1), self.z)

    def mwait(self, i, d):
        block = self.at(flip(self.c, self.all[i][0], self.all[i][1], 1), d)
        remote(block, block, self.ms.at[i, d], self.mr.at[i, d], self.c, self.z).wait_recv()

    def start_z(self):
        if self.own is not None:
            self.own.start()
        for d in range(1, self.hops):
            self.zcopy(d).start()

    def start_x(self):
        for i in range(self.direct):
            self.xcopy(i, 0).start()
        self.mcopy(0, 0).start()

    def relay_z(self):
        for d in range(1, self.hops):
            self.zwait(d)
            for i in range(self.direct):
                self.xcopy(i, d).start()
            self.mcopy(0, d).start()

    def relay_x(self):
        for d in range(self.hops):
            self.relay_near(d)
        self.relay_far()

    def relay_near(self, d):
        for i in range(min(2, len(self.peers))):
            self.xwait(i, d)
            self.mcopy(i + 1, d).start()
            if self.forwards and i == (d >= 2):
                self.fcopy(i, d).start()

    def relay_far(self):
        for d in range(self.hops if len(self.peers) > 2 else 0):
            self.xwait(2, d)
            self.mcopy(3, d).start()

    def arrive_from(self, i):
        for d in range(self.hops):
            self.mwait(i, d)

    def arrive(self):
        if self.own is not None:
            self.own.wait()
        for d in range(self.hops):
            for i in range(len(self.all)):
                self.mwait(i, d)

    def drain(self):
        for d in range(1, self.hops):
            self.zcopy(d).wait_send()
        for d in range(self.hops):
            for i in range(self.direct):
                self.xcopy(i, d).wait_send()
            if self.forwards:
                self.fcopy(int(d >= 2), d).wait_send()
            for i in range(len(self.all)):
                self.mcopy(i, d).wait_send()


def spread_sems(hops=NZ, peers=3):
    dma = pltpu.SemaphoreType.DMA
    return [
        dma, dma((3,)), dma((3,)), dma((peers, hops)), dma((peers, hops)), dma((peers + 1, hops)), dma((peers + 1, hops)),
    ]


def plane_reduce(part, c, z, refs):
    out4, in4, out3, in3, ms, mr, xs, xr = refs
    mate = flip(c, 0, 0, 1)
    order = PEERS + ((0, 0),)

    def to_mate(i):
        return remote(out4.at[i], in4.at[i], ms.at[i], mr.at[i], mate, z)

    def to_chip(i):
        return remote(out3.at[i], in3.at[i], xs.at[i], xr.at[i], flip(c, PEERS[i][0], PEERS[i][1], 0), z)

    for i, (fy, fx) in enumerate(order):
        out4[i] = part(flip(c, fy, fx, 1)).astype(jnp.bfloat16)
        to_mate(i).start()
    for i, (fy, fx) in enumerate(order):
        value = part(flip(c, fy, fx, 0))
        to_mate(i).wait_recv()
        value = value + in4[i].astype(jnp.float32)
        if i < 3:
            out3[i] = value.astype(jnp.bfloat16)
            to_chip(i).start()
    for i in range(3):
        to_chip(i).wait_recv()
        value = value + in3[i].astype(jnp.float32)
    for i in range(4):
        to_mate(i).wait_send()
    for i in range(3):
        to_chip(i).wait_send()
    return value


def plane_scratch(length, width):
    dma = pltpu.SemaphoreType.DMA
    block = lambda n: pltpu.VMEM((n, length, width), jnp.bfloat16)
    return [block(4), block(4), block(3), block(3), dma((4,)), dma((4,)), dma((3,)), dma((3,))]


def swish(values):
    sigma = 1.0 / (1.0 + jnp.exp(-values))
    return values * sigma, sigma * (1.0 + values * (1.0 - sigma))


def norm_factor(values):
    return lax.rsqrt(jnp.mean(values * values, axis=1, keepdims=True) + epsilon)


def turned(values, cosine, sine):
    return values * cosine + pltpu.roll(values, 64, 1) * sine


def take(refs, count):
    taken = refs[:count]
    del refs[:count]
    return taken


def head_rows(c):
    blocks = [2 * c, 2 * c + 1, 16 + 2 * (c // 4), 17 + 2 * (c // 4)]
    return [(b, b // 5) for b in blocks]


def visible(first, count, keys, boundary):
    query = (lax.broadcasted_iota(jnp.int32, (count, 1), 0) + first).astype(jnp.float32)
    key = lax.broadcasted_iota(jnp.int32, (1, keys), 1).astype(jnp.float32)
    query_doc = jnp.where(query >= boundary, 1.0, 0.0)
    key_doc = jnp.where(key >= boundary, 1.0, 0.0)
    return (key <= query) & (key_doc == query_doc)


FRONT_IN = (
    "x", "router", "gains", "doc", "routes", "prio", "cos", "sin", "g", "wq", "wk", "wv", "wo", "eg", "eu", "sg", "su",
    "ed", "sd",
)
FRONT_OUT = (
    "hidden", "tokens", "gates", "psum", "bound", "aall", "wall", "woall", "q1", "k1", "v1", "q2", "k2", "v2",
    "att1", "lse1", "att2", "lse2", "mixed", "db", "dg", "ddn", "dsgu", "dsdn",
    "gall", "wsend", "ball", "tall", "ypart", "accout",
)
FRONT_TMP = (
    "pool", "docs", "pown", "pall", "cut", "wgu", "wdn", "table", "acc", "bg", "gg", "tg", "oh", "ys", "ds",
    "st", "stc", "sty", "ld", "xrecv", "zbuf", "zrecv",
)


def front_kernel(capacity, *refs):
    f32, bf16 = jnp.float32, jnp.bfloat16
    names = FRONT_IN + FRONT_OUT + FRONT_TMP
    r = types.SimpleNamespace(**dict(zip(names, refs)))
    sems = list(refs[len(names) :])
    c = lax.axis_index("ctx")
    z = lax.axis_index("fsdp")
    length, width = r.x.shape
    count = r.cos.shape[0]
    shard = width // NZ
    sub = shard // 4
    quarter = c % 4
    mate = flip(c, 0, 0, 1)
    step = 2 * length
    group = NZ * length
    final = group + 16
    hidden_dev = r.ed.shape[1]

    spread_x = Spread(
        lambda _: r.x, lambda o, _: r.pool.at[rows_at(o * length, length)], take(sems, 7), c, z, 1
    )
    spread_docs = Spread(lambda _: r.docs.at[8], lambda o, _: r.docs.at[o], take(sems, 7), c, z, 1)
    second = lambda o, s: r.wall.at[rows_at(s * shard + (o % 4) * sub, sub), 384:768]
    spread_h2 = Spread(lambda _: second(c, z), second, take(sems, 7), c, z, NZ, ((0, 1),), False)
    spread_g = Spread(lambda _: r.g, lambda o, s: r.gall.at[o, rows_at(s * length, length)], take(sems, 7), c, z)
    shared_in = lambda s: r.wsend.at[s, 2, rows_at((c // 2) * sub, sub), lanes_at(c % 2 * WIDE, WIDE)]
    shared_to = lambda o, s: r.wgu.at[2, rows_at(s * shard + (o // 2) * sub, sub), lanes_at(o % 2 * WIDE, WIDE)]
    spread_s = Spread(shared_in, shared_to, take(sems, 7), c, z)
    spread_b = Spread(lambda _: r.tokens, lambda o, s: r.ball.at[o, rows_at(s * length, length)], take(sems, 7), c, z)
    spread_t = Spread(lambda _: r.table, lambda o, s: r.tall.at[o, s], take(sems, 7), c, z)
    ps, pr, wl, w1s, w1r, wol, wos, wor, wgl, wgs, wgr, rawsem, cutsem, dnsem, acsem = take(sems, 15)
    lsem, ms, mr, xs_s, xs_r, zs, zr, ysem, accsem = take(sems, 9)
    reduce_refs = [r.ys, r.ds, r.zbuf.at[0:3, 0:length]] + take(sems, 5)

    greet(c, z)
    own_rows = rows_at(z * shard, shard)
    sub_rows = rows_at(z * shard + quarter * sub, sub)
    copies = []
    for i, ref in enumerate((r.wq, r.wk, r.wv)):
        copies.append(
            pltpu.make_async_copy(
                ref.at[:, lanes_at(c * 128, 128)], r.wall.at[own_rows, i * 128 : (i + 1) * 128], wl.at[i]
            )
        )
        copies.append(
            pltpu.make_async_copy(
                ref.at[rows_at(quarter * sub, sub), lanes_at((8 + c // 4) * 128, 128)],
                r.wall.at[sub_rows, 384 + i * 128 : 512 + i * 128],
                wl.at[3 + i],
            )
        )
    for copy in copies:
        copy.start()
    spread_x.start_z()
    spread_x.start_x()
    down = [pltpu.make_async_copy(r.ed.at[e], r.wdn.at[e, 0:hidden_dev], dnsem.at[e]) for e in range(2)]
    down.append(pltpu.make_async_copy(r.sd, r.wdn.at[2, 0:hidden_dev], dnsem.at[2]))
    for copy in down:
        copy.start()
    raws = ((r.eg.at[0], r.eu.at[0]), (r.eg.at[1], r.eu.at[1]), (r.sg, r.su))

    units = r.eg.shape[2]
    raw = lambda h: r.gg.at[h * shard : (h + 1) * shard, 0:units]

    def load_raw(e):
        return [pltpu.make_async_copy(raws[e][h], raw(h), rawsem.at[h]) for h in range(2)]

    def store_cut(e):
        return pltpu.make_async_copy(r.cut, r.wsend.at[:, e], cutsem)

    for copy in load_raw(0):
        copy.start()
    row = lax.broadcasted_iota(jnp.int32, (shard, width), 0)
    lane = lax.broadcasted_iota(jnp.int32, (shard, width), 1)
    place = jnp.where(lane == row + z * shard, 1.0, 0.0).astype(bf16)
    r.pown[0:16] = dot(r.router[...], place, TN).astype(bf16)
    r.pown[16:32] = dot(r.gains[...], place).astype(bf16)

    def pcopy(d):
        return remote(r.pown, r.pall.at[d - 1], ps.at[d - 1], pr.at[d - 1], c, (z + d) % NZ)

    for d in range(1, NZ):
        pcopy(d).start()
    spread_g.start_z()
    for copy in copies:
        copy.wait()

    def h1copy(d):
        return remote(
            r.wall.at[own_rows, 0:384], r.wall.at[own_rows, 0:384], w1s.at[d - 1], w1r.at[d - 1], c, (z + d) % NZ
        )

    def h1wait(d):
        here = r.wall.at[rows_at((z + NZ - d) % NZ * shard, shard), 0:384]
        remote(here, here, w1s.at[d - 1], w1r.at[d - 1], c, z).wait_recv()

    spread_h2.start_z()
    for d in range(1, NZ):
        h1copy(d).start()
    spread_h2.start_x()
    def wo_local(j, b):
        return pltpu.make_async_copy(
            r.wo.at[rows_at(b % 5 * 64, 64)], r.woall.at[64 * j : 64 * j + 64], wol.at[j]
        )

    def wo_hop(j, up, b, owner):
        src = r.wo.at[rows_at(b % 5 * 64, 64)] if owner else r.woall.at[64 * j : 64 * j + 64]
        there = z + 1 if up else z - 1
        return remote(src, r.woall.at[64 * j : 64 * j + 64], wos.at[j, int(up)], wor.at[j], c, there)

    def wo_each(visit):
        for j, (b, owner) in enumerate(head_rows(c)):
            visit(j, b, owner)

    def wo_start(j, b, owner):
        @pl.when(owner == z)
        def _():
            wo_local(j, b).start()

        @pl.when((owner == z) & (z < NZ - 1))
        def _():
            wo_hop(j, True, b, True).start()

        @pl.when((owner == z) & (z > 0))
        def _():
            wo_hop(j, False, b, True).start()

    def wo_relay(j, b, owner):
        @pl.when(owner != z)
        def _():
            wo_hop(j, True, b, False).wait_recv()

        @pl.when((owner < z) & (z < NZ - 1))
        def _():
            wo_hop(j, True, b, False).start()

        @pl.when((owner > z) & (z > 0))
        def _():
            wo_hop(j, False, b, False).start()

        @pl.when(owner == z)
        def _():
            wo_local(j, b).wait()

    def wo_drain(j, b, owner):
        @pl.when((owner <= z) & (z < NZ - 1))
        def _():
            wo_hop(j, True, b, False).wait_send()

        @pl.when((owner >= z) & (z > 0))
        def _():
            wo_hop(j, False, b, False).wait_send()

    wo_each(wo_start)
    r.docs[8] = jnp.concatenate([r.doc[...].astype(f32), jnp.ones((7, length), f32)], axis=0)
    spread_docs.start_z()
    spread_docs.start_x()
    spread_x.relay_x()
    spread_docs.relay_x()
    spread_g.start_x()

    for e in range(3):
        for copy in load_raw(e):
            copy.wait()
        if e > 0:
            store_cut(e - 1).wait()
        unit = lax.broadcasted_iota(jnp.int32, (units, WIDE), 0)
        slot = lax.broadcasted_iota(jnp.int32, (units, WIDE), 1)
        for q in range(NZ):
            pick = jnp.where((unit == slot + q * hidden_dev) & (slot < hidden_dev), 1.0, 0.0).astype(bf16)
            for h in range(2):
                r.cut[q, :, h * WIDE : (h + 1) * WIDE] = dot(raw(h)[...], pick).astype(bf16)
        store_cut(e).start()
        if e < 2:
            for copy in load_raw(e + 1):
                copy.start()
    spread_g.relay_z()
    packed = r.pown[...].astype(f32)
    for d in range(1, NZ):
        pcopy(d).wait_recv()
        packed = packed + r.pall[d - 1].astype(f32)
    r.psum[...] = packed
    gain_one = packed[17:18]
    gain_two = packed[16:17]
    spread_x.arrive()

    def make_a(i, carry):
        values = r.pool[rows_at(i * length, length)].astype(f32)
        r.bg[rows_at(i * length, length)] = (values * norm_factor(values) * gain_one).astype(bf16)
        return carry

    lax.fori_loop(0, 8, make_a, 0)
    for d in range(2):
        spread_g.relay_near(d)
    spread_h2.relay_z()
    spread_h2.relay_x()
    spread_h2.arrive()
    for d in range(1, NZ):
        h1wait(d)
    wo_each(wo_relay)

    def wgcopy(e, d):
        there = (z + d) % NZ
        return remote(
            r.wsend.at[there, e], r.wgu.at[e, own_rows, :], wgs.at[e, d - 1], wgr.at[e, d - 1], c, there
        )

    def wgwait(e, d):
        here = r.wgu.at[e, rows_at((z + NZ - d) % NZ * shard, shard), :]
        remote(here, here, wgs.at[e, d - 1], wgr.at[e, d - 1], c, z).wait_recv()

    wgown = pltpu.make_async_copy(r.wsend.at[z, 0:2], r.wgu.at[0:2, own_rows, :], wgl)
    store_cut(2).wait()
    spread_s.start_z()
    spread_s.start_x()
    wgown.start()
    for d in range(1, NZ):
        wgcopy(0, d).start()
    for i in range(count // step):
        part = slice(i * step, (i + 1) * step)
        values = dot(r.bg[part], r.wall[...])
        cosine, sine = r.cos[part], r.sin[part]
        r.q1[part] = turned(values[:, 0:128], cosine, sine).astype(bf16)
        r.k1[part] = turned(values[:, 128:256], cosine, sine).astype(bf16)
        r.v1[part] = values[:, 256:384].astype(bf16)
        r.q2[part] = turned(values[:, 384:512], cosine, sine).astype(bf16)
        r.k2[part] = turned(values[:, 512:640], cosine, sine).astype(bf16)
        r.v2[part] = values[:, 640:768].astype(bf16)
    for d in range(2, NZ):
        spread_g.relay_near(d)
    acopy = pltpu.make_async_copy(r.bg, r.aall, acsem)
    acopy.start()
    spread_docs.arrive()
    flags = jnp.where(r.docs[0:8] == 0.0, 1.0, 0.0)
    boundary = jnp.sum(jnp.sum(flags, axis=0), axis=(0, 1), keepdims=True)
    r.bound[...] = jnp.broadcast_to(boundary, r.bound.shape)

    def attend(queries, first, keys, values, n):
        scores = dot(queries, keys[0:n], NT) * (HEAD_DIM**-0.5)
        scores = jnp.where(visible(first, step, n, boundary), scores, negative)
        top = jnp.max(scores, axis=1, keepdims=True)
        shares = jnp.exp(scores - top)
        total = jnp.sum(shares, axis=1, keepdims=True)
        probs = (shares * (1.0 / total)).astype(bf16)
        return dot(probs, values[0:n]), jnp.broadcast_to(top + jnp.log(total), (step, 128))

    r.mixed[...] = jnp.zeros_like(r.mixed)
    for i in range(count // step):
        part = slice(i * step, (i + 1) * step)
        out, lse = attend(r.q1[part], i * step, r.k1, r.v1, (i + 1) * step)
        r.att1[part] = out
        r.lse1[part] = lse
        r.mixed[part, 0:128] = out.astype(bf16)
        if i == 1:
            spread_g.relay_far()
    mine = rows_at(quarter * step, step)
    out, lse = attend(r.q2[mine], quarter * step, r.k2, r.v2, count)
    r.att2[...] = out
    r.lse2[...] = lse
    r.mixed[mine, 128:256] = out.astype(bf16)
    spread_s.relay_z()

    value = plane_reduce(
        lambda o: dot(r.mixed[rows_at(o * length, length)], r.woall[...]), c, z, reduce_refs
    )
    hidden = r.x[...].astype(f32) + value
    r.hidden[...] = hidden
    tokens = (hidden * norm_factor(hidden) * gain_two).astype(bf16)
    r.tokens[...] = tokens
    logits = dot(packed[0:16].astype(bf16), tokens, NT)
    shifted = jnp.exp(logits - jnp.max(logits, axis=0, keepdims=True))
    gates = shifted / jnp.sum(shifted, axis=0, keepdims=True)
    r.gates[...] = gates
    lane = lax.broadcasted_iota(jnp.int32, (length, 128), 1)
    named = jnp.zeros((length, 128), f32)
    for k in range(r.routes.shape[1]):
        named = named + jnp.where(lane == r.routes[:, k : k + 1], 1.0, 0.0)
    named = named.T[0:16]
    order = jnp.broadcast_to(r.prio[...].astype(f32), (length, length))
    earlier = jnp.where(order.T < order, 1.0, 0.0).astype(bf16)
    rank = dot(named.astype(bf16), earlier)
    kept = (named > 0.0) & (rank < float(capacity))
    r.table[:, 0:length] = jnp.where(kept, rank, -1.0)
    r.table[:, length : 2 * length] = jnp.where(kept, gates, 0.0)
    spread_b.start_z()
    spread_b.start_x()
    spread_t.start_z()
    spread_t.start_x()
    for d in range(1, NZ):
        wgcopy(1, d).start()
    r.acc[...] = jnp.zeros_like(r.acc)
    r.ddn[...] = jnp.zeros_like(r.ddn)
    r.st[group:final] = jnp.zeros((16, width), bf16)
    r.zbuf[...] = jnp.zeros_like(r.zbuf)
    for copy in down:
        copy.wait()
    r.wdn[:, hidden_dev:] = jnp.zeros((3, WIDE - hidden_dev, width), bf16)
    for d in range(NZ):
        spread_s.relay_near(d)
    spread_s.relay_far()
    spread_b.relay_z()
    spread_t.relay_z()
    for d in range(NZ):
        spread_b.relay_near(d)
        spread_t.relay_near(d)
    spread_b.relay_far()
    spread_t.relay_far()
    spread_s.arrive()
    spread_g.arrive()
    spread_b.arrive()
    spread_t.arrive()
    wgown.wait()
    for d in range(1, NZ):
        wgwait(0, d)
        wgwait(1, d)
    spread_x.drain()

    def target(g):
        left = 3 - g // 2
        return flip(c, left % 2, left // 2, 1 - g % 2)

    def loads(g):
        slot = g % 2
        there = target(g)
        return (
            pltpu.make_async_copy(r.ball.at[there], r.bg.at[rows_at(slot * group, group)], lsem.at[slot, 0]),
            pltpu.make_async_copy(r.gall.at[there], r.gg.at[rows_at(slot * group, group)], lsem.at[slot, 1]),
            pltpu.make_async_copy(r.tall.at[there], r.tg.at[slot], lsem.at[slot, 2]),
        )

    final = group + 16

    def to_mate(s):
        return remote(r.st, r.ld.at[s % 2], ms.at[s], mr.at[s], mate, z)

    def to_chip(s, d):
        left = 3 - s
        there = flip(c, left % 2, left // 2, 0)
        if d == NZ:
            part = (slice(group, final), slice(0, group))
        else:
            part = (rows_at((z + d) % NZ * length, length), slice(None))
        return remote(r.stc.at[(s,) + part], r.xrecv.at[(s,) + part], xs_s.at[s, d], xs_r.at[s, d], there, z)

    def keep_y(s):
        return pltpu.make_async_copy(r.sty, r.ypart.at[s], ysem)

    slot_ids = lax.broadcasted_iota(jnp.int32, (SLOTS, length), 0).astype(f32)
    row_ids = lax.broadcasted_iota(jnp.int32, (16, length), 0)
    table_rows = lax.broadcasted_iota(jnp.int32, (16, 2 * length), 0)

    acopy.wait()
    for copy in loads(0):
        copy.start()

    def body(s, carry):
        for par in range(2):
            one_group(s, par)
        return carry

    def one_group(s, par):
        g = 2 * s + par
        slot = par
        for copy in loads(g):
            copy.wait()

        @pl.when(g < 7)
        def _():
            for copy in loads(g + 1):
                copy.start()

        @pl.when(s > 0)
        def _():
            if par == 0:
                to_mate(s - 1).wait_send()
            else:
                keep_y(s - 1).wait()

        scales = [[], []]
        for q in range(NZ):
            hits = []
            for e in range(2):
                mine = jnp.sum(jnp.where(table_rows == 2 * c + e, r.tg[slot, q], 0.0), axis=0, keepdims=True)
                rank = mine[:, :length]
                share = mine[:, length:]
                hit = slot_ids == rank
                scales[e].append(jnp.sum(jnp.where(hit, share, 0.0), axis=1, keepdims=True))
                hits.append(jnp.where(hit, 1.0, 0.0))
            hot = jnp.concatenate(hits, axis=0).astype(bf16)
            r.oh[q] = hot
            for ref, at in ((r.bg, 0), (r.gg, group)):
                first = slot * group + q * length
                part = dot(hot, ref[first : first + length]).astype(bf16)
                r.pool[at + q * SLOTS : at + (q + 1) * SLOTS] = part[:SLOTS]
                r.pool[at + step + q * SLOTS : at + step + (q + 1) * SLOTS] = part[SLOTS:]
        back = [0.0] * NZ
        for e in range(2):
            own = slice(step * e, step * (e + 1))
            other = slice(group + step * e, group + step * (e + 1))
            scale = jnp.concatenate(scales[e], axis=0)
            both = dot(r.pool[own], r.wgu[e])
            up = both[:, WIDE:]
            silu, slope = swish(both[:, :WIDE])
            inner = (silu * up).astype(bf16)
            scaled = (inner.astype(f32) * scale).astype(bf16)
            out = dot(scaled, r.wdn[e]).astype(bf16)
            pull = dot(r.pool[other], r.wdn[e], NT)
            gain = jnp.sum(inner.astype(f32) * pull, axis=1, keepdims=True)
            pull = pull * scale
            turn = jnp.concatenate([(pull * up * slope).astype(bf16), (pull * silu).astype(bf16)], axis=1)
            r.ddn[e] += dot(scaled, r.pool[other], TN)
            r.acc[e] += dot(r.pool[own], turn, TN)
            into = dot(turn, r.wgu[e], NT).astype(bf16)
            for q in range(NZ):
                part = slice(q * SLOTS, (q + 1) * SLOTS)
                r.ys[q, e * SLOTS : (e + 1) * SLOTS] = out[part]
                r.ds[q, e * SLOTS : (e + 1) * SLOTS] = into[part]
                hit = r.oh[q, e * SLOTS : (e + 1) * SLOTS].astype(f32)
                line = jnp.sum(hit * gain[part], axis=0, keepdims=True)
                back[q] = back[q] + jnp.where(row_ids == 2 * c + e, line, 0.0)
        if par == 1:
            to_mate(s).wait_recv()
        for q in range(NZ):
            part = slice(q * length, (q + 1) * length)
            more = slice(final + q * length, final + (q + 1) * length)
            pulled = dot(r.oh[q], r.ds[q], TN)
            value = dot(r.oh[q], r.ys[q], TN)
            if par == 0:
                r.st[part] = pulled.astype(bf16)
                r.st[more] = value.astype(bf16)
                r.st[group:final, part] = back[q].astype(bf16)
            else:
                arrived = r.ld.at[s % 2]
                r.stc[s, part] = (pulled + arrived[part].astype(f32)).astype(bf16)
                r.sty[part] = (value + arrived[more].astype(f32)).astype(bf16)
                r.stc[s, group:final, part] = (back[q] + arrived[group:final, part].astype(f32)).astype(bf16)

        def own_column():
            for h in range(2):
                first = slot * group + h * step
                tokens = r.bg[first : first + step]
                upper = r.gg[first : first + step]
                both = dot(tokens, r.wgu[2])
                up = both[:, WIDE:]
                silu, slope = swish(both[:, :WIDE])
                inner = (silu * up).astype(bf16)
                part = slice(step * h, step * (h + 1))
                r.sty[part] = (r.sty[part].astype(f32) + dot(inner, r.wdn[2])).astype(bf16)
                pull = dot(upper, r.wdn[2], NT)
                turn = jnp.concatenate([(pull * up * slope).astype(bf16), (pull * silu).astype(bf16)], axis=1)
                r.stc[3, part] = (r.stc[3, part].astype(f32) + dot(turn, r.wgu[2], NT)).astype(bf16)
                if h == 0:
                    r.dsdn[...] = dot(inner, upper, TN).astype(bf16)
                    r.dsgu[...] = dot(tokens, turn, TN).astype(bf16)
                else:
                    r.dsdn[...] = (r.dsdn[...].astype(f32) + dot(inner, upper, TN)).astype(bf16)
                    r.dsgu[...] = (r.dsgu[...].astype(f32) + dot(tokens, turn, TN)).astype(bf16)

        if par == 0:
            to_mate(s).start()
        else:
            pl.when(s == 3)(own_column)
            keep_y(s).start()

            @pl.when(s < 3)
            def _():
                for d in range(NZ + 1):
                    to_chip(s, d).start()

    lax.fori_loop(0, 4, body, 0)
    for i in range(3):
        to_chip(i, NZ).wait_recv()

    def zcopy(d):
        there = (z + d) % NZ
        return remote(
            r.zbuf.at[there, 0:length], r.zrecv.at[d - 1, 0:length], zs.at[d - 1, 0], zr.at[d - 1, 0], c, there
        )

    def zsmall(d):
        there = (z + d) % NZ
        lanes = (slice(length, length + 16), slice(0, length))
        return remote(
            r.zbuf.at[(there,) + lanes], r.zrecv.at[(d - 1,) + lanes], zs.at[d - 1, 1], zr.at[d - 1, 1], c, there
        )

    for d in (1, 2, 3, 0):
        q = (z + d) % NZ
        for i in range(3):
            to_chip(i, d).wait_recv()

        def add(i, carry):
            part = rows_at(i * 16, 16)
            there = rows_at(q * length + i * 16, 16)
            total = r.stc[3, there].astype(f32)
            for k in range(3):
                total = total + r.xrecv[k, there].astype(f32)
            r.zbuf[q, part] = total.astype(bf16)
            return carry

        lax.fori_loop(0, length // 16, add, 0)
        total = r.stc[3, group:final, lanes_at(q * length, length)].astype(f32)
        for k in range(3):
            total = total + r.xrecv[k, group:final, lanes_at(q * length, length)].astype(f32)
        r.zbuf[q, length : length + 16, 0:length] = total.astype(bf16)
        if d:
            zcopy(d).start()
            zsmall(d).start()
    r.wgu[0:2] = r.acc[...].astype(bf16)
    acccopy = pltpu.make_async_copy(r.wgu.at[0:2], r.accout, accsem)
    acccopy.start()
    for d in range(1, NZ):
        zcopy(d).wait_recv()
        zsmall(d).wait_recv()

    def settle(i, carry):
        part = rows_at(i * 16, 16)
        value = r.zbuf[z, part].astype(f32)
        for d in range(3):
            value = value + r.zrecv[d, part].astype(f32)
        r.db[part] = value
        return carry

    lax.fori_loop(0, length // 16, settle, 0)
    value = r.zbuf[z, length : length + 16, 0:length].astype(f32)
    for d in range(3):
        value = value + r.zrecv[d, length : length + 16, 0:length].astype(f32)
    r.dg[...] = value
    acccopy.wait()
    to_mate(3).wait_send()
    for i in range(3):
        for d in range(NZ + 1):
            to_chip(i, d).wait_send()
    keep_y(3).wait()
    wo_each(wo_drain)
    for d in range(1, NZ):
        zcopy(d).wait_send()
        zsmall(d).wait_send()
        wgcopy(0, d).wait_send()
        wgcopy(1, d).wait_send()
        h1copy(d).wait_send()
        pcopy(d).wait_send()
    for spread in (spread_docs, spread_h2, spread_g, spread_s, spread_b, spread_t):
        spread.drain()


def front_stage(capacity, *operands):
    x, cosine = operands[0], operands[6]
    length, width = x.shape
    count = cosine.shape[0]
    shard = width // NZ
    group = NZ * length
    final = group + 16
    inner = 2 * WIDE
    dma = pltpu.SemaphoreType.DMA
    hbm = pl.BlockSpec(memory_space=pl.ANY)
    vmem = pl.BlockSpec(memory_space=pltpu.VMEM)
    f32, bf16 = jnp.float32, jnp.bfloat16
    shape = jax.ShapeDtypeStruct
    head = lambda rows, kind: shape((rows, HEAD_DIM), kind)
    return pl.pallas_call(
        functools.partial(front_kernel, capacity),
        name="front",
        out_shape=[
            shape((length, width), f32), shape((length, width), bf16), shape((16, length), f32),
            shape((32, width), f32), shape((8, 128), f32),
            shape((count, width), bf16), shape((width, 768), bf16), shape((256, width), bf16),
            head(count, bf16), head(count, bf16), head(count, bf16), head(count, bf16), head(count, bf16),
            head(count, bf16), head(count, f32), head(count, f32), head(2 * length, f32), head(2 * length, f32),
            shape((count, 256), bf16), shape((length, width), f32), shape((16, length), f32),
            shape((2, WIDE, width), f32), shape((width, inner), bf16), shape((WIDE, width), bf16),
            shape((8, group, width), bf16), shape((NZ, 3, shard, inner), bf16), shape((8, group, width), bf16), shape((8, NZ, 16, 2 * length), f32),
            shape((4, group, width), bf16), shape((2, width, inner), bf16),
        ],
        in_specs=[vmem] * 8 + [hbm] * 11,
        out_specs=[vmem] * 5 + [hbm] + [vmem] * 18 + [hbm] * 6,
        scratch_shapes=[
            pltpu.VMEM((2 * group, width), bf16), pltpu.VMEM((9, 8, 128), f32), pltpu.VMEM((32, width), bf16),
            pltpu.VMEM((3, 32, width), bf16),
            pltpu.VMEM((NZ, shard, inner), bf16), pltpu.VMEM((3, width, inner), bf16),
            pltpu.VMEM((3, WIDE, width), bf16), pltpu.VMEM((16, 2 * length), f32), pltpu.VMEM((2, width, inner), f32),
            pltpu.VMEM((2 * group, width), bf16), pltpu.VMEM((2 * group, width), bf16),
            pltpu.VMEM((2, NZ, 16, 2 * length), f32), pltpu.VMEM((NZ, 2 * SLOTS, length), bf16),
            pltpu.VMEM((NZ, 2 * SLOTS, width), bf16), pltpu.VMEM((NZ, 2 * SLOTS, width), bf16),
            pltpu.VMEM((group + final, width), bf16), pltpu.VMEM((4, final, width), bf16),
            pltpu.VMEM((group, width), bf16), pltpu.VMEM((2, group + final, width), bf16),
            pltpu.VMEM((3, final, width), bf16), pltpu.VMEM((NZ, length + 16, width), bf16),
            pltpu.VMEM((3, length + 16, width), bf16),
        ]
        + spread_sems(1) + spread_sems(1) + spread_sems(NZ, 1) + spread_sems() + spread_sems() + spread_sems()
        + spread_sems()
        + [
            dma((3,)), dma((3,)), dma((6,)), dma((3,)), dma((3,)), dma((4,)), dma((4, 2)), dma((4,)),
            dma, dma((2, 3)), dma((2, 3)), dma((2,)), dma, dma((3,)), dma,
            dma((2, 3)), dma((4,)), dma((4,)), dma((3, NZ + 1)), dma((3, NZ + 1)), dma((3, 2)), dma((3, 2)), dma, dma,
        ]
        + plane_scratch(length, width)[3:],
        compiler_params=pltpu.CompilerParams(
            collective_id=1, has_side_effects=True, vmem_limit_bytes=62 * MIB
        ),
    )(*operands)


def backward_kernel(
    ypart, accout, dsgu, dsdn, db_ref, dg_ref, g_ref, x_ref, hidden_ref, b_ref, gates_ref, psum_ref, bound_ref, cos_ref, sin_ref,
    aall, wall, woall, q1, k1, v1, q2, k2, v2, att1, lse1, att2, lse2, mixed,
    out_ref, gtok_ref, small_ref, wfinal, wofinal, dgu, sfin, sdfin, yrecv,
    dhb, dhall, dm, dk, dv, cat, wst, wrecv, wsum, dwo, worecv, wosum, small4,
    sgm, sdm, sgs, sds, sgx, sdx, sgt, sgz, sdt, ybuf, ysend, yz, *sems,
):
    f32, bf16 = jnp.float32, jnp.bfloat16
    c = lax.axis_index("ctx")
    z = lax.axis_index("fsdp")
    length, width = x_ref.shape
    count = aall.shape[0]
    shard = width // NZ
    quarter = c % 4
    mate = flip(c, 0, 0, 1)
    scale = HEAD_DIM**-0.5
    sems = list(sems)

    spread_h = Spread(lambda _: dhb, lambda o, _: dhall.at[o], take(sems, 7), c, z, 1)
    spread_w = Spread(lambda _: wsum, lambda o, _: wfinal.at[o], take(sems, 7), c, z, 1)
    wzs, wzr, ozs, ozr, oxs, oxr, oms, omr, ss, sr = take(sems, 10)
    yxs, yxr, yzs, yzr, gas, gar, gal, sms, smr, sxs, sxr, szs, szr, ylsem, olsem = take(sems, 15)
    spread_s = Spread(lambda _: sgz, lambda o, _: sfin.at[o], take(sems, 7), c, z, 1)
    spread_d = Spread(lambda _: sdt, lambda o, _: sdfin.at[o], take(sems, 7), c, z, 1)
    reduce_refs = take(sems, 8)
    core = c % 2
    chip = c // 2
    sub = shard // 4
    part_rows = sdt.shape[0]

    def ycopy(i):
        return remote(
            ypart.at[(1, 2, 0)[i]], yrecv.at[i], yxs.at[i], yxr.at[i], flip(c, PEERS[i][0], PEERS[i][1], 0), z
        )

    def yload(i):
        src = ypart.at[3] if i == 3 else yrecv.at[i]
        return pltpu.make_async_copy(src, ybuf.at[i], ylsem.at[i])

    def yhop(d):
        return remote(ysend.at[(z + d) % NZ], yz.at[d - 1], yzs.at[d - 1], yzr.at[d - 1], c, (z + d) % NZ)

    def gcopy(d):
        there = (z + d) % NZ
        return remote(
            accout.at[:, rows_at(there * shard, shard), :], dgu.at[z], gas.at[d - 1], gar.at[d - 1], c, there
        )

    gown = pltpu.make_async_copy(accout.at[:, rows_at(z * shard, shard), :], dgu.at[z], gal)

    def smate(i):
        if i == 0:
            return remote(dsgu.at[:, lanes_at((1 - core) * WIDE, WIDE)], sgm, sms.at[0], smr.at[0], mate, z)
        return remote(dsdn.at[rows_at((1 - core) * 4 * part_rows, 4 * part_rows)], sdm, sms.at[1], smr.at[1], mate, z)

    def schip(i, kind):
        there = flip(c, PEERS[i][0], PEERS[i][1], 0)
        if kind == 0:
            return remote(sgs.at[:, there // 2], sgx.at[i], sxs.at[i, 0], sxr.at[i, 0], there, z)
        return remote(sds.at[there // 2], sdx.at[i], sxs.at[i, 1], sxr.at[i, 1], there, z)

    def shop(d):
        there = (z + d) % NZ
        return remote(sgt.at[there], sgz.at[z], szs.at[d - 1], szr.at[d - 1], c, there)
    greet(c, z)
    packed = psum_ref[...]
    gain_one = packed[17:18]
    gain_two = packed[16:17]
    router = packed[0:16].astype(bf16)
    hidden = hidden_ref[...]
    factor_two = norm_factor(hidden)
    normed_two = hidden * factor_two
    gates = gates_ref[...]
    d_gates = dg_ref[...]
    d_logits = gates * (d_gates - jnp.sum(gates * d_gates, axis=0, keepdims=True))
    d_b = db_ref[...] + split_dot(d_logits, router, TN)
    small_ref[...] = jnp.zeros_like(small_ref)
    small_ref[0:16] = split_dot(d_logits, b_ref[...])
    small_ref[16:17] = jnp.sum(d_b * normed_two, axis=0, keepdims=True)
    pulled = d_b * gain_two
    d_hidden = g_ref[...].astype(f32) + factor_two * (
        pulled - normed_two * jnp.mean(pulled * normed_two, axis=1, keepdims=True)
    )
    dhb[...] = d_hidden.astype(bf16)
    spread_h.start_z()
    spread_h.start_x()
    smate(0).start()
    smate(1).start()
    gown.start()
    for d in range(1, NZ):
        gcopy(d).start()
    dk[...] = jnp.zeros_like(dk)
    dv[...] = jnp.zeros_like(dv)
    cat[:, 384:512] = jnp.zeros((count, 128), bf16)
    spread_h.relay_x()
    for i in range(3):
        ycopy(i).start()
    spread_h.arrive()
    step = 2 * length
    for i in range(count // step):
        block = dhall[2 * i : 2 * i + 2].reshape(step, width)
        dm[i * step : (i + 1) * step] = dot(block, woall[...], NT).astype(bf16)
        part = dot(mixed[i * step : (i + 1) * step], block, TN)
        if i == 0:
            dwo[...] = part
        else:
            dwo[...] += part
    wosum[...] = dwo[...].astype(bf16).reshape(wosum.shape)

    def oz(j, owner):
        d = (owner + NZ - z) % NZ
        return remote(wosum.at[j], worecv.at[j, d - 1], ozs.at[j], ozr.at[j, d - 1], c, owner)

    def oz_wait(j, d):
        return remote(wosum.at[j], worecv.at[j, d], ozs.at[j], ozr.at[j, d], c, z)

    for j, (_, owner) in enumerate(head_rows(c)):

        @pl.when(owner != z)
        def _(j=j, owner=owner):
            oz(j, owner).start()

    smate(0).wait_recv()
    smate(1).wait_recv()
    for q in range(NZ):
        for j in range(4):
            part = slice(q * shard + j * sub, q * shard + (j + 1) * sub)
            own = dsgu[part, lanes_at(core * WIDE, WIDE)].astype(f32)
            sgs[q, j] = (own + sgm[part].astype(f32)).astype(bf16)
    for j in range(4):
        own = dsdn[rows_at(core * 4 * part_rows + j * part_rows, part_rows)].astype(f32)
        sds[j] = (own + sdm[j * part_rows : (j + 1) * part_rows].astype(f32)).astype(bf16)
    for i in range(3):
        schip(i, 0).start()
        schip(i, 1).start()
    boundary = bound_ref[0:1, 0:1]

    def pull_back(queries, first, keys, values, n, upper, out, lse, which):
        scores = dot(queries, keys[0:n], NT) * scale
        scores = jnp.where(visible(first, step, n, boundary), scores, negative)
        shares = jnp.exp(scores - lse[:, 0:1])
        delta = jnp.sum(upper.astype(f32) * out, axis=1, keepdims=True)
        pulled = (scale * (shares * (dot(upper, values[0:n], NT) - delta))).astype(bf16)
        dk[which, 0:n] += dot(pulled, queries, TN)
        dv[which, 0:n] += dot(shares.astype(bf16), upper, TN)
        return dot(pulled, keys[0:n]).astype(bf16).astype(f32)

    for i in range(count // step):
        part = slice(i * step, (i + 1) * step)
        got = pull_back(q1[part], i * step, k1, v1, (i + 1) * step, dm[part, 0:128], att1[part], lse1[part], 0)
        cat[part, 0:128] = turned(got, cos_ref[part], -sin_ref[part]).astype(bf16)
    mine = rows_at(quarter * step, step)
    got = pull_back(q2[mine], quarter * step, k2, v2, count, dm[mine, 128:256], att2[...], lse2[...], 1)
    cat[mine, 384:512] = turned(got, cos_ref[mine], -sin_ref[mine]).astype(bf16)
    for which in range(2):
        at = 384 * which
        keys = dk[which].astype(bf16).astype(f32)
        cat[:, at + 128 : at + 256] = turned(keys, cos_ref[...], -sin_ref[...]).astype(bf16)
        cat[:, at + 256 : at + 384] = dv[which].astype(bf16)
    for i in range(width // 256):
        wst[256 * i : 256 * i + 256] = dot(aall[:, 256 * i : 256 * i + 256], cat[...], TN).astype(bf16)

    def wz(d):
        there = (z + d) % NZ
        return remote(
            wst.at[rows_at(there * shard, shard)], wrecv.at[d - 1], wzs.at[d - 1], wzr.at[d - 1], c, there
        )

    for d in range(1, NZ):
        wz(d).start()

    total_up = [sgs[q, chip].astype(f32) for q in range(NZ)]
    total_down = sds[chip].astype(f32)
    for i in range(3):
        schip(i, 0).wait_recv()
        schip(i, 1).wait_recv()
        for q in range(NZ):
            total_up[q] = total_up[q] + sgx[i, q].astype(f32)
        total_down = total_down + sdx[i].astype(f32)
    for q in range(NZ):
        sgt[q] = total_up[q].astype(bf16)
    sdt[...] = total_down.astype(bf16)
    sgz[z] = sgt[z]
    for d in range(1, NZ):
        shop(d).start()
    spread_d.start_z()
    spread_d.start_x()

    def ox(j, i):
        there = flip(c, PEERS[i][0], PEERS[i][1], 0)
        return remote(wosum.at[j], wofinal.at[c, j], oxs.at[j, i], oxr.at[j, i], there, z)

    def om(j, i):
        fy, fx = (((0, 0),) + PEERS)[i]
        origin = flip(c, fy, fx, 0)
        src = wosum.at[j] if i == 0 else wofinal.at[origin, j]
        return remote(src, wofinal.at[origin, j], oms.at[j, i], omr.at[j, i], mate, z)

    def wo_keep(j):
        return pltpu.make_async_copy(wosum.at[j], wofinal.at[c, j], olsem.at[j])

    for j, (_, owner) in enumerate(head_rows(c)):

        @pl.when(owner == z)
        def _(j=j):
            for d in range(3):
                oz_wait(j, d).wait_recv()
            total = wosum[j].astype(f32)
            for d in range(3):
                total = total + worecv[j, d].astype(f32)
            wosum[j] = total.astype(bf16)
            wo_keep(j).start()
            for i in range(3):
                ox(j, i).start()
            om(j, 0).start()

    value = plane_reduce(
        lambda o: dot(cat[rows_at(o * length, length)], wall[...], NT), c, z, reduce_refs
    )
    x = x_ref[...].astype(f32)
    factor_one = norm_factor(x)
    normed_one = x * factor_one
    small_ref[17:18] = jnp.sum(value * normed_one, axis=0, keepdims=True)
    pulled = value * gain_one
    gtok_ref[...] = (
        d_hidden
        + factor_one * (pulled - normed_one * jnp.mean(pulled * normed_one, axis=1, keepdims=True))
    ).astype(bf16)

    def exchange(stage, slots, targets):
        copies = [
            remote(small4.at[stage], small4.at[slot], ss.at[slot], sr.at[slot], tc, tz)
            for slot, (tc, tz) in zip(slots, targets)
        ]
        for copy in copies:
            copy.start()
        for copy in copies:
            copy.wait_recv()
        value = small4[stage]
        for slot in slots:
            value = value + small4[slot]
        return value, copies

    small4[0] = small_ref[...]
    value, sent = exchange(0, (1,), ((mate, z),))
    small4[2] = value
    value, more = exchange(2, (3, 4, 5), [(flip(c, fy, fx, 0), z) for fy, fx in PEERS])
    sent += more
    small4[6] = value
    last_hop = [
        remote(small4.at[6], small4.at[6 + d], ss.at[6 + d], sr.at[6 + d], c, (z + d) % NZ) for d in range(1, NZ)
    ]
    for copy in last_hop:
        copy.start()
    for i in range(3):
        ycopy(i).wait_recv()
        yload(i).start()
    yload(3).start()
    for d in range(1, NZ):
        shop_wait = sgz.at[(z + NZ - d) % NZ]
        remote(shop_wait, shop_wait, szs.at[d - 1], szr.at[d - 1], c, z).wait_recv()
    spread_s.start_z()
    spread_s.start_x()
    total = wst[rows_at(z * shard, shard)].astype(f32)
    for d in range(1, NZ):
        wz(d).wait_recv()
        total = total + wrecv[d - 1].astype(f32)
    wsum[...] = total.astype(bf16)
    spread_w.start_z()
    spread_w.start_x()

    for i in range(4):
        yload(i).wait()

    def ysum(i, carry):
        part = rows_at(i * 16, 16)
        value = ybuf[0, part].astype(f32)
        for k in range(1, 4):
            value = value + ybuf[k, part].astype(f32)
        ysend[i // (length // 16), rows_at(i % (length // 16) * 16, 16)] = value.astype(bf16)
        return carry

    lax.fori_loop(0, NZ * length // 16, ysum, 0)
    for d in range(1, NZ):
        yhop(d).start()

    for i in range(3):
        for j, (_, owner) in enumerate(head_rows(flip(c, PEERS[i][0], PEERS[i][1], 0))):

            @pl.when(owner == z)
            def _(j=j, i=i):
                origin = flip(c, PEERS[i][0], PEERS[i][1], 0)
                block = wofinal.at[origin, j]
                remote(block, block, oxs.at[j, i], oxr.at[j, i], c, z).wait_recv()
                om(j, i + 1).start()

    spread_w.relay_x()
    for i in range(4):
        fy, fx = (((0, 0),) + PEERS)[i]
        for j, (_, owner) in enumerate(head_rows(flip(c, fy, fx, 1))):

            @pl.when(owner == z)
            def _(j=j, i=i, fy=fy, fx=fx):
                block = wofinal.at[flip(c, fy, fx, 1), j]
                remote(block, block, oms.at[j, i], omr.at[j, i], c, z).wait_recv()

    value = small4[6]
    for d in range(1, NZ):
        last_hop[d - 1].wait_recv()
        value = value + small4[6 + d]
    small_ref[...] = value
    spread_s.relay_x()
    spread_d.relay_x()
    value = hidden + ysend[z].astype(f32)
    for d in range(1, NZ):
        yhop(d).wait_recv()
        value = value + yz[d - 1].astype(f32)
    out_ref[...] = value.astype(bf16)
    spread_w.arrive()
    spread_s.arrive()
    spread_d.arrive()
    gown.wait()
    for d in range(1, NZ):
        gcopy(d).wait()
        yhop(d).wait_send()
        shop(d).wait_send()
    for i in range(3):
        ycopy(i).wait_send()
        schip(i, 0).wait_send()
        schip(i, 1).wait_send()
    smate(0).wait_send()
    smate(1).wait_send()
    for copy in sent + last_hop:
        copy.wait_send()
    for j, (_, owner) in enumerate(head_rows(c)):

        @pl.when(owner != z)
        def _(j=j, owner=owner):
            oz(j, owner).wait_send()

        @pl.when(owner == z)
        def _(j=j):
            for i in range(3):
                ox(j, i).wait_send()
            om(j, 0).wait_send()
            wo_keep(j).wait()

    for i in range(3):
        for j, (_, owner) in enumerate(head_rows(flip(c, PEERS[i][0], PEERS[i][1], 0))):

            @pl.when(owner == z)
            def _(j=j, i=i):
                om(j, i + 1).wait_send()

    for d in range(1, NZ):
        wz(d).wait_send()
    for spread in (spread_h, spread_w, spread_s, spread_d):
        spread.drain()


def backward_stage(*operands):
    x, aall, dsdn = operands[7], operands[15], operands[3]
    length, width = x.shape
    count = aall.shape[0]
    shard = width // NZ
    sub = shard // 4
    part_rows = dsdn.shape[0] // 8
    dma = pltpu.SemaphoreType.DMA
    hbm = pl.BlockSpec(memory_space=pl.ANY)
    vmem = pl.BlockSpec(memory_space=pltpu.VMEM)
    f32, bf16 = jnp.float32, jnp.bfloat16
    shape = jax.ShapeDtypeStruct
    return pl.pallas_call(
        backward_kernel,
        name="backward",
        out_shape=[
            shape((length, width), bf16), shape((length, width), bf16), shape((32, width), f32),
            shape((8, shard, 768), bf16), shape((8, 4, 64, width), bf16), shape((NZ, 2, shard, 2 * WIDE), bf16),
            shape((8, NZ, sub, WIDE), bf16), shape((8, part_rows, width), bf16), shape((3, NZ * length, width), bf16),
        ],
        in_specs=[hbm] * 2 + [vmem] * (len(operands) - 2),
        out_specs=[vmem] * 3 + [hbm] * 6,
        scratch_shapes=[
            pltpu.VMEM((length, width), bf16), pltpu.VMEM((8, length, width), bf16), pltpu.VMEM((count, 256), bf16),
            pltpu.VMEM((2, count, 128), f32), pltpu.VMEM((2, count, 128), f32), pltpu.VMEM((count, 768), bf16),
            pltpu.VMEM((width, 768), bf16), pltpu.VMEM((3, shard, 768), bf16), pltpu.VMEM((shard, 768), bf16),
            pltpu.VMEM((256, width), f32), pltpu.VMEM((4, 3, 64, width), bf16),
            pltpu.VMEM((4, 64, width), bf16), pltpu.VMEM((10, 32, width), f32),
            pltpu.VMEM((width, WIDE), bf16), pltpu.VMEM((4 * part_rows, width), bf16),
            pltpu.VMEM((NZ, 4, sub, WIDE), bf16), pltpu.VMEM((4, part_rows, width), bf16),
            pltpu.VMEM((3, NZ, sub, WIDE), bf16), pltpu.VMEM((3, part_rows, width), bf16),
            pltpu.VMEM((NZ, sub, WIDE), bf16), pltpu.VMEM((NZ, sub, WIDE), bf16), pltpu.VMEM((part_rows, width), bf16),
            pltpu.VMEM((4, NZ * length, width), bf16), pltpu.VMEM((NZ, length, width), bf16),
            pltpu.VMEM((3, length, width), bf16),
        ]
        + spread_sems(1) + spread_sems(1)
        + [
            dma((3,)), dma((3,)), dma((4,)), dma((4, 3)), dma((4, 3)), dma((4, 3)), dma((4, 4)), dma((4, 4)),
            dma((10,)), dma((10,)),
            dma((3,)), dma((3,)), dma((3,)), dma((3,)), dma((3,)), dma((3,)), dma, dma((2,)), dma((2,)),
            dma((3, 2)), dma((3, 2)), dma((3,)), dma((3,)), dma((4,)), dma((4,)),
        ]
        + spread_sems(1) + spread_sems(1)
        + plane_scratch(length, width),
        compiler_params=pltpu.CompilerParams(
            collective_id=3, has_side_effects=True, vmem_limit_bytes=62 * MIB
        ),
    )(*operands)


def gather_kernel(
    wfinal, wofinal, dgu, sfin, sdfin, ddn, gwq, gwk, gwv, gwo, gsg, gsu, gsd, geg, geu, ged,
):
    f32, bf16 = jnp.float32, jnp.bfloat16
    z = lax.axis_index("fsdp")
    hidden_dev = gsd.shape[0]
    sub = sfin.shape[2]
    for n, ref in enumerate((gwq, gwk, gwv)):
        for o in range(8):
            ref[:, 128 * o : 128 * o + 128] = wfinal[o, :, 128 * n : 128 * n + 128].astype(f32)
        for y in range(2):
            lanes = slice(384 + 128 * n, 512 + 128 * n)
            ref[:, 1024 + 128 * y : 1152 + 128 * y] = sum(
                wfinal[4 * y + k, :, lanes].astype(f32) for k in range(4)
            )
    for i in range(5):
        b = 5 * z + i

        @pl.when(b < 16)
        def _(b=b, i=i):
            low = jnp.minimum(b, 15)
            gwo[64 * i : 64 * i + 64] = wofinal[low // 2, low % 2].astype(f32)

        @pl.when(b >= 16)
        def _(b=b, i=i):
            high = jnp.maximum(b, 16) - 16
            gwo[64 * i : 64 * i + 64] = sum(
                wofinal[4 * (high // 2) + k, 2 + high % 2].astype(f32) for k in range(4)
            )

    units = geg.shape[2]
    for e in range(2):
        ged[e] = ddn[e, 0:hidden_dev]
    for o in range(8):
        start = 128 * (o % 2) + 32 * (o // 2)
        size = min(32, hidden_dev - start)
        if size > 0:
            gsd[start : start + size] = sdfin[o, 0:size].astype(f32)
    slot = lax.broadcasted_iota(jnp.int32, (WIDE, units), 0)
    unit = lax.broadcasted_iota(jnp.int32, (WIDE, units), 1)
    for q in range(NZ):
        put = jnp.where((unit == slot + q * hidden_dev) & (slot < hidden_dev), 1.0, 0.0).astype(bf16)
        for h, (ref, shared) in enumerate(((geg, gsg), (geu, gsu))):
            for e in range(2):
                part = dot(dgu[q, e, :, h * WIDE : (h + 1) * WIDE], put)
                if q == 0:
                    ref[e] = part
                else:
                    ref[e] += part
            for j in range(4):
                part = dot(sfin[2 * j + h, q], put)
                if q == 0:
                    shared[sub * j : sub * j + sub] = part
                else:
                    shared[sub * j : sub * j + sub] += part


def gather_stage(wfinal, wofinal, dgu, sfin, sdfin, ddn, hidden_dev):
    width = wofinal.shape[3]
    shard = wfinal.shape[1]
    units = NZ * hidden_dev
    f32 = jnp.float32
    shape = jax.ShapeDtypeStruct
    vmem = pl.BlockSpec(memory_space=pltpu.VMEM)
    square = shape((shard, width), f32)
    return pl.pallas_call(
        gather_kernel,
        name="assemble",
        out_shape=[
            square, square, square, square, shape((shard, units), f32), shape((shard, units), f32),
            shape((hidden_dev, width), f32), shape((2, shard, units), f32), shape((2, shard, units), f32),
            shape((2, hidden_dev, width), f32),
        ],
        in_specs=[vmem] * 6,
        out_specs=[vmem] * 10,
        compiler_params=pltpu.CompilerParams(vmem_limit_bytes=60 * MIB),
    )(wfinal, wofinal, dgu, sfin, sdfin, ddn)


def per_device_fast(
    tokens,
    documents,
    routes,
    priority,
    attention_gain,
    query_weight,
    key_weight,
    value_weight,
    output_weight,
    feedforward_gain,
    router_weight,
    shared_gate,
    shared_up,
    shared_down,
    expert_gate,
    expert_up,
    expert_down,
    cotangent,
):
    f32, bf16 = jnp.float32, jnp.bfloat16
    z = lax.axis_index("fsdp")
    length = tokens.shape[1]
    row_length = length * 8
    experts = EXP_DEV * 8
    capacity = 9 * length * TOPK // (8 * experts)
    shard = query_weight.shape[0]
    hidden_dev = expert_gate.shape[2] // NZ
    frequency = theta_base ** (-np.arange(HEAD_DIM // 2, dtype=np.float32) / (HEAD_DIM // 2))
    angles = np.arange(row_length, dtype=np.float32)[:, None] * frequency.astype(np.float32)[None, :]
    cosine, sine = np.cos(angles), np.sin(angles)
    cosine_wide = jnp.asarray(np.concatenate([cosine, cosine], axis=1), f32)
    sine_wide = jnp.asarray(np.concatenate([-sine, sine], axis=1), f32)
    gains = jnp.concatenate([feedforward_gain[None], attention_gain[None], jnp.zeros((14, shard), bf16)], axis=0)
    front = dict(
        zip(
            FRONT_OUT,
            front_stage(
                capacity, tokens[0], router_weight, gains, documents, routes[0], priority[0], cosine_wide, sine_wide,
                cotangent[0], query_weight, key_weight, value_weight, output_weight, expert_gate, expert_up,
                shared_gate, shared_up, expert_down, shared_down,
            ),
        )
    )
    kept = FRONT_OUT[5:19]
    output_rows, grad_tokens, small, wfinal, wofinal, dgu, sfin, sdfin = backward_stage(
        *[front[n] for n in ("ypart", "accout", "dsgu", "dsdn", "db", "dg")], cotangent[0], tokens[0],
        *[front[n] for n in ("hidden", "tokens", "gates", "psum", "bound")], cosine_wide, sine_wide,
        *[front[n] for n in kept]
    )[:8]
    gwq, gwk, gwv, gwo, gsg, gsu, gsd, geg, geu, ged = gather_stage(
        wfinal, wofinal, dgu, sfin, sdfin, front["ddn"], hidden_dev
    )
    mine = lax.dynamic_slice_in_dim(small, z * shard, shard, 1)
    return (
        output_rows[None], grad_tokens[None], mine[17], gwq, gwk, gwv, gwo, mine[16], mine[:16].T, gsg, gsu, gsd, geg,
        geu, ged,
    )


def per_device(
    tokens,
    documents,
    routes,
    priority,
    attention_gain,
    query_weight,
    key_weight,
    value_weight,
    output_weight,
    feedforward_gain,
    router_weight,
    shared_gate,
    shared_up,
    shared_down,
    expert_gate,
    expert_up,
    expert_down,
    cotangent,
):
    gathered = (
        lax.all_gather(attention_gain, "fsdp", axis=0, tiled=True),
        lax.all_gather(query_weight, "fsdp", axis=0, tiled=True),
        lax.all_gather(key_weight, "fsdp", axis=0, tiled=True),
        lax.all_gather(value_weight, "fsdp", axis=0, tiled=True),
        lax.all_gather(output_weight, "fsdp", axis=0, tiled=True),
        lax.all_gather(feedforward_gain, "fsdp", axis=0, tiled=True),
        lax.all_gather(router_weight, "fsdp", axis=0, tiled=True),
        lax.all_gather(shared_gate, "fsdp", axis=0, tiled=True),
        lax.all_gather(shared_up, "fsdp", axis=0, tiled=True),
        lax.all_gather(shared_down, "fsdp", axis=0, tiled=True),
        lax.all_gather(expert_gate, "fsdp", axis=1, tiled=True),
        lax.all_gather(expert_up, "fsdp", axis=1, tiled=True),
        lax.all_gather(expert_down, "fsdp", axis=1, tiled=True),
    )
    (
        gain_one,
        w_query,
        w_key,
        w_value,
        w_output,
        gain_two,
        w_router,
        w_shared_gate,
        w_shared_up,
        w_shared_down,
        w_expert_gate,
        w_expert_up,
        w_expert_down,
    ) = gathered
    groups = lax.axis_size("ctx")
    length = tokens.shape[1]
    row_length = length * groups
    experts = EXP_DEV * groups
    capacity = 9 * length * TOPK // (8 * experts)
    inner_width = HEADS * HEAD_DIM
    score_scale = HEAD_DIM ** (-0.5)
    spare_slot = experts * capacity
    first_here = lax.axis_index("ctx") * length
    positions = first_here + jnp.arange(length, dtype=jnp.int32)
    last_here = first_here + length - 1
    doc_here = documents[0].astype(jnp.float32)
    doc_wire = documents[0].astype(jnp.bfloat16)
    inputs = tokens[0].astype(jnp.float32)
    upstream_low = cotangent[0]
    upstream = upstream_low.astype(jnp.float32)
    factor_one = rms_factor(inputs)
    normed_one = inputs * factor_one
    gain_one_wide = gain_one.astype(jnp.float32)
    attn_input = (normed_one * gain_one_wide).astype(jnp.bfloat16)
    query_pre = jnp.dot(attn_input, w_query, preferred_element_type=jnp.float32).reshape(
        length, HEADS, HEAD_DIM
    )
    key_pre = jnp.dot(attn_input, w_key, preferred_element_type=jnp.float32).reshape(
        length, HEADS, HEAD_DIM
    )
    cosine, sine = rotary_tables(positions, HEAD_DIM // 2)
    queries = rotate(query_pre, cosine, sine).astype(jnp.bfloat16)
    key_rows = rotate(key_pre, cosine, sine).astype(jnp.bfloat16)
    value_rows = (
        jnp.dot(attn_input, w_value, preferred_element_type=jnp.float32)
        .astype(jnp.bfloat16)
        .reshape(length, HEADS, HEAD_DIM)
    )
    initial = (
        jnp.zeros((HEADS, length, HEAD_DIM), jnp.float32),
        jnp.full((HEADS, length), negative, jnp.float32),
        jnp.zeros((HEADS, length), jnp.float32),
    )
    key_all = lax.all_gather(key_rows, "ctx", axis=0, tiled=True)
    value_all = lax.all_gather(value_rows, "ctx", axis=0, tiled=True)
    docs_all = lax.all_gather(doc_wire, "ctx", axis=0, tiled=True)

    def visit(progress, within, rows_now):

        def compute(progress):
            accum, highest_seen, totals = progress
            key_block = lax.dynamic_slice_in_dim(key_all, within, rows_now, 0)
            value_block = lax.dynamic_slice_in_dim(value_all, within, rows_now, 0)
            docs_block = lax.dynamic_slice_in_dim(docs_all, within, rows_now, 0).astype(jnp.float32)
            key_pos = within + jnp.arange(rows_now, dtype=jnp.int32)
            allowed = allowed_mask(positions, doc_here, key_pos, docs_block)[None]
            scores = jnp.einsum(
                "qhd,khd->hqk", queries, key_block, preferred_element_type=jnp.float32
            )
            scores = jnp.where(allowed, scores * score_scale, negative)
            newest = jnp.maximum(highest_seen, jnp.max(scores, axis=-1))
            shrink = jnp.exp(highest_seen - newest)
            shares = jnp.exp(scores - newest[..., None]) * allowed
            totals = totals * shrink + jnp.sum(shares, axis=-1)
            accum = accum * shrink[..., None] + jnp.einsum(
                "hqk,khd->hqd",
                shares.astype(jnp.bfloat16),
                value_block,
                preferred_element_type=jnp.float32,
            )
            return (accum, newest, totals)

        return lax.cond(within > last_here, unchanged, compute, progress)

    accum, highest_seen, totals = blockwise(key_all.shape[0], visit, initial)
    attended = accum / totals[..., None]
    log_total = highest_seen + jnp.log(totals)
    mixed_rows = (
        jnp.transpose(attended, (1, 0, 2)).reshape(length, inner_width).astype(jnp.bfloat16)
    )
    hidden = inputs + jnp.dot(mixed_rows, w_output, preferred_element_type=jnp.float32)
    factor_two = rms_factor(hidden)
    normed_two = hidden * factor_two
    gain_two_wide = gain_two.astype(jnp.float32)
    moe_input = (normed_two * gain_two_wide).astype(jnp.bfloat16)
    moe_wide = moe_input.astype(jnp.float32)
    router_wide = w_router.astype(jnp.float32)
    gate_probs = jax.nn.softmax(jnp.dot(moe_wide, router_wide, precision=highest), axis=-1)
    route_now = routes[0]
    order_now = priority[0, 0]
    onehot = (route_now[:, :, None] == jnp.arange(experts, dtype=jnp.int32)).astype(jnp.float32)
    counts = jnp.sum(onehot, axis=1)
    earlier = (order_now[None, :] < order_now[:, None]).astype(jnp.bfloat16)
    before = jnp.dot(earlier, counts.astype(jnp.bfloat16), preferred_element_type=jnp.float32)
    ranking = jnp.sum(onehot * before[:, None, :], axis=-1).astype(jnp.int32)
    kept_mask = ranking < capacity
    slot_index = jnp.where(
        kept_mask,
        route_now % EXP_DEV * (groups * capacity) + route_now // EXP_DEV * capacity + ranking,
        spare_slot,
    )
    chosen = jnp.sum(onehot * gate_probs[:, None, :], axis=-1)
    weight = jnp.where(kept_mask, chosen, 0.0)
    flat_slots = slot_index.reshape(-1)
    copies = jnp.broadcast_to(moe_input[:, None, :], (length, TOPK, D)).reshape(length * TOPK, D)
    outgoing = jnp.zeros((spare_slot + 1, D), jnp.bfloat16).at[flat_slots].set(copies)[:spare_slot]
    arrived = lax.all_to_all(
        outgoing.reshape(EXP_DEV, groups, capacity, D),
        "ctx",
        split_axis=1,
        concat_axis=1,
        tiled=True,
    ).reshape(EXP_DEV, groups * capacity, D)
    gate_act = jnp.einsum(
        "erd,edf->erf", arrived, w_expert_gate, preferred_element_type=jnp.float32
    )
    up_act = jnp.einsum("erd,edf->erf", arrived, w_expert_up, preferred_element_type=jnp.float32)
    silu_gate, slope_gate = silu_parts(gate_act)
    expert_hidden = (silu_gate * up_act).astype(jnp.bfloat16)
    expert_out = jnp.einsum(
        "erf,efd->erd", expert_hidden, w_expert_down, preferred_element_type=jnp.float32
    ).astype(jnp.bfloat16)
    returned = lax.all_to_all(
        expert_out.reshape(EXP_DEV, groups, capacity, D),
        "ctx",
        split_axis=1,
        concat_axis=1,
        tiled=True,
    ).reshape(spare_slot, D)
    returned = jnp.concatenate([returned, jnp.zeros((1, D), jnp.bfloat16)], axis=0)
    picked = returned[slot_index]
    routed = jnp.sum(weight[..., None] * picked, axis=1)
    shared_gate_act = jnp.dot(moe_input, w_shared_gate, preferred_element_type=jnp.float32)
    shared_up_act = jnp.dot(moe_input, w_shared_up, preferred_element_type=jnp.float32)
    silu_shared, slope_shared = silu_parts(shared_gate_act)
    shared_hidden = (silu_shared * shared_up_act).astype(jnp.bfloat16)
    shared_out = jnp.dot(shared_hidden, w_shared_down, preferred_element_type=jnp.float32)
    output_rows = (hidden + shared_out + routed).astype(jnp.bfloat16)
    grad_shared_down = jnp.dot(shared_hidden.T, upstream_low, preferred_element_type=jnp.float32)
    grad_shared_hidden = jnp.dot(upstream_low, w_shared_down.T, preferred_element_type=jnp.float32)
    grad_shared_gate_act = (grad_shared_hidden * shared_up_act * slope_shared).astype(jnp.bfloat16)
    grad_shared_up_act = (grad_shared_hidden * silu_shared).astype(jnp.bfloat16)
    grad_shared_gate = jnp.dot(
        moe_input.T, grad_shared_gate_act, preferred_element_type=jnp.float32
    )
    grad_shared_up = jnp.dot(moe_input.T, grad_shared_up_act, preferred_element_type=jnp.float32)
    grad_moe = jnp.dot(
        grad_shared_gate_act, w_shared_gate.T, preferred_element_type=jnp.float32
    ) + jnp.dot(grad_shared_up_act, w_shared_up.T, preferred_element_type=jnp.float32)
    grad_copies = (
        (weight[..., None] * upstream[:, None, :]).astype(jnp.bfloat16).reshape(length * TOPK, D)
    )
    grad_weight = jnp.sum(picked.astype(jnp.float32) * upstream[:, None, :], axis=-1)
    grad_outgoing = (
        jnp.zeros((spare_slot + 1, D), jnp.bfloat16).at[flat_slots].set(grad_copies)[:spare_slot]
    )
    grad_arrived = lax.all_to_all(
        grad_outgoing.reshape(EXP_DEV, groups, capacity, D),
        "ctx",
        split_axis=1,
        concat_axis=1,
        tiled=True,
    ).reshape(EXP_DEV, groups * capacity, D)
    grad_expert_hidden = jnp.einsum(
        "erd,efd->erf", grad_arrived, w_expert_down, preferred_element_type=jnp.float32
    )
    grad_expert_down = jnp.einsum(
        "erf,erd->efd", expert_hidden, grad_arrived, preferred_element_type=jnp.float32
    )
    grad_gate_act = (grad_expert_hidden * up_act * slope_gate).astype(jnp.bfloat16)
    grad_up_act = (grad_expert_hidden * silu_gate).astype(jnp.bfloat16)
    grad_expert_gate = jnp.einsum(
        "erd,erf->edf", arrived, grad_gate_act, preferred_element_type=jnp.float32
    )
    grad_expert_up = jnp.einsum(
        "erd,erf->edf", arrived, grad_up_act, preferred_element_type=jnp.float32
    )
    grad_arrived_in = (
        jnp.einsum("erf,edf->erd", grad_gate_act, w_expert_gate, preferred_element_type=jnp.float32)
        + jnp.einsum("erf,edf->erd", grad_up_act, w_expert_up, preferred_element_type=jnp.float32)
    ).astype(jnp.bfloat16)
    sent_back = lax.all_to_all(
        grad_arrived_in.reshape(EXP_DEV, groups, capacity, D),
        "ctx",
        split_axis=1,
        concat_axis=1,
        tiled=True,
    ).reshape(spare_slot, D)
    sent_back = jnp.concatenate([sent_back, jnp.zeros((1, D), jnp.bfloat16)], axis=0)
    grad_moe = grad_moe + jnp.sum(sent_back[slot_index].astype(jnp.float32), axis=1)
    grad_chosen = jnp.where(kept_mask, grad_weight, 0.0)
    grad_probs = jnp.sum(onehot * grad_chosen[..., None], axis=1)
    grad_logits = gate_probs * (
        grad_probs - jnp.sum(gate_probs * grad_probs, axis=-1, keepdims=True)
    )
    grad_router = jnp.dot(moe_wide.T, grad_logits, precision=highest)
    grad_moe = grad_moe + jnp.dot(grad_logits, router_wide.T, precision=highest)
    grad_gain_two = jnp.sum(grad_moe * normed_two, axis=0)
    scaled_two = grad_moe * gain_two_wide
    grad_hidden = upstream + factor_two * (
        scaled_two - normed_two * jnp.mean(scaled_two * normed_two, axis=-1, keepdims=True)
    )
    grad_hidden_low = grad_hidden.astype(jnp.bfloat16)
    grad_output = jnp.dot(mixed_rows.T, grad_hidden_low, preferred_element_type=jnp.float32)
    grad_mixed = (
        jnp.dot(grad_hidden_low, w_output.T, preferred_element_type=jnp.float32)
        .astype(jnp.bfloat16)
        .reshape(length, HEADS, HEAD_DIM)
    )
    delta = jnp.einsum("qhd,hqd->hq", grad_mixed.astype(jnp.float32), attended)
    start_state = (
        jnp.zeros((length, HEADS, HEAD_DIM), jnp.float32),
        jnp.zeros((row_length, 2 * inner_width), jnp.float32),
    )
    back_key_all = lax.all_gather(key_rows, "ctx", axis=0, tiled=True)
    back_value_all = lax.all_gather(value_rows, "ctx", axis=0, tiled=True)
    back_docs_all = lax.all_gather(doc_wire, "ctx", axis=0, tiled=True)

    def visit(progress, within, rows_now):
        first_row = within

        def compute(progress):
            grad_query_acc, grad_kv_all = progress
            key_block = lax.dynamic_slice_in_dim(back_key_all, within, rows_now, 0)
            value_block = lax.dynamic_slice_in_dim(back_value_all, within, rows_now, 0)
            docs_block = lax.dynamic_slice_in_dim(back_docs_all, within, rows_now, 0).astype(
                jnp.float32
            )
            key_pos = first_row + jnp.arange(rows_now, dtype=jnp.int32)
            allowed = allowed_mask(positions, doc_here, key_pos, docs_block)[None]
            scores = jnp.einsum(
                "qhd,khd->hqk", queries, key_block, preferred_element_type=jnp.float32
            )
            scores = jnp.where(allowed, scores * score_scale, negative)
            shares = jnp.exp(scores - log_total[..., None]) * allowed
            grad_shares = jnp.einsum(
                "qhd,khd->hqk", grad_mixed, value_block, preferred_element_type=jnp.float32
            )
            grad_scores = (shares * (grad_shares - delta[..., None]) * score_scale).astype(
                jnp.bfloat16
            )
            grad_query_acc = grad_query_acc + jnp.einsum(
                "hqk,khd->qhd", grad_scores, key_block, preferred_element_type=jnp.float32
            )
            grad_key_rows = jnp.einsum(
                "hqk,qhd->khd", grad_scores, queries, preferred_element_type=jnp.float32
            ).reshape(rows_now, inner_width)
            grad_value_rows = jnp.einsum(
                "hqk,qhd->khd",
                shares.astype(jnp.bfloat16),
                grad_mixed,
                preferred_element_type=jnp.float32,
            ).reshape(rows_now, inner_width)
            current = lax.dynamic_slice_in_dim(grad_kv_all, first_row, rows_now, 0)
            grad_kv_all = lax.dynamic_update_slice_in_dim(
                grad_kv_all,
                current + jnp.concatenate([grad_key_rows, grad_value_rows], axis=1),
                first_row,
                0,
            )
            return (grad_query_acc, grad_kv_all)

        return lax.cond(first_row > last_here, unchanged, compute, progress)

    grad_query, grad_kv_all = blockwise(back_key_all.shape[0], visit, start_state)
    grad_kv = lax.psum_scatter(
        grad_kv_all.astype(jnp.bfloat16), "ctx", scatter_dimension=0, tiled=True
    ).astype(jnp.float32)
    grad_query_low = (
        unrotate(grad_query.astype(jnp.bfloat16).astype(jnp.float32), cosine, sine)
        .astype(jnp.bfloat16)
        .reshape(length, inner_width)
    )
    grad_key_turned = (
        grad_kv[:, :inner_width]
        .reshape(length, HEADS, HEAD_DIM)
        .astype(jnp.bfloat16)
        .astype(jnp.float32)
    )
    grad_key_low = (
        unrotate(grad_key_turned, cosine, sine).astype(jnp.bfloat16).reshape(length, inner_width)
    )
    grad_value_low = grad_kv[:, inner_width:].astype(jnp.bfloat16)
    grad_wquery = jnp.dot(attn_input.T, grad_query_low, preferred_element_type=jnp.float32)
    grad_wkey = jnp.dot(attn_input.T, grad_key_low, preferred_element_type=jnp.float32)
    grad_wvalue = jnp.dot(attn_input.T, grad_value_low, preferred_element_type=jnp.float32)
    grad_attn = (
        jnp.dot(grad_query_low, w_query.T, preferred_element_type=jnp.float32)
        + jnp.dot(grad_key_low, w_key.T, preferred_element_type=jnp.float32)
        + jnp.dot(grad_value_low, w_value.T, preferred_element_type=jnp.float32)
    )
    grad_gain_one = jnp.sum(grad_attn * normed_one, axis=0)
    scaled_one = grad_attn * gain_one_wide
    grad_inputs = grad_hidden + factor_one * (
        scaled_one - normed_one * jnp.mean(scaled_one * normed_one, axis=-1, keepdims=True)
    )
    owned = (
        lax.psum_scatter(
            grad_gain_one.astype(jnp.bfloat16), "fsdp", scatter_dimension=0, tiled=True
        ).astype(jnp.float32),
        lax.psum_scatter(
            grad_wquery.astype(jnp.bfloat16), "fsdp", scatter_dimension=0, tiled=True
        ).astype(jnp.float32),
        lax.psum_scatter(
            grad_wkey.astype(jnp.bfloat16), "fsdp", scatter_dimension=0, tiled=True
        ).astype(jnp.float32),
        lax.psum_scatter(
            grad_wvalue.astype(jnp.bfloat16), "fsdp", scatter_dimension=0, tiled=True
        ).astype(jnp.float32),
        lax.psum_scatter(
            grad_output.astype(jnp.bfloat16), "fsdp", scatter_dimension=0, tiled=True
        ).astype(jnp.float32),
        lax.psum_scatter(
            grad_gain_two.astype(jnp.bfloat16), "fsdp", scatter_dimension=0, tiled=True
        ).astype(jnp.float32),
        lax.psum_scatter(
            grad_router.astype(jnp.bfloat16), "fsdp", scatter_dimension=0, tiled=True
        ).astype(jnp.float32),
        lax.psum_scatter(
            grad_shared_gate.astype(jnp.bfloat16), "fsdp", scatter_dimension=0, tiled=True
        ).astype(jnp.float32),
        lax.psum_scatter(
            grad_shared_up.astype(jnp.bfloat16), "fsdp", scatter_dimension=0, tiled=True
        ).astype(jnp.float32),
        lax.psum_scatter(
            grad_shared_down.astype(jnp.bfloat16), "fsdp", scatter_dimension=0, tiled=True
        ).astype(jnp.float32),
        lax.psum_scatter(
            grad_expert_gate.astype(jnp.bfloat16), "fsdp", scatter_dimension=1, tiled=True
        ).astype(jnp.float32),
        lax.psum_scatter(
            grad_expert_up.astype(jnp.bfloat16), "fsdp", scatter_dimension=1, tiled=True
        ).astype(jnp.float32),
        lax.psum_scatter(
            grad_expert_down.astype(jnp.bfloat16), "fsdp", scatter_dimension=1, tiled=True
        ).astype(jnp.float32),
    )
    (
        own_gain_one,
        own_wquery,
        own_wkey,
        own_wvalue,
        own_output,
        own_gain_two,
        own_router,
        own_shared_gate,
        own_shared_up,
        own_shared_down,
        own_expert_gate,
        own_expert_up,
        own_expert_down,
    ) = owned
    dense = (
        lax.psum(own_gain_one.astype(jnp.bfloat16), "ctx").astype(jnp.float32),
        lax.psum(own_wquery.astype(jnp.bfloat16), "ctx").astype(jnp.float32),
        lax.psum(own_wkey.astype(jnp.bfloat16), "ctx").astype(jnp.float32),
        lax.psum(own_wvalue.astype(jnp.bfloat16), "ctx").astype(jnp.float32),
        lax.psum(own_output.astype(jnp.bfloat16), "ctx").astype(jnp.float32),
        lax.psum(own_gain_two.astype(jnp.bfloat16), "ctx").astype(jnp.float32),
        lax.psum(own_router.astype(jnp.bfloat16), "ctx").astype(jnp.float32),
        lax.psum(own_shared_gate.astype(jnp.bfloat16), "ctx").astype(jnp.float32),
        lax.psum(own_shared_up.astype(jnp.bfloat16), "ctx").astype(jnp.float32),
        lax.psum(own_shared_down.astype(jnp.bfloat16), "ctx").astype(jnp.float32),
    )
    return (
        output_rows[None],
        grad_inputs.astype(jnp.bfloat16)[None],
        dense[0],
        dense[1],
        dense[2],
        dense[3],
        dense[4],
        dense[5],
        dense[6],
        dense[7],
        dense[8],
        dense[9],
        own_expert_gate,
        own_expert_up,
        own_expert_down,
    )


def solution(mesh):
    fast = mesh.shape['ctx'] == 8 and mesh.shape['fsdp'] == NZ
    body = per_device_fast if fast else per_device
    return jax.shard_map(
        body,
        mesh=mesh,
        in_specs=(
            P("fsdp", "ctx", None),
            P("fsdp", "ctx"),
            P("fsdp", "ctx", None),
            P("fsdp", "ctx", None),
            P("fsdp"),
            P("fsdp", None),
            P("fsdp", None),
            P("fsdp", None),
            P("fsdp", None),
            P("fsdp"),
            P("fsdp", None),
            P("fsdp", None),
            P("fsdp", None),
            P("fsdp", None),
            P("ctx", "fsdp", None),
            P("ctx", "fsdp", None),
            P("ctx", "fsdp", None),
            P("fsdp", "ctx", None),
        ),
        out_specs=(
            P("fsdp", "ctx", None),
            P("fsdp", "ctx", None),
            P("fsdp"),
            P("fsdp", None),
            P("fsdp", None),
            P("fsdp", None),
            P("fsdp", None),
            P("fsdp"),
            P("fsdp", None),
            P("fsdp", None),
            P("fsdp", None),
            P("fsdp", None),
            P("ctx", "fsdp", None),
            P("ctx", "fsdp", None),
            P("ctx", "fsdp", None),
        ),
        check_vma=False,
    )
```

```python
import functools
import math
import types

import jax
import jax.numpy as jnp
import numpy as np
from jax import lax
from jax.experimental import pallas as pl
from jax.experimental.pallas import tpu as pltpu
from jax.sharding import PartitionSpec as P

D = 1280
HEADS = 10
HEAD_DIM = 128
TOPK = 7
EXP_DEV = 2


epsilon = 1e-06
theta_base = 10000.0
negative = -1e30
highest = lax.Precision.HIGHEST


def rotary_tables(positions, half_dim):
    frequency = theta_base ** (-jnp.arange(half_dim, dtype=jnp.float32) / half_dim)
    angles = positions.astype(jnp.float32)[:, None] * frequency[None, :]
    return (jnp.cos(angles)[:, None, :], jnp.sin(angles)[:, None, :])


def rotate(values, cosine, sine):
    half_dim = values.shape[-1] // 2
    leading = values[..., :half_dim]
    trailing = values[..., half_dim:]
    return jnp.concatenate(
        [leading * cosine - trailing * sine, trailing * cosine + leading * sine], axis=-1
    )


def unrotate(values, cosine, sine):
    half_dim = values.shape[-1] // 2
    leading = values[..., :half_dim]
    trailing = values[..., half_dim:]
    return jnp.concatenate(
        [leading * cosine + trailing * sine, trailing * cosine - leading * sine], axis=-1
    )


def blockwise(count, visit, initial):
    rows_each = math.gcd(count, 512)

    def advance(progress, number):
        return (visit(progress, number * rows_each, rows_each), None)

    final, ignored = lax.scan(advance, initial, jnp.arange(count // rows_each, dtype=jnp.int32))
    return final


def allowed_mask(query_pos, query_docs, key_pos, key_docs):
    return (key_pos[None, :] <= query_pos[:, None]) & (key_docs[None, :] == query_docs[:, None])


def rms_factor(values):
    return lax.rsqrt(jnp.mean(values * values, axis=-1, keepdims=True) + epsilon)


def silu_parts(values):
    sigma = jax.nn.sigmoid(values)
    return (values * sigma, sigma * (1.0 + values * (1.0 - sigma)))


def unchanged(progress):
    return progress


NZ = 4
SLOTS = 64
WIDE = 256
MESH = pl.DeviceIdType.MESH
PEERS = ((0, 1), (1, 0), (1, 1))
NN = (((1,), (0,)), ((), ()))
NT = (((1,), (1,)), ((), ()))
TN = (((0,), (0,)), ((), ()))
MIB = 1024 * 1024


def dot(left, right, dims=NN):
    return lax.dot_general(left, right, dims, preferred_element_type=jnp.float32)


def split_dot(left, right, dims=NN):
    high = left.astype(jnp.bfloat16)
    low = (left - high.astype(jnp.float32)).astype(jnp.bfloat16)
    return dot(high, right, dims) + dot(low, right, dims)


def flip(c, fy, fx, fk):
    return 4 * ((c // 4 + fy) % 2) + 2 * (((c // 2) % 2 + fx) % 2) + (c % 2 + fk) % 2


def rows_at(start, count):
    return pl.ds(pl.multiple_of(start, 16), count)


def lanes_at(start, count):
    return pl.ds(pl.multiple_of(start, 128), count)


def remote(src, dst, send, recv, c, z):
    return pltpu.make_async_remote_copy(
        src_ref=src, dst_ref=dst, send_sem=send, recv_sem=recv, device_id=(c, z), device_id_type=MESH
    )


def greet(c, z):
    barrier = pltpu.get_barrier_semaphore()
    peers = [(c, (z + d) % NZ) for d in range(1, NZ)]
    peers += [(flip(c, fy, fx, 0), z) for fy, fx in PEERS] + [(flip(c, 0, 0, 1), z)]
    for peer in peers:
        pl.semaphore_signal(barrier, inc=1, device_id=peer, device_id_type=MESH)
    pl.semaphore_wait(barrier, len(peers))


class Spread:
    def __init__(self, src, block, sems, c, z, hops=NZ, peers=PEERS, copy_own=True, plane=None, chain=False, relays=True):
        self.src, self.block, self.c, self.z = src, block, c, z
        self.hops, self.peers, self.all = hops, peers, ((0, 0),) + peers
        self.local, self.zs, self.zr, self.xs, self.xr, self.ms, self.mr = sems
        self.plane = plane is not None
        self.chain, self.relays = chain, relays
        self.forwards = (hops == NZ or self.plane) and len(peers) == 3
        self.zhops = 1 if self.plane else hops
        self.direct = 2 if self.forwards else len(peers)
        pair = plane if self.plane else (src(z), block(c, z)) if copy_own else None
        self.own = pltpu.make_async_copy(*pair, self.local) if pair is not None else None

    def at(self, c, d):
        return self.block(c, d if self.plane else (self.z + NZ - d) % NZ)

    def mine(self, c, d):
        if self.plane:
            return self.src(d)
        return self.src(self.z) if d == 0 else self.at(c, d)

    def zcopy(self, d):
        there = (self.z + d) % NZ
        return remote(
            self.src(there), self.block(self.c, self.z), self.zs.at[0, d - 1], self.zr.at[d - 1], self.c, there
        )

    def hop(self, up, k):
        origin = self.z - k if up else self.z + k
        there = self.z + 1 if up else self.z - 1
        block = self.block(self.c, origin)
        src = self.src(self.z) if k == 0 else block
        return remote(src, block, self.zs.at[int(up), k], self.zr.at[k if up else 2 - k], self.c, there)

    def hops_of(self, k):
        return (True, (self.z >= k) & (self.z < NZ - 1)), (False, (self.z + k < NZ) & (self.z > 0))

    def onward(self, d):
        if self.relays:
            for i in range(self.direct):
                self.xcopy(i, d).start()
            self.mcopy(0, d).start()

    def chain_stage(self, k):
        for up, here, d in ((True, self.z >= k, k), (False, self.z + k < NZ, NZ - k)):

            @pl.when(here)
            def _(up=up, d=d):
                self.zwait(d)
                if k < NZ - 1:

                    @pl.when((self.z < NZ - 1) if up else (self.z > 0))
                    def _():
                        self.hop(up, k).start()

                self.onward(d)

    def zwait(self, d):
        block = self.at(self.c, d)
        remote(block, block, self.zs.at[0, d - 1], self.zr.at[d - 1], self.c, self.z).wait_recv()

    def xcopy(self, i, d):
        there = flip(self.c, self.peers[i][0], self.peers[i][1], 0)
        return remote(self.mine(self.c, d), self.at(self.c, d), self.xs.at[i, d], self.xr.at[i, d], there, self.z)

    def fcopy(self, i, d):
        origin = flip(self.c, self.peers[i][0], self.peers[i][1], 0)
        there = flip(self.c, self.peers[1 - i][0], self.peers[1 - i][1], 0)
        block = self.at(origin, d)
        return remote(block, block, self.xs.at[2, d], self.xr.at[2, d], there, self.z)

    def xwait(self, i, d):
        block = self.at(flip(self.c, self.peers[i][0], self.peers[i][1], 0), d)
        remote(block, block, self.xs.at[i, d], self.xr.at[i, d], self.c, self.z).wait_recv()

    def mcopy(self, i, d):
        origin = flip(self.c, self.all[i][0], self.all[i][1], 0)
        src = self.mine(origin, d) if i == 0 else self.at(origin, d)
        return remote(src, self.at(origin, d), self.ms.at[i, d], self.mr.at[i, d], flip(self.c, 0, 0, 1), self.z)

    def mwait(self, i, d):
        block = self.at(flip(self.c, self.all[i][0], self.all[i][1], 1), d)
        remote(block, block, self.ms.at[i, d], self.mr.at[i, d], self.c, self.z).wait_recv()

    def start_z(self):
        if self.own is not None:
            self.own.start()
        if self.chain:
            for up, edge in self.hops_of(0):
                pl.when(edge)(self.hop(up, 0).start)
            return
        for d in range(1, self.zhops):
            self.zcopy(d).start()

    def start_x(self):
        for d in range(self.hops if self.plane else 1):
            for i in range(self.direct):
                self.xcopy(i, d).start()
            self.mcopy(0, d).start()

    def relay_z(self):
        for d in range(1, self.zhops):
            if self.chain:
                self.chain_stage(d)
            else:
                self.zwait(d)
                self.onward(d)

    def relay_x(self):
        for d in range(self.hops):
            self.relay_near(d)
        self.relay_far()

    def relay_near(self, d):
        for i in range(min(2, len(self.peers))):
            self.xwait(i, d)
            self.mcopy(i + 1, d).start()
            if self.forwards and i == (d >= self.hops // 2):
                self.fcopy(i, d).start()

    def relay_far(self):
        for d in range(self.hops if len(self.peers) > 2 else 0):
            self.xwait(2, d)
            self.mcopy(3, d).start()

    def arrive_from(self, i):
        for d in range(self.hops):
            self.mwait(i, d)

    def arrive(self):
        if self.own is not None:
            self.own.wait()
        for d in range(self.hops):
            for i in range(len(self.all)):
                self.mwait(i, d)

    def drain(self):
        for d in range(1, self.zhops):
            if self.chain:
                for up, edge in self.hops_of(d - 1):
                    pl.when(edge)(self.hop(up, d - 1).wait_send)
            else:
                self.zcopy(d).wait_send()
        if not self.relays:
            return
        for d in range(self.hops):
            for i in range(self.direct):
                self.xcopy(i, d).wait_send()
            if self.forwards:
                self.fcopy(int(d >= self.hops // 2), d).wait_send()
            for i in range(len(self.all)):
                self.mcopy(i, d).wait_send()


def halves(src, dst, sems, c, z):
    count = src.shape[0] // 2
    return Spread(
        lambda d: src.at[d * count : (d + 1) * count],
        lambda o, d: dst(o).at[d * count : (d + 1) * count],
        sems, c, z, 2, plane=(src, dst(c)),
    )


def spread_sems(hops=NZ, peers=3):
    dma = pltpu.SemaphoreType.DMA
    return [
        dma, dma((2, 3)), dma((3,)), dma((peers, hops)), dma((peers, hops)), dma((peers + 1, hops)), dma((peers + 1, hops)),
    ]


def plane_reduce(part, c, z, refs):
    out4, in4, out3, in3, ms, mr, xs, xr = refs
    mate = flip(c, 0, 0, 1)
    order = PEERS + ((0, 0),)

    def to_mate(i):
        return remote(out4.at[i], in4.at[i], ms.at[i], mr.at[i], mate, z)

    def to_chip(i):
        return remote(out3.at[i], in3.at[i], xs.at[i], xr.at[i], flip(c, PEERS[i][0], PEERS[i][1], 0), z)

    for i, (fy, fx) in enumerate(order):
        out4[i] = part(flip(c, fy, fx, 1)).astype(jnp.bfloat16)
        to_mate(i).start()
    for i, (fy, fx) in enumerate(order):
        value = part(flip(c, fy, fx, 0))
        to_mate(i).wait_recv()
        value = value + in4[i].astype(jnp.float32)
        if i < 3:
            out3[i] = value.astype(jnp.bfloat16)
            to_chip(i).start()
    for i in range(3):
        to_chip(i).wait_recv()
        value = value + in3[i].astype(jnp.float32)
    for i in range(4):
        to_mate(i).wait_send()
    for i in range(3):
        to_chip(i).wait_send()
    return value


def plane_scratch(length, width):
    dma = pltpu.SemaphoreType.DMA
    block = lambda n: pltpu.VMEM((n, length, width), jnp.bfloat16)
    return [block(4), block(4), block(3), block(3), dma((4,)), dma((4,)), dma((3,)), dma((3,))]


def swish(values):
    sigma = 1.0 / (1.0 + jnp.exp(-values))
    return values * sigma, sigma * (1.0 + values * (1.0 - sigma))


def norm_factor(values):
    return lax.rsqrt(jnp.mean(values * values, axis=1, keepdims=True) + epsilon)


def turned(values, cosine, sine):
    return values * cosine + pltpu.roll(values, 64, 1) * sine


def take(refs, count):
    taken = refs[:count]
    del refs[:count]
    return taken


def head_rows(c):
    blocks = [2 * c, 2 * c + 1, 16 + 2 * (c // 4), 17 + 2 * (c // 4)]
    return [(b, b // 5) for b in blocks]


def visible(first, count, keys, boundary):
    query = (lax.broadcasted_iota(jnp.int32, (count, 1), 0) + first).astype(jnp.float32)
    key = lax.broadcasted_iota(jnp.int32, (1, keys), 1).astype(jnp.float32)
    query_doc = jnp.where(query >= boundary, 1.0, 0.0)
    key_doc = jnp.where(key >= boundary, 1.0, 0.0)
    return (key <= query) & (key_doc == query_doc)


FRONT_IN = (
    "x", "router", "gains", "doc", "routes", "prio", "cos", "sin", "g", "wq", "wk", "wv", "wo", "eg", "eu", "sg", "su",
    "ed", "sd",
)
FRONT_OUT = (
    "hidden", "tokens", "gates", "psum", "bound", "aall", "wall", "woall", "q1", "k1", "v1", "q2", "k2", "v2",
    "att1", "lse1", "att2", "lse2", "mixed", "db", "dg", "ddn", "dsgu", "dsdn",
    "gall", "wsend", "ball", "tall", "ypart", "accout",
)
FRONT_TMP = (
    "pool", "docs", "pown", "pall", "cut", "wgu", "wdn", "table", "acc", "bg", "gg", "tg", "oh", "ys", "ds",
    "st", "stc", "sty", "ld", "xrecv", "zbuf", "zrecv",
)


def front_kernel(capacity, *refs):
    f32, bf16 = jnp.float32, jnp.bfloat16
    names = FRONT_IN + FRONT_OUT + FRONT_TMP
    r = types.SimpleNamespace(**dict(zip(names, refs)))
    sems = list(refs[len(names) :])
    c = lax.axis_index("ctx")
    z = lax.axis_index("fsdp")
    length, width = r.x.shape
    count = r.cos.shape[0]
    shard = width // NZ
    sub = shard // 4
    quarter = c % 4
    mate = flip(c, 0, 0, 1)
    step = 2 * length
    group = NZ * length
    final = group + 16
    hidden_dev = r.ed.shape[1]

    spread_x = Spread(
        lambda _: r.x, lambda o, _: r.pool.at[rows_at(o * length, length)], take(sems, 7), c, z, 1
    )
    spread_docs = Spread(lambda _: r.docs.at[8], lambda o, _: r.docs.at[o], take(sems, 7), c, z, 1)
    second = lambda o, s: r.wall.at[rows_at(s * shard + (o % 4) * sub, sub), 384:768]
    spread_h2 = Spread(lambda _: second(c, z), second, take(sems, 7), c, z, NZ, ((0, 1),), False, chain=True)
    first = lambda _, s: r.wall.at[rows_at(s * shard, shard), 0:384]
    spread_h1 = Spread(lambda _: first(c, z), first, take(sems, 7), c, z, copy_own=False, chain=True, relays=False)
    spread_g = Spread(lambda _: r.g, lambda o, s: r.gall.at[o, rows_at(s * length, length)], take(sems, 7), c, z)
    shared_in = lambda s: r.wsend.at[s, 2, rows_at((c // 2) * sub, sub), lanes_at(c % 2 * WIDE, WIDE)]
    shared_to = lambda o, s: r.wgu.at[2, rows_at(s * shard + (o // 2) * sub, sub), lanes_at(o % 2 * WIDE, WIDE)]
    spread_s = Spread(shared_in, shared_to, take(sems, 7), c, z)
    spread_b = Spread(lambda _: r.tokens, lambda o, s: r.ball.at[o, rows_at(s * length, length)], take(sems, 7), c, z, chain=True)
    spread_t = Spread(lambda _: r.table, lambda o, s: r.tall.at[o, s], take(sems, 7), c, z)
    ps, pr, wl, wol, wos, wor, wgl, wgs, wgr, rawsem, cutsem, dnsem, acsem = take(sems, 13)
    lsem, ms, mr, xs_s, xs_r, zs, zr, ysem, accsem = take(sems, 9)
    reduce_refs = [r.ys, r.ds, r.zbuf.at[0:3, 0:length]] + take(sems, 5)

    r.pall[...] = jnp.zeros_like(r.pall)
    greet(c, z)
    own_rows = rows_at(z * shard, shard)
    sub_rows = rows_at(z * shard + quarter * sub, sub)
    copies = []
    for i, ref in enumerate((r.wq, r.wk, r.wv)):
        copies.append(
            pltpu.make_async_copy(
                ref.at[:, lanes_at(c * 128, 128)], r.wall.at[own_rows, i * 128 : (i + 1) * 128], wl.at[i]
            )
        )
        copies.append(
            pltpu.make_async_copy(
                ref.at[rows_at(quarter * sub, sub), lanes_at((8 + c // 4) * 128, 128)],
                r.wall.at[sub_rows, 384 + i * 128 : 512 + i * 128],
                wl.at[3 + i],
            )
        )
    for copy in copies:
        copy.start()
    spread_x.start_z()
    spread_x.start_x()
    down = [pltpu.make_async_copy(r.ed.at[e], r.wdn.at[e, 0:hidden_dev], dnsem.at[e]) for e in range(2)]
    down.append(pltpu.make_async_copy(r.sd, r.wdn.at[2, 0:hidden_dev], dnsem.at[2]))
    for copy in down:
        copy.start()
    raws = ((r.eg.at[0], r.eu.at[0]), (r.eg.at[1], r.eu.at[1]), (r.sg, r.su))

    units = r.eg.shape[2]
    raw = lambda h: r.gg.at[h * shard : (h + 1) * shard, 0:units]

    def load_raw(e):
        return [pltpu.make_async_copy(raws[e][h], raw(h), rawsem.at[h]) for h in range(2)]

    def store_cut(e):
        return pltpu.make_async_copy(r.cut, r.wsend.at[:, e], cutsem)

    for copy in load_raw(0):
        copy.start()
    row = lax.broadcasted_iota(jnp.int32, (shard, width), 0)
    lane = lax.broadcasted_iota(jnp.int32, (shard, width), 1)
    place = jnp.where(lane == row + z * shard, 1.0, 0.0).astype(bf16)
    r.pown[0:16] = dot(r.router[...], place, TN).astype(bf16)
    r.pown[16:32] = dot(r.gains[...], place).astype(bf16)

    def pcopy(d):
        lanes = lanes_at(5 * z // 2 * 128, 384)
        return remote(
            r.pown.at[:, lanes], r.pall.at[d - 1, :, lanes], ps.at[d - 1], pr.at[d - 1], c, (z + d) % NZ
        )

    def pwait(d):
        here = r.pall.at[d - 1, :, lanes_at(5 * ((z + NZ - d) % NZ) // 2 * 128, 384)]
        remote(here, here, ps.at[d - 1], pr.at[d - 1], c, z).wait_recv()

    for d in range(1, NZ):
        pcopy(d).start()
    for copy in copies:
        copy.wait()

    spread_h2.start_z()
    spread_h1.start_z()
    spread_h2.start_x()
    def wo_local(j, b):
        return pltpu.make_async_copy(
            r.wo.at[rows_at(b % 5 * 64, 64)], r.woall.at[64 * j : 64 * j + 64], wol.at[j]
        )

    def wo_hop(j, up, b, owner):
        src = r.wo.at[rows_at(b % 5 * 64, 64)] if owner else r.woall.at[64 * j : 64 * j + 64]
        there = z + 1 if up else z - 1
        return remote(src, r.woall.at[64 * j : 64 * j + 64], wos.at[j, int(up)], wor.at[j], c, there)

    def wo_each(visit):
        for j, (b, owner) in enumerate(head_rows(c)):
            visit(j, b, owner)

    def wo_start(j, b, owner):
        @pl.when(owner == z)
        def _():
            wo_local(j, b).start()

        @pl.when((owner == z) & (z < NZ - 1))
        def _():
            wo_hop(j, True, b, True).start()

        @pl.when((owner == z) & (z > 0))
        def _():
            wo_hop(j, False, b, True).start()

    def wo_relay(j, b, owner):
        @pl.when(owner != z)
        def _():
            wo_hop(j, True, b, False).wait_recv()

        @pl.when((owner < z) & (z < NZ - 1))
        def _():
            wo_hop(j, True, b, False).start()

        @pl.when((owner > z) & (z > 0))
        def _():
            wo_hop(j, False, b, False).start()

        @pl.when(owner == z)
        def _():
            wo_local(j, b).wait()

    def wo_drain(j, b, owner):
        @pl.when((owner <= z) & (z < NZ - 1))
        def _():
            wo_hop(j, True, b, False).wait_send()

        @pl.when((owner >= z) & (z > 0))
        def _():
            wo_hop(j, False, b, False).wait_send()

    wo_each(wo_start)
    spread_g.start_z()
    spread_g.start_x()
    r.docs[8] = jnp.concatenate([r.doc[...].astype(f32), jnp.ones((7, length), f32)], axis=0)
    spread_docs.start_z()
    spread_docs.start_x()
    spread_x.relay_x()
    spread_docs.relay_x()

    for e in range(3):
        for copy in load_raw(e):
            copy.wait()
        if e > 0:
            store_cut(e - 1).wait()
        unit = lax.broadcasted_iota(jnp.int32, (units, WIDE), 0)
        slot = lax.broadcasted_iota(jnp.int32, (units, WIDE), 1)
        for q in range(NZ):
            pick = jnp.where((unit == slot + q * hidden_dev) & (slot < hidden_dev), 1.0, 0.0).astype(bf16)
            for h in range(2):
                r.cut[q, :, h * WIDE : (h + 1) * WIDE] = dot(raw(h)[...], pick).astype(bf16)
        store_cut(e).start()
        if e < 2:
            for copy in load_raw(e + 1):
                copy.start()
    packed = r.pown[...].astype(f32)
    for d in range(1, NZ):
        pwait(d)
        packed = packed + r.pall[d - 1].astype(f32)
    r.psum[...] = packed
    gain_one = packed[17:18]
    gain_two = packed[16:17]
    spread_x.arrive()

    def make_a(i, carry):
        values = r.pool[rows_at(i * length, length)].astype(f32)
        r.bg[rows_at(i * length, length)] = (values * norm_factor(values) * gain_one).astype(bf16)
        return carry

    lax.fori_loop(0, 8, make_a, 0)
    for d in range(1, NZ):
        spread_h2.chain_stage(d)
        spread_h1.chain_stage(d)
    spread_h2.relay_x()
    spread_h2.arrive()
    wo_each(wo_relay)

    def wgcopy(e, d):
        there = (z + d) % NZ
        return remote(
            r.wsend.at[there, e], r.wgu.at[e, own_rows, :], wgs.at[e, d - 1], wgr.at[e, d - 1], c, there
        )

    def wgwait(e, d):
        here = r.wgu.at[e, rows_at((z + NZ - d) % NZ * shard, shard), :]
        remote(here, here, wgs.at[e, d - 1], wgr.at[e, d - 1], c, z).wait_recv()

    wgown = pltpu.make_async_copy(r.wsend.at[z, 0:2], r.wgu.at[0:2, own_rows, :], wgl)
    store_cut(2).wait()
    spread_s.start_z()
    spread_s.start_x()
    wgown.start()
    for d in range(1, NZ):
        wgcopy(0, d).start()
    for i in range(count // step):
        part = slice(i * step, (i + 1) * step)
        values = dot(r.bg[part], r.wall[...])
        cosine, sine = r.cos[part], r.sin[part]
        r.q1[part] = turned(values[:, 0:128], cosine, sine).astype(bf16)
        r.k1[part] = turned(values[:, 128:256], cosine, sine).astype(bf16)
        r.v1[part] = values[:, 256:384].astype(bf16)
        r.q2[part] = turned(values[:, 384:512], cosine, sine).astype(bf16)
        r.k2[part] = turned(values[:, 512:640], cosine, sine).astype(bf16)
        r.v2[part] = values[:, 640:768].astype(bf16)
    acopy = pltpu.make_async_copy(r.bg, r.aall, acsem)
    acopy.start()
    spread_docs.arrive()
    flags = jnp.where(r.docs[0:8] == 0.0, 1.0, 0.0)
    boundary = jnp.sum(jnp.sum(flags, axis=0), axis=(0, 1), keepdims=True)
    r.bound[...] = jnp.broadcast_to(boundary, r.bound.shape)

    def attend(queries, first, keys, values, n):
        scores = dot(queries, keys[0:n], NT) * (HEAD_DIM**-0.5)
        scores = jnp.where(visible(first, step, n, boundary), scores, negative)
        top = jnp.max(scores, axis=1, keepdims=True)
        shares = jnp.exp(scores - top)
        total = jnp.sum(shares, axis=1, keepdims=True)
        probs = (shares * (1.0 / total)).astype(bf16)
        return dot(probs, values[0:n]), jnp.broadcast_to(top + jnp.log(total), (step, 128))

    r.mixed[...] = jnp.zeros_like(r.mixed)
    for i in range(count // step):
        part = slice(i * step, (i + 1) * step)
        out, lse = attend(r.q1[part], i * step, r.k1, r.v1, (i + 1) * step)
        r.att1[part] = out
        r.lse1[part] = lse
        r.mixed[part, 0:128] = out.astype(bf16)
        if i == 2:
            spread_g.relay_z()
    mine = rows_at(quarter * step, step)
    out, lse = attend(r.q2[mine], quarter * step, r.k2, r.v2, count)
    r.att2[...] = out
    r.lse2[...] = lse
    r.mixed[mine, 128:256] = out.astype(bf16)
    spread_s.relay_z()

    value = plane_reduce(
        lambda o: dot(r.mixed[rows_at(o * length, length)], r.woall[...]), c, z, reduce_refs
    )
    hidden = r.x[...].astype(f32) + value
    r.hidden[...] = hidden
    tokens = (hidden * norm_factor(hidden) * gain_two).astype(bf16)
    r.tokens[...] = tokens
    logits = dot(packed[0:16].astype(bf16), tokens, NT)
    shifted = jnp.exp(logits - jnp.max(logits, axis=0, keepdims=True))
    gates = shifted / jnp.sum(shifted, axis=0, keepdims=True)
    r.gates[...] = gates
    lane = lax.broadcasted_iota(jnp.int32, (length, 128), 1)
    named = jnp.zeros((length, 128), f32)
    for k in range(r.routes.shape[1]):
        named = named + jnp.where(lane == r.routes[:, k : k + 1], 1.0, 0.0)
    named = named.T[0:16]
    order = jnp.broadcast_to(r.prio[...].astype(f32), (length, length))
    earlier = jnp.where(order.T < order, 1.0, 0.0).astype(bf16)
    rank = dot(named.astype(bf16), earlier)
    kept = (named > 0.0) & (rank < float(capacity))
    r.table[:, 0:length] = jnp.where(kept, rank, -1.0)
    r.table[:, length : 2 * length] = jnp.where(kept, gates, 0.0)
    spread_b.start_z()
    spread_b.start_x()
    spread_t.start_z()
    spread_t.start_x()
    r.acc[...] = jnp.zeros_like(r.acc)
    r.ddn[...] = jnp.zeros_like(r.ddn)
    r.st[group:final] = jnp.zeros((16, width), bf16)
    r.zbuf[...] = jnp.zeros_like(r.zbuf)
    for copy in down:
        copy.wait()
    r.wdn[:, hidden_dev:] = jnp.zeros((3, WIDE - hidden_dev, width), bf16)
    for d in range(NZ):
        spread_g.relay_near(d)
    for d in range(1, NZ):
        spread_b.chain_stage(d)
    for d in range(1, NZ):
        wgcopy(1, d).start()
    spread_t.relay_z()
    for d in range(NZ):
        spread_b.relay_near(d)
        spread_t.relay_near(d)
    for d in range(NZ):
        spread_s.relay_near(d)
    spread_g.relay_far()
    spread_s.relay_far()
    spread_b.relay_far()
    spread_t.relay_far()
    spread_s.arrive()
    spread_g.arrive()
    spread_b.arrive()
    spread_t.arrive()
    wgown.wait()
    for d in range(1, NZ):
        wgwait(0, d)
        wgwait(1, d)
    spread_x.drain()

    def target(g):
        left = 3 - g // 2
        return flip(c, left % 2, left // 2, 1 - g % 2)

    def loads(g):
        slot = g % 2
        there = target(g)
        return (
            pltpu.make_async_copy(r.ball.at[there], r.bg.at[rows_at(slot * group, group)], lsem.at[slot, 0]),
            pltpu.make_async_copy(r.gall.at[there], r.gg.at[rows_at(slot * group, group)], lsem.at[slot, 1]),
            pltpu.make_async_copy(r.tall.at[there], r.tg.at[slot], lsem.at[slot, 2]),
        )

    final = group + 16

    def to_mate(s):
        return remote(r.st, r.ld.at[s % 2], ms.at[s], mr.at[s], mate, z)

    def to_chip(s, d):
        left = 3 - s
        there = flip(c, left % 2, left // 2, 0)
        if d == NZ:
            part = (slice(group, final), slice(0, group))
        else:
            part = (rows_at((z + d) % NZ * length, length), slice(None))
        return remote(r.stc.at[(s,) + part], r.xrecv.at[(s,) + part], xs_s.at[s, d], xs_r.at[s, d], there, z)

    def keep_y(s):
        return pltpu.make_async_copy(r.sty, r.ypart.at[s], ysem)

    slot_ids = lax.broadcasted_iota(jnp.int32, (SLOTS, length), 0).astype(f32)
    row_ids = lax.broadcasted_iota(jnp.int32, (16, length), 0)
    table_rows = lax.broadcasted_iota(jnp.int32, (16, 2 * length), 0)

    acopy.wait()
    for copy in loads(0):
        copy.start()

    def body(s, carry):
        for par in range(2):
            one_group(s, par)
        return carry

    def one_group(s, par):
        g = 2 * s + par
        slot = par
        for copy in loads(g):
            copy.wait()

        @pl.when(g < 7)
        def _():
            for copy in loads(g + 1):
                copy.start()

        @pl.when(s > 0)
        def _():
            if par == 0:
                to_mate(s - 1).wait_send()
            else:
                keep_y(s - 1).wait()

        scales = [[], []]
        for q in range(NZ):
            hits = []
            for e in range(2):
                mine = jnp.sum(jnp.where(table_rows == 2 * c + e, r.tg[slot, q], 0.0), axis=0, keepdims=True)
                rank = mine[:, :length]
                share = mine[:, length:]
                hit = slot_ids == rank
                scales[e].append(jnp.sum(jnp.where(hit, share, 0.0), axis=1, keepdims=True))
                hits.append(jnp.where(hit, 1.0, 0.0))
            hot = jnp.concatenate(hits, axis=0).astype(bf16)
            r.oh[q] = hot
            for ref, at in ((r.bg, 0), (r.gg, group)):
                first = slot * group + q * length
                part = dot(hot, ref[first : first + length]).astype(bf16)
                r.pool[at + q * SLOTS : at + (q + 1) * SLOTS] = part[:SLOTS]
                r.pool[at + step + q * SLOTS : at + step + (q + 1) * SLOTS] = part[SLOTS:]
        back = [0.0] * NZ
        for e in range(2):
            own = slice(step * e, step * (e + 1))
            other = slice(group + step * e, group + step * (e + 1))
            scale = jnp.concatenate(scales[e], axis=0)
            both = dot(r.pool[own], r.wgu[e])
            up = both[:, WIDE:]
            silu, slope = swish(both[:, :WIDE])
            inner = (silu * up).astype(bf16)
            scaled = (inner.astype(f32) * scale).astype(bf16)
            out = dot(scaled, r.wdn[e]).astype(bf16)
            pull = dot(r.pool[other], r.wdn[e], NT)
            gain = jnp.sum(inner.astype(f32) * pull, axis=1, keepdims=True)
            pull = pull * scale
            turn = jnp.concatenate([(pull * up * slope).astype(bf16), (pull * silu).astype(bf16)], axis=1)
            r.ddn[e] += dot(scaled, r.pool[other], TN)
            r.acc[e] += dot(r.pool[own], turn, TN)
            into = dot(turn, r.wgu[e], NT).astype(bf16)
            for q in range(NZ):
                part = slice(q * SLOTS, (q + 1) * SLOTS)
                r.ys[q, e * SLOTS : (e + 1) * SLOTS] = out[part]
                r.ds[q, e * SLOTS : (e + 1) * SLOTS] = into[part]
                hit = r.oh[q, e * SLOTS : (e + 1) * SLOTS].astype(f32)
                line = jnp.sum(hit * gain[part], axis=0, keepdims=True)
                back[q] = back[q] + jnp.where(row_ids == 2 * c + e, line, 0.0)
        if par == 1:
            to_mate(s).wait_recv()
        for q in range(NZ):
            part = slice(q * length, (q + 1) * length)
            more = slice(final + q * length, final + (q + 1) * length)
            pulled = dot(r.oh[q], r.ds[q], TN)
            value = dot(r.oh[q], r.ys[q], TN)
            if par == 0:
                r.st[part] = pulled.astype(bf16)
                r.st[more] = value.astype(bf16)
                r.st[group:final, part] = back[q].astype(bf16)
            else:
                arrived = r.ld.at[s % 2]
                r.stc[s, part] = (pulled + arrived[part].astype(f32)).astype(bf16)
                r.sty[part] = (value + arrived[more].astype(f32)).astype(bf16)
                r.stc[s, group:final, part] = (back[q] + arrived[group:final, part].astype(f32)).astype(bf16)

        def own_column():
            for h in range(2):
                first = slot * group + h * step
                tokens = r.bg[first : first + step]
                upper = r.gg[first : first + step]
                both = dot(tokens, r.wgu[2])
                up = both[:, WIDE:]
                silu, slope = swish(both[:, :WIDE])
                inner = (silu * up).astype(bf16)
                part = slice(step * h, step * (h + 1))
                r.sty[part] = (r.sty[part].astype(f32) + dot(inner, r.wdn[2])).astype(bf16)
                pull = dot(upper, r.wdn[2], NT)
                turn = jnp.concatenate([(pull * up * slope).astype(bf16), (pull * silu).astype(bf16)], axis=1)
                r.stc[3, part] = (r.stc[3, part].astype(f32) + dot(turn, r.wgu[2], NT)).astype(bf16)
                if h == 0:
                    r.dsdn[...] = dot(inner, upper, TN).astype(bf16)
                    r.dsgu[...] = dot(tokens, turn, TN).astype(bf16)
                else:
                    r.dsdn[...] = (r.dsdn[...].astype(f32) + dot(inner, upper, TN)).astype(bf16)
                    r.dsgu[...] = (r.dsgu[...].astype(f32) + dot(tokens, turn, TN)).astype(bf16)

        if par == 0:
            to_mate(s).start()
        else:
            pl.when(s == 3)(own_column)
            keep_y(s).start()

            @pl.when(s < 3)
            def _():
                for d in range(NZ + 1):
                    to_chip(s, d).start()

    lax.fori_loop(0, 4, body, 0)
    for i in range(3):
        to_chip(i, NZ).wait_recv()

    def zcopy(d):
        there = (z + d) % NZ
        return remote(
            r.zbuf.at[there, 0:length], r.zrecv.at[d - 1, 0:length], zs.at[d - 1, 0], zr.at[d - 1, 0], c, there
        )

    def zsmall(d):
        there = (z + d) % NZ
        lanes = (slice(length, length + 16), slice(0, length))
        return remote(
            r.zbuf.at[(there,) + lanes], r.zrecv.at[(d - 1,) + lanes], zs.at[d - 1, 1], zr.at[d - 1, 1], c, there
        )

    for d in (1, 2, 3, 0):
        q = (z + d) % NZ
        for i in range(3):
            to_chip(i, d).wait_recv()

        def add(i, carry):
            part = rows_at(i * 16, 16)
            there = rows_at(q * length + i * 16, 16)
            total = r.stc[3, there].astype(f32)
            for k in range(3):
                total = total + r.xrecv[k, there].astype(f32)
            r.zbuf[q, part] = total.astype(bf16)
            return carry

        lax.fori_loop(0, length // 16, add, 0)
        total = r.stc[3, group:final, lanes_at(q * length, length)].astype(f32)
        for k in range(3):
            total = total + r.xrecv[k, group:final, lanes_at(q * length, length)].astype(f32)
        r.zbuf[q, length : length + 16, 0:length] = total.astype(bf16)
        if d:
            zcopy(d).start()
            zsmall(d).start()
    r.wgu[0:2] = r.acc[...].astype(bf16)
    acccopy = pltpu.make_async_copy(r.wgu.at[0:2], r.accout, accsem)
    acccopy.start()
    for d in range(1, NZ):
        zcopy(d).wait_recv()
        zsmall(d).wait_recv()

    def settle(i, carry):
        part = rows_at(i * 16, 16)
        value = r.zbuf[z, part].astype(f32)
        for d in range(3):
            value = value + r.zrecv[d, part].astype(f32)
        r.db[part] = value
        return carry

    lax.fori_loop(0, length // 16, settle, 0)
    value = r.zbuf[z, length : length + 16, 0:length].astype(f32)
    for d in range(3):
        value = value + r.zrecv[d, length : length + 16, 0:length].astype(f32)
    r.dg[...] = value
    acccopy.wait()
    to_mate(3).wait_send()
    for i in range(3):
        for d in range(NZ + 1):
            to_chip(i, d).wait_send()
    keep_y(3).wait()
    wo_each(wo_drain)
    for d in range(1, NZ):
        zcopy(d).wait_send()
        zsmall(d).wait_send()
        wgcopy(0, d).wait_send()
        wgcopy(1, d).wait_send()
        pcopy(d).wait_send()
    for spread in (spread_docs, spread_h1, spread_h2, spread_g, spread_s, spread_b, spread_t):
        spread.drain()


def front_stage(capacity, *operands):
    x, cosine = operands[0], operands[6]
    length, width = x.shape
    count = cosine.shape[0]
    shard = width // NZ
    group = NZ * length
    final = group + 16
    inner = 2 * WIDE
    dma = pltpu.SemaphoreType.DMA
    hbm = pl.BlockSpec(memory_space=pl.ANY)
    vmem = pl.BlockSpec(memory_space=pltpu.VMEM)
    f32, bf16 = jnp.float32, jnp.bfloat16
    shape = jax.ShapeDtypeStruct
    head = lambda rows, kind: shape((rows, HEAD_DIM), kind)
    return pl.pallas_call(
        functools.partial(front_kernel, capacity),
        name="front",
        out_shape=[
            shape((length, width), f32), shape((length, width), bf16), shape((16, length), f32),
            shape((32, width), f32), shape((8, 128), f32),
            shape((count, width), bf16), shape((width, 768), bf16), shape((256, width), bf16),
            head(count, bf16), head(count, bf16), head(count, bf16), head(count, bf16), head(count, bf16),
            head(count, bf16), head(count, f32), head(count, f32), head(2 * length, f32), head(2 * length, f32),
            shape((count, 256), bf16), shape((length, width), f32), shape((16, length), f32),
            shape((2, WIDE, width), f32), shape((width, inner), bf16), shape((WIDE, width), bf16),
            shape((8, group, width), bf16), shape((NZ, 3, shard, inner), bf16), shape((8, group, width), bf16), shape((8, NZ, 16, 2 * length), f32),
            shape((4, group, width), bf16), shape((2, width, inner), bf16),
        ],
        in_specs=[vmem] * 8 + [hbm] * 11,
        out_specs=[vmem] * 5 + [hbm] + [vmem] * 18 + [hbm] * 6,
        scratch_shapes=[
            pltpu.VMEM((2 * group, width), bf16), pltpu.VMEM((9, 8, 128), f32), pltpu.VMEM((32, width), bf16),
            pltpu.VMEM((3, 32, width), bf16),
            pltpu.VMEM((NZ, shard, inner), bf16), pltpu.VMEM((3, width, inner), bf16),
            pltpu.VMEM((3, WIDE, width), bf16), pltpu.VMEM((16, 2 * length), f32), pltpu.VMEM((2, width, inner), f32),
            pltpu.VMEM((2 * group, width), bf16), pltpu.VMEM((2 * group, width), bf16),
            pltpu.VMEM((2, NZ, 16, 2 * length), f32), pltpu.VMEM((NZ, 2 * SLOTS, length), bf16),
            pltpu.VMEM((NZ, 2 * SLOTS, width), bf16), pltpu.VMEM((NZ, 2 * SLOTS, width), bf16),
            pltpu.VMEM((group + final, width), bf16), pltpu.VMEM((4, final, width), bf16),
            pltpu.VMEM((group, width), bf16), pltpu.VMEM((2, group + final, width), bf16),
            pltpu.VMEM((3, final, width), bf16), pltpu.VMEM((NZ, length + 16, width), bf16),
            pltpu.VMEM((3, length + 16, width), bf16),
        ]
        + spread_sems(1) + spread_sems(1) + spread_sems(NZ, 1) + spread_sems() + spread_sems() + spread_sems() + spread_sems()
        + spread_sems()
        + [
            dma((3,)), dma((3,)), dma((6,)), dma((4,)), dma((4, 2)), dma((4,)),
            dma, dma((2, 3)), dma((2, 3)), dma((2,)), dma, dma((3,)), dma,
            dma((2, 3)), dma((4,)), dma((4,)), dma((3, NZ + 1)), dma((3, NZ + 1)), dma((3, 2)), dma((3, 2)), dma, dma,
        ]
        + plane_scratch(length, width)[3:],
        compiler_params=pltpu.CompilerParams(
            collective_id=1, has_side_effects=True, vmem_limit_bytes=62 * MIB
        ),
    )(*operands)


def backward_kernel(
    ypart, accout, dsgu, dsdn, db_ref, dg_ref, g_ref, x_ref, hidden_ref, b_ref, gates_ref, psum_ref, bound_ref, cos_ref, sin_ref,
    aall, wall, woall, q1, k1, v1, q2, k2, v2, att1, lse1, att2, lse2, mixed,
    out_ref, gtok_ref, small_ref, wfinal, wfinal2, wofinal, dgu, sfin, sdfin, yrecv,
    dhb, dhall, dm, dk, dv, cat, wst, wrecv, wsum, dwo, worecv, wosum, small4,
    sgm, sdm, sgs, sds, sgx, sdx, sgt, sgz, sdt, ybuf, ysend, yz, yhalf, yadd, wm, wpair, wrecv2, wsum2, *sems,
):
    f32, bf16 = jnp.float32, jnp.bfloat16
    c = lax.axis_index("ctx")
    z = lax.axis_index("fsdp")
    length, width = x_ref.shape
    count = aall.shape[0]
    shard = width // NZ
    quarter = c % 4
    mate = flip(c, 0, 0, 1)
    scale = HEAD_DIM**-0.5
    sems = list(sems)

    spread_h = halves(dhb, lambda o: dhall.at[o], take(sems, 7), c, z)
    spread_w = halves(wsum, lambda o: wfinal.at[o], take(sems, 7), c, z)
    spread_v = halves(wsum2, lambda o: wfinal2.at[o], take(sems, 7), c, z)
    wzs, wzr, wms, wmr, ozs, ozr, oxs, oxr, oms, omr, ss, sr = take(sems, 12)
    yxs, yxr, yzs, yzr, gas, gar, gal, sms, smr, sxs, sxr, szs, szr, ylsem, olsem, yasem = take(sems, 16)
    spread_s = halves(sgz, lambda o: sfin.at[o], take(sems, 7), c, z)
    spread_d = halves(sdt, lambda o: sdfin.at[o], take(sems, 7), c, z)
    reduce_refs = take(sems, 8)
    core = c % 2
    chip = c // 2
    sub = shard // 4
    part_rows = sdt.shape[0]

    half = ypart.shape[1] // 2
    upper, lower = slice(0, half), slice(half, 2 * half)
    x_chip, y_chip = flip(c, 0, 1, 0), flip(c, 1, 0, 0)

    def ycopy(i):
        src, dst, there = (
            (ypart.at[0, upper], yhalf.at[0], x_chip),
            (ypart.at[0, lower], yhalf.at[1], y_chip),
            (ypart.at[1, upper], yrecv.at[0, upper], x_chip),
            (ypart.at[2, lower], yrecv.at[1, lower], y_chip),
            (yadd.at[0], yrecv.at[1, upper], y_chip),
            (yadd.at[1], yrecv.at[0, lower], x_chip),
        )[i]
        return remote(src, dst, yxs.at[i], yxr.at[i], there, z)

    def ytake(i):
        src = (ypart.at[2, upper], ypart.at[1, lower])[i]
        return pltpu.make_async_copy(src, yadd.at[i], yasem.at[i])

    def yload(i):
        src = ypart.at[3] if i == 2 else yrecv.at[i]
        return pltpu.make_async_copy(src, ybuf.at[i], ylsem.at[i])

    def yhop(d):
        return remote(ysend.at[(z + d) % NZ], yz.at[d - 1], yzs.at[d - 1], yzr.at[d - 1], c, (z + d) % NZ)

    def gcopy(d):
        there = (z + d) % NZ
        return remote(
            accout.at[:, rows_at(there * shard, shard), :], dgu.at[z], gas.at[d - 1], gar.at[d - 1], c, there
        )

    gown = pltpu.make_async_copy(accout.at[:, rows_at(z * shard, shard), :], dgu.at[z], gal)

    def smate(i):
        if i == 0:
            return remote(dsgu.at[:, lanes_at((1 - core) * WIDE, WIDE)], sgm, sms.at[0], smr.at[0], mate, z)
        return remote(dsdn.at[rows_at((1 - core) * 4 * part_rows, 4 * part_rows)], sdm, sms.at[1], smr.at[1], mate, z)

    def schip(i, kind):
        there = flip(c, PEERS[i][0], PEERS[i][1], 0)
        if kind == 0:
            return remote(sgs.at[:, there // 2], sgx.at[i], sxs.at[i, 0], sxr.at[i, 0], there, z)
        return remote(sds.at[there // 2], sdx.at[i], sxs.at[i, 1], sxr.at[i, 1], there, z)

    def shop(d):
        there = (z + d) % NZ
        return remote(sgt.at[there], sgz.at[z], szs.at[d - 1], szr.at[d - 1], c, there)
    greet(c, z)
    packed = psum_ref[...]
    gain_one = packed[17:18]
    gain_two = packed[16:17]
    router = packed[0:16].astype(bf16)
    hidden = hidden_ref[...]
    factor_two = norm_factor(hidden)
    normed_two = hidden * factor_two
    gates = gates_ref[...]
    d_gates = dg_ref[...]
    d_logits = gates * (d_gates - jnp.sum(gates * d_gates, axis=0, keepdims=True))
    d_b = db_ref[...] + split_dot(d_logits, router, TN)
    small_ref[...] = jnp.zeros_like(small_ref)
    small_ref[0:16] = split_dot(d_logits, b_ref[...])
    small_ref[16:17] = jnp.sum(d_b * normed_two, axis=0, keepdims=True)
    pulled = d_b * gain_two
    d_hidden = g_ref[...].astype(f32) + factor_two * (
        pulled - normed_two * jnp.mean(pulled * normed_two, axis=1, keepdims=True)
    )
    dhb[...] = d_hidden.astype(bf16)
    spread_h.start_z()
    spread_h.start_x()
    smate(0).start()
    smate(1).start()
    gown.start()
    for d in range(1, NZ):
        gcopy(d).start()
    dk[...] = jnp.zeros_like(dk)
    dv[...] = jnp.zeros_like(dv)
    cat[:, 384:512] = jnp.zeros((count, 128), bf16)
    spread_h.relay_x()
    for i in range(4):
        ycopy(i).start()
    for i in range(2):
        ytake(i).start()
    spread_h.arrive()
    step = 2 * length
    for i in range(count // step):
        block = dhall[2 * i : 2 * i + 2].reshape(step, width)
        dm[i * step : (i + 1) * step] = dot(block, woall[...], NT).astype(bf16)
        part = dot(mixed[i * step : (i + 1) * step], block, TN)
        if i == 0:
            dwo[...] = part
        else:
            dwo[...] += part
    wosum[...] = dwo[...].astype(bf16).reshape(wosum.shape)

    def oz(j, owner):
        d = (owner + NZ - z) % NZ
        return remote(wosum.at[j], worecv.at[j, d - 1], ozs.at[j], ozr.at[j, d - 1], c, owner)

    def oz_wait(j, d):
        return remote(wosum.at[j], worecv.at[j, d], ozs.at[j], ozr.at[j, d], c, z)

    for j, (_, owner) in enumerate(head_rows(c)):

        @pl.when(owner != z)
        def _(j=j, owner=owner):
            oz(j, owner).start()

    for i in range(2):
        ycopy(i).wait_recv()
        ytake(i).wait()

        def yjoin(n, carry):
            part = rows_at(n * 16, 16)
            yadd[i, part] = (yadd[i, part].astype(f32) + yhalf[i, part].astype(f32)).astype(bf16)
            return carry

        lax.fori_loop(0, half // 16, yjoin, 0)
        ycopy(4 + i).start()
    smate(0).wait_recv()
    smate(1).wait_recv()
    for q in range(NZ):
        for j in range(4):
            part = slice(q * shard + j * sub, q * shard + (j + 1) * sub)
            own = dsgu[part, lanes_at(core * WIDE, WIDE)].astype(f32)
            sgs[q, j] = (own + sgm[part].astype(f32)).astype(bf16)
    for j in range(4):
        own = dsdn[rows_at(core * 4 * part_rows + j * part_rows, part_rows)].astype(f32)
        sds[j] = (own + sdm[j * part_rows : (j + 1) * part_rows].astype(f32)).astype(bf16)
    for i in range(3):
        schip(i, 0).start()
        schip(i, 1).start()
    boundary = bound_ref[0:1, 0:1]

    def pull_back(queries, first, keys, values, n, upper, out, lse, which):
        scores = dot(queries, keys[0:n], NT) * scale
        scores = jnp.where(visible(first, step, n, boundary), scores, negative)
        shares = jnp.exp(scores - lse[:, 0:1])
        delta = jnp.sum(upper.astype(f32) * out, axis=1, keepdims=True)
        pulled = (scale * (shares * (dot(upper, values[0:n], NT) - delta))).astype(bf16)
        dk[which, 0:n] += dot(pulled, queries, TN)
        dv[which, 0:n] += dot(shares.astype(bf16), upper, TN)
        return dot(pulled, keys[0:n]).astype(bf16).astype(f32)

    for i in range(count // step):
        part = slice(i * step, (i + 1) * step)
        got = pull_back(q1[part], i * step, k1, v1, (i + 1) * step, dm[part, 0:128], att1[part], lse1[part], 0)
        cat[part, 0:128] = turned(got, cos_ref[part], -sin_ref[part]).astype(bf16)
    mine = rows_at(quarter * step, step)
    got = pull_back(q2[mine], quarter * step, k2, v2, count, dm[mine, 128:256], att2[...], lse2[...], 1)
    cat[mine, 384:512] = turned(got, cos_ref[mine], -sin_ref[mine]).astype(bf16)
    for which in range(2):
        at = 384 * which
        keys = dk[which].astype(bf16).astype(f32)
        cat[:, at + 128 : at + 256] = turned(keys, cos_ref[...], -sin_ref[...]).astype(bf16)
        cat[:, at + 256 : at + 384] = dv[which].astype(bf16)
    for i in range(width // 256):
        wst[256 * i : 256 * i + 256] = dot(aall[:, 256 * i : 256 * i + 256], cat[...], TN).astype(bf16)

    def wz(d, second):
        there = (z + d) % NZ
        src = wpair.at[there] if second else wst.at[rows_at(there * shard, shard), 0:384]
        dst = wrecv2 if second else wrecv
        return remote(src, dst.at[d - 1], wzs.at[d - 1, second], wzr.at[d - 1, second], c, there)

    def wmate(q):
        rows = rows_at(q * shard + (1 - core) * (shard // 2), shard // 2)
        return remote(wst.at[rows, 384:768], wm.at[q], wms.at[q], wmr.at[q], mate, z)

    for q in range(NZ):
        wmate(q).start()
    for d in range(1, NZ):
        wz(d, 0).start()
    for q in range(NZ):
        wmate(q).wait_recv()
        own = wst[rows_at(q * shard + core * (shard // 2), shard // 2), 384:768].astype(f32)
        wpair[q] = (own + wm[q].astype(f32)).astype(bf16)
    for d in range(1, NZ):
        wz(d, 1).start()

    total_up = [sgs[q, chip].astype(f32) for q in range(NZ)]
    total_down = sds[chip].astype(f32)
    for i in range(3):
        schip(i, 0).wait_recv()
        schip(i, 1).wait_recv()
        for q in range(NZ):
            total_up[q] = total_up[q] + sgx[i, q].astype(f32)
        total_down = total_down + sdx[i].astype(f32)
    for q in range(NZ):
        sgt[q] = total_up[q].astype(bf16)
    sdt[...] = total_down.astype(bf16)
    sgz[z] = sgt[z]
    for d in range(1, NZ):
        shop(d).start()
    spread_d.start_z()
    spread_d.start_x()

    def ox(j, i):
        there = flip(c, PEERS[i][0], PEERS[i][1], 0)
        return remote(wosum.at[j], wofinal.at[c, j], oxs.at[j, i], oxr.at[j, i], there, z)

    def om(j, i):
        fy, fx = (((0, 0),) + PEERS)[i]
        origin = flip(c, fy, fx, 0)
        src = wosum.at[j] if i == 0 else wofinal.at[origin, j]
        return remote(src, wofinal.at[origin, j], oms.at[j, i], omr.at[j, i], mate, z)

    def wo_keep(j):
        return pltpu.make_async_copy(wosum.at[j], wofinal.at[c, j], olsem.at[j])

    for j, (_, owner) in enumerate(head_rows(c)):

        @pl.when(owner == z)
        def _(j=j):
            for d in range(3):
                oz_wait(j, d).wait_recv()
            total = wosum[j].astype(f32)
            for d in range(3):
                total = total + worecv[j, d].astype(f32)
            wosum[j] = total.astype(bf16)
            wo_keep(j).start()
            for i in range(3):
                ox(j, i).start()
            om(j, 0).start()

    value = plane_reduce(
        lambda o: dot(cat[rows_at(o * length, length)], wall[...], NT), c, z, reduce_refs
    )
    x = x_ref[...].astype(f32)
    factor_one = norm_factor(x)
    normed_one = x * factor_one
    small_ref[17:18] = jnp.sum(value * normed_one, axis=0, keepdims=True)
    pulled = value * gain_one
    gtok_ref[...] = (
        d_hidden
        + factor_one * (pulled - normed_one * jnp.mean(pulled * normed_one, axis=1, keepdims=True))
    ).astype(bf16)

    def exchange(stage, slots, targets):
        copies = [
            remote(small4.at[stage], small4.at[slot], ss.at[slot], sr.at[slot], tc, tz)
            for slot, (tc, tz) in zip(slots, targets)
        ]
        for copy in copies:
            copy.start()
        for copy in copies:
            copy.wait_recv()
        value = small4[stage]
        for slot in slots:
            value = value + small4[slot]
        return value, copies

    small4[0] = small_ref[...]
    value, sent = exchange(0, (1,), ((mate, z),))
    small4[2] = value
    value, more = exchange(2, (3, 4, 5), [(flip(c, fy, fx, 0), z) for fy, fx in PEERS])
    sent += more
    small4[6] = value
    window = lambda s: lanes_at(5 * s // 2 * 128, 384)
    last_hop = [
        remote(
            small4.at[6, :, window((z + d) % NZ)], small4.at[6 + d, :, window((z + d) % NZ)],
            ss.at[6 + d], sr.at[6 + d], c, (z + d) % NZ,
        )
        for d in range(1, NZ)
    ]
    last_wait = [
        remote(
            small4.at[6 + d, :, window(z)], small4.at[6 + d, :, window(z)], ss.at[6 + d], sr.at[6 + d], c, z
        )
        for d in range(1, NZ)
    ]
    for copy in last_hop:
        copy.start()
    yload(2).start()
    for i in range(2):
        ycopy(2 + i).wait_recv()
        ycopy(5 - i).wait_recv()
        yload(i).start()
    for d in range(1, NZ):
        shop_wait = sgz.at[(z + NZ - d) % NZ]
        remote(shop_wait, shop_wait, szs.at[d - 1], szr.at[d - 1], c, z).wait_recv()
    spread_s.start_z()
    spread_s.start_x()
    total = wst[rows_at(z * shard, shard), 0:384].astype(f32)
    for d in range(1, NZ):
        wz(d, 0).wait_recv()
        total = total + wrecv[d - 1].astype(f32)
    wsum[...] = total.astype(bf16)
    spread_w.start_z()
    spread_w.start_x()
    total = wpair[z].astype(f32)
    for d in range(1, NZ):
        wz(d, 1).wait_recv()
        total = total + wrecv2[d - 1].astype(f32)
    wsum2[...] = total.astype(bf16)
    spread_v.start_z()
    spread_v.start_x()

    for i in range(3):
        yload(i).wait()

    def ysum(i, carry):
        part = rows_at(i * 16, 16)
        value = ybuf[0, part].astype(f32)
        for k in range(1, 3):
            value = value + ybuf[k, part].astype(f32)
        ysend[i // (length // 16), rows_at(i % (length // 16) * 16, 16)] = value.astype(bf16)
        return carry

    lax.fori_loop(0, NZ * length // 16, ysum, 0)
    for d in range(1, NZ):
        yhop(d).start()

    for i in range(3):
        for j, (_, owner) in enumerate(head_rows(flip(c, PEERS[i][0], PEERS[i][1], 0))):

            @pl.when(owner == z)
            def _(j=j, i=i):
                origin = flip(c, PEERS[i][0], PEERS[i][1], 0)
                block = wofinal.at[origin, j]
                remote(block, block, oxs.at[j, i], oxr.at[j, i], c, z).wait_recv()
                om(j, i + 1).start()

    spread_w.relay_x()
    spread_v.relay_x()
    for i in range(4):
        fy, fx = (((0, 0),) + PEERS)[i]
        for j, (_, owner) in enumerate(head_rows(flip(c, fy, fx, 1))):

            @pl.when(owner == z)
            def _(j=j, i=i, fy=fy, fx=fx):
                block = wofinal.at[flip(c, fy, fx, 1), j]
                remote(block, block, oms.at[j, i], omr.at[j, i], c, z).wait_recv()

    value = small4[6, :, window(z)]
    for d in range(1, NZ):
        last_wait[d - 1].wait_recv()
        value = value + small4[6 + d, :, window(z)]
    small_ref[:, window(z)] = value
    spread_s.relay_x()
    spread_d.relay_x()
    value = hidden + ysend[z].astype(f32)
    for d in range(1, NZ):
        yhop(d).wait_recv()
        value = value + yz[d - 1].astype(f32)
    out_ref[...] = value.astype(bf16)
    spread_w.arrive()
    spread_v.arrive()
    spread_s.arrive()
    spread_d.arrive()
    gown.wait()
    for d in range(1, NZ):
        gcopy(d).wait()
        yhop(d).wait_send()
        shop(d).wait_send()
    for i in range(6):
        ycopy(i).wait_send()
    for i in range(3):
        schip(i, 0).wait_send()
        schip(i, 1).wait_send()
    smate(0).wait_send()
    smate(1).wait_send()
    for copy in sent + last_hop:
        copy.wait_send()
    for j, (_, owner) in enumerate(head_rows(c)):

        @pl.when(owner != z)
        def _(j=j, owner=owner):
            oz(j, owner).wait_send()

        @pl.when(owner == z)
        def _(j=j):
            for i in range(3):
                ox(j, i).wait_send()
            om(j, 0).wait_send()
            wo_keep(j).wait()

    for i in range(3):
        for j, (_, owner) in enumerate(head_rows(flip(c, PEERS[i][0], PEERS[i][1], 0))):

            @pl.when(owner == z)
            def _(j=j, i=i):
                om(j, i + 1).wait_send()

    for d in range(1, NZ):
        wz(d, 0).wait_send()
        wz(d, 1).wait_send()
    for q in range(NZ):
        wmate(q).wait_send()
    for spread in (spread_h, spread_w, spread_v, spread_s, spread_d):
        spread.drain()


def backward_stage(*operands):
    x, aall, dsdn = operands[7], operands[15], operands[3]
    length, width = x.shape
    count = aall.shape[0]
    shard = width // NZ
    sub = shard // 4
    part_rows = dsdn.shape[0] // 8
    dma = pltpu.SemaphoreType.DMA
    hbm = pl.BlockSpec(memory_space=pl.ANY)
    vmem = pl.BlockSpec(memory_space=pltpu.VMEM)
    f32, bf16 = jnp.float32, jnp.bfloat16
    shape = jax.ShapeDtypeStruct
    return pl.pallas_call(
        backward_kernel,
        name="backward",
        out_shape=[
            shape((length, width), bf16), shape((length, width), bf16), shape((32, width), f32),
            shape((8, shard, 384), bf16), shape((8, shard // 2, 384), bf16), shape((8, 4, 64, width), bf16), shape((NZ, 2, shard, 2 * WIDE), bf16),
            shape((8, NZ, sub, WIDE), bf16), shape((8, part_rows, width), bf16), shape((2, NZ * length, width), bf16),
        ],
        in_specs=[hbm] * 2 + [vmem] * (len(operands) - 2),
        out_specs=[vmem] * 3 + [hbm] * 7,
        scratch_shapes=[
            pltpu.VMEM((length, width), bf16), pltpu.VMEM((8, length, width), bf16), pltpu.VMEM((count, 256), bf16),
            pltpu.VMEM((2, count, 128), f32), pltpu.VMEM((2, count, 128), f32), pltpu.VMEM((count, 768), bf16),
            pltpu.VMEM((width, 768), bf16), pltpu.VMEM((3, shard, 384), bf16), pltpu.VMEM((shard, 384), bf16),
            pltpu.VMEM((256, width), f32), pltpu.VMEM((4, 3, 64, width), bf16),
            pltpu.VMEM((4, 64, width), bf16), pltpu.VMEM((10, 32, width), f32),
            pltpu.VMEM((width, WIDE), bf16), pltpu.VMEM((4 * part_rows, width), bf16),
            pltpu.VMEM((NZ, 4, sub, WIDE), bf16), pltpu.VMEM((4, part_rows, width), bf16),
            pltpu.VMEM((3, NZ, sub, WIDE), bf16), pltpu.VMEM((3, part_rows, width), bf16),
            pltpu.VMEM((NZ, sub, WIDE), bf16), pltpu.VMEM((NZ, sub, WIDE), bf16), pltpu.VMEM((part_rows, width), bf16),
            pltpu.VMEM((3, NZ * length, width), bf16), pltpu.VMEM((NZ, length, width), bf16),
            pltpu.VMEM((3, length, width), bf16), pltpu.VMEM((2, 2 * length, width), bf16),
            pltpu.VMEM((2, 2 * length, width), bf16), pltpu.VMEM((NZ, shard // 2, 384), bf16),
            pltpu.VMEM((NZ, shard // 2, 384), bf16), pltpu.VMEM((3, shard // 2, 384), bf16),
            pltpu.VMEM((shard // 2, 384), bf16),
        ]
        + spread_sems(2) + spread_sems(2) + spread_sems(2)
        + [
            dma((3, 2)), dma((3, 2)), dma((4,)), dma((4,)), dma((4,)), dma((4, 3)), dma((4, 3)), dma((4, 3)), dma((4, 4)), dma((4, 4)),
            dma((10,)), dma((10,)),
            dma((6,)), dma((6,)), dma((3,)), dma((3,)), dma((3,)), dma((3,)), dma, dma((2,)), dma((2,)),
            dma((3, 2)), dma((3, 2)), dma((3,)), dma((3,)), dma((4,)), dma((4,)), dma((2,)),
        ]
        + spread_sems(2) + spread_sems(2)
        + plane_scratch(length, width),
        compiler_params=pltpu.CompilerParams(
            collective_id=3, has_side_effects=True, vmem_limit_bytes=62 * MIB
        ),
    )(*operands)


def gather_kernel(
    wfinal, wfinal2, wofinal, dgu, sfin, sdfin, ddn, *refs
):
    gwq, gwk, gwv, gwo, gsg, gsu, gsd, geg, geu, ged = refs

    z = lax.axis_index("fsdp")
    f32, bf16 = jnp.float32, jnp.bfloat16
    hidden_dev = gsd.shape[0]
    sub = sfin.shape[2]
    units = geg.shape[2]
    for e in range(2):
        ged[e] = ddn[e, 0:hidden_dev]
    for o in range(8):
        start = 128 * (o % 2) + 32 * (o // 2)
        size = min(32, hidden_dev - start)
        if size > 0:
            gsd[start : start + size] = sdfin[o, 0:size].astype(f32)
    slot = lax.broadcasted_iota(jnp.int32, (WIDE, units), 0)
    unit = lax.broadcasted_iota(jnp.int32, (WIDE, units), 1)
    for q in range(NZ):
        put = jnp.where((unit == slot + q * hidden_dev) & (slot < hidden_dev), 1.0, 0.0).astype(bf16)
        for h, (ref, shared) in enumerate(((geg, gsg), (geu, gsu))):
            for e in range(2):
                part = dot(dgu[q, e, :, h * WIDE : (h + 1) * WIDE], put)
                if q == 0:
                    ref[e] = part
                else:
                    ref[e] += part
            for j in range(4):
                part = dot(sfin[2 * j + h, q], put)
                if q == 0:
                    shared[sub * j : sub * j + sub] = part
                else:
                    shared[sub * j : sub * j + sub] += part
    for n, ref in enumerate((gwq, gwk, gwv)):
        for o in range(8):
            ref[:, 128 * o : 128 * o + 128] = wfinal[o, :, 128 * n : 128 * n + 128].astype(f32)
        half = wfinal2.shape[1]
        lanes = slice(128 * n, 128 * n + 128)
        for y in range(2):
            for k in range(2):
                ref[half * k : half * k + half, 1024 + 128 * y : 1152 + 128 * y] = (
                    wfinal2[4 * y + k, :, lanes].astype(f32) + wfinal2[4 * y + 2 + k, :, lanes].astype(f32)
                )
    for i in range(5):
        b = 5 * z + i

        @pl.when(b < 16)
        def _(b=b, i=i):
            low = jnp.minimum(b, 15)
            gwo[64 * i : 64 * i + 64] = wofinal[low // 2, low % 2].astype(f32)

        @pl.when(b >= 16)
        def _(b=b, i=i):
            high = jnp.maximum(b, 16) - 16
            gwo[64 * i : 64 * i + 64] = sum(
                wofinal[4 * (high // 2) + k, 2 + high % 2].astype(f32) for k in range(4)
            )


def gather_stage(wfinal, wfinal2, wofinal, dgu, sfin, sdfin, ddn, hidden_dev):
    width = wofinal.shape[3]
    shard = wfinal.shape[1]
    units = NZ * hidden_dev
    f32 = jnp.float32
    shape = jax.ShapeDtypeStruct
    vmem = pl.BlockSpec(memory_space=pltpu.VMEM)
    square = shape((shard, width), f32)
    outs = [
        square, square, square, square, shape((shard, units), f32), shape((shard, units), f32),
        shape((hidden_dev, width), f32), shape((2, shard, units), f32), shape((2, shard, units), f32),
        shape((2, hidden_dev, width), f32),
    ]
    return pl.pallas_call(
        gather_kernel,
        name="assemble",
        out_shape=outs,
        in_specs=[vmem] * 7,
        out_specs=[vmem] * 10,
        compiler_params=pltpu.CompilerParams(vmem_limit_bytes=60 * MIB),
    )(wfinal, wfinal2, wofinal, dgu, sfin, sdfin, ddn)


def per_device_fast(
    tokens,
    documents,
    routes,
    priority,
    attention_gain,
    query_weight,
    key_weight,
    value_weight,
    output_weight,
    feedforward_gain,
    router_weight,
    shared_gate,
    shared_up,
    shared_down,
    expert_gate,
    expert_up,
    expert_down,
    cotangent,
):
    f32, bf16 = jnp.float32, jnp.bfloat16
    z = lax.axis_index("fsdp")
    length = tokens.shape[1]
    row_length = length * 8
    experts = EXP_DEV * 8
    capacity = 9 * length * TOPK // (8 * experts)
    shard = query_weight.shape[0]
    hidden_dev = expert_gate.shape[2] // NZ
    frequency = theta_base ** (-np.arange(HEAD_DIM // 2, dtype=np.float32) / (HEAD_DIM // 2))
    angles = np.arange(row_length, dtype=np.float32)[:, None] * frequency.astype(np.float32)[None, :]
    cosine, sine = np.cos(angles), np.sin(angles)
    cosine_wide = jnp.asarray(np.concatenate([cosine, cosine], axis=1), f32)
    sine_wide = jnp.asarray(np.concatenate([-sine, sine], axis=1), f32)
    gains = jnp.concatenate([feedforward_gain[None], attention_gain[None], jnp.zeros((14, shard), bf16)], axis=0)
    front = dict(
        zip(
            FRONT_OUT,
            front_stage(
                capacity, tokens[0], router_weight, gains, documents, routes[0], priority[0], cosine_wide, sine_wide,
                cotangent[0], query_weight, key_weight, value_weight, output_weight, expert_gate, expert_up,
                shared_gate, shared_up, expert_down, shared_down,
            ),
        )
    )
    kept = FRONT_OUT[5:19]
    output_rows, grad_tokens, small, wfinal, wfinal2, wofinal, dgu, sfin, sdfin = backward_stage(
        *[front[n] for n in ("ypart", "accout", "dsgu", "dsdn", "db", "dg")], cotangent[0], tokens[0],
        *[front[n] for n in ("hidden", "tokens", "gates", "psum", "bound")], cosine_wide, sine_wide,
        *[front[n] for n in kept]
    )[:9]
    gwq, gwk, gwv, gwo, gsg, gsu, gsd, geg, geu, ged = gather_stage(
        wfinal, wfinal2, wofinal, dgu, sfin, sdfin, front["ddn"], hidden_dev
    )
    mine = lax.dynamic_slice_in_dim(small, z * shard, shard, 1)
    return (
        output_rows[None], grad_tokens[None], mine[17], gwq, gwk, gwv, gwo, mine[16], mine[:16].T, gsg, gsu, gsd, geg,
        geu, ged,
    )


def per_device(
    tokens,
    documents,
    routes,
    priority,
    attention_gain,
    query_weight,
    key_weight,
    value_weight,
    output_weight,
    feedforward_gain,
    router_weight,
    shared_gate,
    shared_up,
    shared_down,
    expert_gate,
    expert_up,
    expert_down,
    cotangent,
):
    gathered = (
        lax.all_gather(attention_gain, "fsdp", axis=0, tiled=True),
        lax.all_gather(query_weight, "fsdp", axis=0, tiled=True),
        lax.all_gather(key_weight, "fsdp", axis=0, tiled=True),
        lax.all_gather(value_weight, "fsdp", axis=0, tiled=True),
        lax.all_gather(output_weight, "fsdp", axis=0, tiled=True),
        lax.all_gather(feedforward_gain, "fsdp", axis=0, tiled=True),
        lax.all_gather(router_weight, "fsdp", axis=0, tiled=True),
        lax.all_gather(shared_gate, "fsdp", axis=0, tiled=True),
        lax.all_gather(shared_up, "fsdp", axis=0, tiled=True),
        lax.all_gather(shared_down, "fsdp", axis=0, tiled=True),
        lax.all_gather(expert_gate, "fsdp", axis=1, tiled=True),
        lax.all_gather(expert_up, "fsdp", axis=1, tiled=True),
        lax.all_gather(expert_down, "fsdp", axis=1, tiled=True),
    )
    (
        gain_one,
        w_query,
        w_key,
        w_value,
        w_output,
        gain_two,
        w_router,
        w_shared_gate,
        w_shared_up,
        w_shared_down,
        w_expert_gate,
        w_expert_up,
        w_expert_down,
    ) = gathered
    groups = lax.axis_size("ctx")
    length = tokens.shape[1]
    row_length = length * groups
    experts = EXP_DEV * groups
    capacity = 9 * length * TOPK // (8 * experts)
    inner_width = HEADS * HEAD_DIM
    score_scale = HEAD_DIM ** (-0.5)
    spare_slot = experts * capacity
    first_here = lax.axis_index("ctx") * length
    positions = first_here + jnp.arange(length, dtype=jnp.int32)
    last_here = first_here + length - 1
    doc_here = documents[0].astype(jnp.float32)
    doc_wire = documents[0].astype(jnp.bfloat16)
    inputs = tokens[0].astype(jnp.float32)
    upstream_low = cotangent[0]
    upstream = upstream_low.astype(jnp.float32)
    factor_one = rms_factor(inputs)
    normed_one = inputs * factor_one
    gain_one_wide = gain_one.astype(jnp.float32)
    attn_input = (normed_one * gain_one_wide).astype(jnp.bfloat16)
    query_pre = jnp.dot(attn_input, w_query, preferred_element_type=jnp.float32).reshape(
        length, HEADS, HEAD_DIM
    )
    key_pre = jnp.dot(attn_input, w_key, preferred_element_type=jnp.float32).reshape(
        length, HEADS, HEAD_DIM
    )
    cosine, sine = rotary_tables(positions, HEAD_DIM // 2)
    queries = rotate(query_pre, cosine, sine).astype(jnp.bfloat16)
    key_rows = rotate(key_pre, cosine, sine).astype(jnp.bfloat16)
    value_rows = (
        jnp.dot(attn_input, w_value, preferred_element_type=jnp.float32)
        .astype(jnp.bfloat16)
        .reshape(length, HEADS, HEAD_DIM)
    )
    initial = (
        jnp.zeros((HEADS, length, HEAD_DIM), jnp.float32),
        jnp.full((HEADS, length), negative, jnp.float32),
        jnp.zeros((HEADS, length), jnp.float32),
    )
    key_all = lax.all_gather(key_rows, "ctx", axis=0, tiled=True)
    value_all = lax.all_gather(value_rows, "ctx", axis=0, tiled=True)
    docs_all = lax.all_gather(doc_wire, "ctx", axis=0, tiled=True)

    def visit(progress, within, rows_now):

        def compute(progress):
            accum, highest_seen, totals = progress
            key_block = lax.dynamic_slice_in_dim(key_all, within, rows_now, 0)
            value_block = lax.dynamic_slice_in_dim(value_all, within, rows_now, 0)
            docs_block = lax.dynamic_slice_in_dim(docs_all, within, rows_now, 0).astype(jnp.float32)
            key_pos = within + jnp.arange(rows_now, dtype=jnp.int32)
            allowed = allowed_mask(positions, doc_here, key_pos, docs_block)[None]
            scores = jnp.einsum(
                "qhd,khd->hqk", queries, key_block, preferred_element_type=jnp.float32
            )
            scores = jnp.where(allowed, scores * score_scale, negative)
            newest = jnp.maximum(highest_seen, jnp.max(scores, axis=-1))
            shrink = jnp.exp(highest_seen - newest)
            shares = jnp.exp(scores - newest[..., None]) * allowed
            totals = totals * shrink + jnp.sum(shares, axis=-1)
            accum = accum * shrink[..., None] + jnp.einsum(
                "hqk,khd->hqd",
                shares.astype(jnp.bfloat16),
                value_block,
                preferred_element_type=jnp.float32,
            )
            return (accum, newest, totals)

        return lax.cond(within > last_here, unchanged, compute, progress)

    accum, highest_seen, totals = blockwise(key_all.shape[0], visit, initial)
    attended = accum / totals[..., None]
    log_total = highest_seen + jnp.log(totals)
    mixed_rows = (
        jnp.transpose(attended, (1, 0, 2)).reshape(length, inner_width).astype(jnp.bfloat16)
    )
    hidden = inputs + jnp.dot(mixed_rows, w_output, preferred_element_type=jnp.float32)
    factor_two = rms_factor(hidden)
    normed_two = hidden * factor_two
    gain_two_wide = gain_two.astype(jnp.float32)
    moe_input = (normed_two * gain_two_wide).astype(jnp.bfloat16)
    moe_wide = moe_input.astype(jnp.float32)
    router_wide = w_router.astype(jnp.float32)
    gate_probs = jax.nn.softmax(jnp.dot(moe_wide, router_wide, precision=highest), axis=-1)
    route_now = routes[0]
    order_now = priority[0, 0]
    onehot = (route_now[:, :, None] == jnp.arange(experts, dtype=jnp.int32)).astype(jnp.float32)
    counts = jnp.sum(onehot, axis=1)
    earlier = (order_now[None, :] < order_now[:, None]).astype(jnp.bfloat16)
    before = jnp.dot(earlier, counts.astype(jnp.bfloat16), preferred_element_type=jnp.float32)
    ranking = jnp.sum(onehot * before[:, None, :], axis=-1).astype(jnp.int32)
    kept_mask = ranking < capacity
    slot_index = jnp.where(
        kept_mask,
        route_now % EXP_DEV * (groups * capacity) + route_now // EXP_DEV * capacity + ranking,
        spare_slot,
    )
    chosen = jnp.sum(onehot * gate_probs[:, None, :], axis=-1)
    weight = jnp.where(kept_mask, chosen, 0.0)
    flat_slots = slot_index.reshape(-1)
    copies = jnp.broadcast_to(moe_input[:, None, :], (length, TOPK, D)).reshape(length * TOPK, D)
    outgoing = jnp.zeros((spare_slot + 1, D), jnp.bfloat16).at[flat_slots].set(copies)[:spare_slot]
    arrived = lax.all_to_all(
        outgoing.reshape(EXP_DEV, groups, capacity, D),
        "ctx",
        split_axis=1,
        concat_axis=1,
        tiled=True,
    ).reshape(EXP_DEV, groups * capacity, D)
    gate_act = jnp.einsum(
        "erd,edf->erf", arrived, w_expert_gate, preferred_element_type=jnp.float32
    )
    up_act = jnp.einsum("erd,edf->erf", arrived, w_expert_up, preferred_element_type=jnp.float32)
    silu_gate, slope_gate = silu_parts(gate_act)
    expert_hidden = (silu_gate * up_act).astype(jnp.bfloat16)
    expert_out = jnp.einsum(
        "erf,efd->erd", expert_hidden, w_expert_down, preferred_element_type=jnp.float32
    ).astype(jnp.bfloat16)
    returned = lax.all_to_all(
        expert_out.reshape(EXP_DEV, groups, capacity, D),
        "ctx",
        split_axis=1,
        concat_axis=1,
        tiled=True,
    ).reshape(spare_slot, D)
    returned = jnp.concatenate([returned, jnp.zeros((1, D), jnp.bfloat16)], axis=0)
    picked = returned[slot_index]
    routed = jnp.sum(weight[..., None] * picked, axis=1)
    shared_gate_act = jnp.dot(moe_input, w_shared_gate, preferred_element_type=jnp.float32)
    shared_up_act = jnp.dot(moe_input, w_shared_up, preferred_element_type=jnp.float32)
    silu_shared, slope_shared = silu_parts(shared_gate_act)
    shared_hidden = (silu_shared * shared_up_act).astype(jnp.bfloat16)
    shared_out = jnp.dot(shared_hidden, w_shared_down, preferred_element_type=jnp.float32)
    output_rows = (hidden + shared_out + routed).astype(jnp.bfloat16)
    grad_shared_down = jnp.dot(shared_hidden.T, upstream_low, preferred_element_type=jnp.float32)
    grad_shared_hidden = jnp.dot(upstream_low, w_shared_down.T, preferred_element_type=jnp.float32)
    grad_shared_gate_act = (grad_shared_hidden * shared_up_act * slope_shared).astype(jnp.bfloat16)
    grad_shared_up_act = (grad_shared_hidden * silu_shared).astype(jnp.bfloat16)
    grad_shared_gate = jnp.dot(
        moe_input.T, grad_shared_gate_act, preferred_element_type=jnp.float32
    )
    grad_shared_up = jnp.dot(moe_input.T, grad_shared_up_act, preferred_element_type=jnp.float32)
    grad_moe = jnp.dot(
        grad_shared_gate_act, w_shared_gate.T, preferred_element_type=jnp.float32
    ) + jnp.dot(grad_shared_up_act, w_shared_up.T, preferred_element_type=jnp.float32)
    grad_copies = (
        (weight[..., None] * upstream[:, None, :]).astype(jnp.bfloat16).reshape(length * TOPK, D)
    )
    grad_weight = jnp.sum(picked.astype(jnp.float32) * upstream[:, None, :], axis=-1)
    grad_outgoing = (
        jnp.zeros((spare_slot + 1, D), jnp.bfloat16).at[flat_slots].set(grad_copies)[:spare_slot]
    )
    grad_arrived = lax.all_to_all(
        grad_outgoing.reshape(EXP_DEV, groups, capacity, D),
        "ctx",
        split_axis=1,
        concat_axis=1,
        tiled=True,
    ).reshape(EXP_DEV, groups * capacity, D)
    grad_expert_hidden = jnp.einsum(
        "erd,efd->erf", grad_arrived, w_expert_down, preferred_element_type=jnp.float32
    )
    grad_expert_down = jnp.einsum(
        "erf,erd->efd", expert_hidden, grad_arrived, preferred_element_type=jnp.float32
    )
    grad_gate_act = (grad_expert_hidden * up_act * slope_gate).astype(jnp.bfloat16)
    grad_up_act = (grad_expert_hidden * silu_gate).astype(jnp.bfloat16)
    grad_expert_gate = jnp.einsum(
        "erd,erf->edf", arrived, grad_gate_act, preferred_element_type=jnp.float32
    )
    grad_expert_up = jnp.einsum(
        "erd,erf->edf", arrived, grad_up_act, preferred_element_type=jnp.float32
    )
    grad_arrived_in = (
        jnp.einsum("erf,edf->erd", grad_gate_act, w_expert_gate, preferred_element_type=jnp.float32)
        + jnp.einsum("erf,edf->erd", grad_up_act, w_expert_up, preferred_element_type=jnp.float32)
    ).astype(jnp.bfloat16)
    sent_back = lax.all_to_all(
        grad_arrived_in.reshape(EXP_DEV, groups, capacity, D),
        "ctx",
        split_axis=1,
        concat_axis=1,
        tiled=True,
    ).reshape(spare_slot, D)
    sent_back = jnp.concatenate([sent_back, jnp.zeros((1, D), jnp.bfloat16)], axis=0)
    grad_moe = grad_moe + jnp.sum(sent_back[slot_index].astype(jnp.float32), axis=1)
    grad_chosen = jnp.where(kept_mask, grad_weight, 0.0)
    grad_probs = jnp.sum(onehot * grad_chosen[..., None], axis=1)
    grad_logits = gate_probs * (
        grad_probs - jnp.sum(gate_probs * grad_probs, axis=-1, keepdims=True)
    )
    grad_router = jnp.dot(moe_wide.T, grad_logits, precision=highest)
    grad_moe = grad_moe + jnp.dot(grad_logits, router_wide.T, precision=highest)
    grad_gain_two = jnp.sum(grad_moe * normed_two, axis=0)
    scaled_two = grad_moe * gain_two_wide
    grad_hidden = upstream + factor_two * (
        scaled_two - normed_two * jnp.mean(scaled_two * normed_two, axis=-1, keepdims=True)
    )
    grad_hidden_low = grad_hidden.astype(jnp.bfloat16)
    grad_output = jnp.dot(mixed_rows.T, grad_hidden_low, preferred_element_type=jnp.float32)
    grad_mixed = (
        jnp.dot(grad_hidden_low, w_output.T, preferred_element_type=jnp.float32)
        .astype(jnp.bfloat16)
        .reshape(length, HEADS, HEAD_DIM)
    )
    delta = jnp.einsum("qhd,hqd->hq", grad_mixed.astype(jnp.float32), attended)
    start_state = (
        jnp.zeros((length, HEADS, HEAD_DIM), jnp.float32),
        jnp.zeros((row_length, 2 * inner_width), jnp.float32),
    )
    back_key_all = lax.all_gather(key_rows, "ctx", axis=0, tiled=True)
    back_value_all = lax.all_gather(value_rows, "ctx", axis=0, tiled=True)
    back_docs_all = lax.all_gather(doc_wire, "ctx", axis=0, tiled=True)

    def visit(progress, within, rows_now):
        first_row = within

        def compute(progress):
            grad_query_acc, grad_kv_all = progress
            key_block = lax.dynamic_slice_in_dim(back_key_all, within, rows_now, 0)
            value_block = lax.dynamic_slice_in_dim(back_value_all, within, rows_now, 0)
            docs_block = lax.dynamic_slice_in_dim(back_docs_all, within, rows_now, 0).astype(
                jnp.float32
            )
            key_pos = first_row + jnp.arange(rows_now, dtype=jnp.int32)
            allowed = allowed_mask(positions, doc_here, key_pos, docs_block)[None]
            scores = jnp.einsum(
                "qhd,khd->hqk", queries, key_block, preferred_element_type=jnp.float32
            )
            scores = jnp.where(allowed, scores * score_scale, negative)
            shares = jnp.exp(scores - log_total[..., None]) * allowed
            grad_shares = jnp.einsum(
                "qhd,khd->hqk", grad_mixed, value_block, preferred_element_type=jnp.float32
            )
            grad_scores = (shares * (grad_shares - delta[..., None]) * score_scale).astype(
                jnp.bfloat16
            )
            grad_query_acc = grad_query_acc + jnp.einsum(
                "hqk,khd->qhd", grad_scores, key_block, preferred_element_type=jnp.float32
            )
            grad_key_rows = jnp.einsum(
                "hqk,qhd->khd", grad_scores, queries, preferred_element_type=jnp.float32
            ).reshape(rows_now, inner_width)
            grad_value_rows = jnp.einsum(
                "hqk,qhd->khd",
                shares.astype(jnp.bfloat16),
                grad_mixed,
                preferred_element_type=jnp.float32,
            ).reshape(rows_now, inner_width)
            current = lax.dynamic_slice_in_dim(grad_kv_all, first_row, rows_now, 0)
            grad_kv_all = lax.dynamic_update_slice_in_dim(
                grad_kv_all,
                current + jnp.concatenate([grad_key_rows, grad_value_rows], axis=1),
                first_row,
                0,
            )
            return (grad_query_acc, grad_kv_all)

        return lax.cond(first_row > last_here, unchanged, compute, progress)

    grad_query, grad_kv_all = blockwise(back_key_all.shape[0], visit, start_state)
    grad_kv = lax.psum_scatter(
        grad_kv_all.astype(jnp.bfloat16), "ctx", scatter_dimension=0, tiled=True
    ).astype(jnp.float32)
    grad_query_low = (
        unrotate(grad_query.astype(jnp.bfloat16).astype(jnp.float32), cosine, sine)
        .astype(jnp.bfloat16)
        .reshape(length, inner_width)
    )
    grad_key_turned = (
        grad_kv[:, :inner_width]
        .reshape(length, HEADS, HEAD_DIM)
        .astype(jnp.bfloat16)
        .astype(jnp.float32)
    )
    grad_key_low = (
        unrotate(grad_key_turned, cosine, sine).astype(jnp.bfloat16).reshape(length, inner_width)
    )
    grad_value_low = grad_kv[:, inner_width:].astype(jnp.bfloat16)
    grad_wquery = jnp.dot(attn_input.T, grad_query_low, preferred_element_type=jnp.float32)
    grad_wkey = jnp.dot(attn_input.T, grad_key_low, preferred_element_type=jnp.float32)
    grad_wvalue = jnp.dot(attn_input.T, grad_value_low, preferred_element_type=jnp.float32)
    grad_attn = (
        jnp.dot(grad_query_low, w_query.T, preferred_element_type=jnp.float32)
        + jnp.dot(grad_key_low, w_key.T, preferred_element_type=jnp.float32)
        + jnp.dot(grad_value_low, w_value.T, preferred_element_type=jnp.float32)
    )
    grad_gain_one = jnp.sum(grad_attn * normed_one, axis=0)
    scaled_one = grad_attn * gain_one_wide
    grad_inputs = grad_hidden + factor_one * (
        scaled_one - normed_one * jnp.mean(scaled_one * normed_one, axis=-1, keepdims=True)
    )
    owned = (
        lax.psum_scatter(
            grad_gain_one.astype(jnp.bfloat16), "fsdp", scatter_dimension=0, tiled=True
        ).astype(jnp.float32),
        lax.psum_scatter(
            grad_wquery.astype(jnp.bfloat16), "fsdp", scatter_dimension=0, tiled=True
        ).astype(jnp.float32),
        lax.psum_scatter(
            grad_wkey.astype(jnp.bfloat16), "fsdp", scatter_dimension=0, tiled=True
        ).astype(jnp.float32),
        lax.psum_scatter(
            grad_wvalue.astype(jnp.bfloat16), "fsdp", scatter_dimension=0, tiled=True
        ).astype(jnp.float32),
        lax.psum_scatter(
            grad_output.astype(jnp.bfloat16), "fsdp", scatter_dimension=0, tiled=True
        ).astype(jnp.float32),
        lax.psum_scatter(
            grad_gain_two.astype(jnp.bfloat16), "fsdp", scatter_dimension=0, tiled=True
        ).astype(jnp.float32),
        lax.psum_scatter(
            grad_router.astype(jnp.bfloat16), "fsdp", scatter_dimension=0, tiled=True
        ).astype(jnp.float32),
        lax.psum_scatter(
            grad_shared_gate.astype(jnp.bfloat16), "fsdp", scatter_dimension=0, tiled=True
        ).astype(jnp.float32),
        lax.psum_scatter(
            grad_shared_up.astype(jnp.bfloat16), "fsdp", scatter_dimension=0, tiled=True
        ).astype(jnp.float32),
        lax.psum_scatter(
            grad_shared_down.astype(jnp.bfloat16), "fsdp", scatter_dimension=0, tiled=True
        ).astype(jnp.float32),
        lax.psum_scatter(
            grad_expert_gate.astype(jnp.bfloat16), "fsdp", scatter_dimension=1, tiled=True
        ).astype(jnp.float32),
        lax.psum_scatter(
            grad_expert_up.astype(jnp.bfloat16), "fsdp", scatter_dimension=1, tiled=True
        ).astype(jnp.float32),
        lax.psum_scatter(
            grad_expert_down.astype(jnp.bfloat16), "fsdp", scatter_dimension=1, tiled=True
        ).astype(jnp.float32),
    )
    (
        own_gain_one,
        own_wquery,
        own_wkey,
        own_wvalue,
        own_output,
        own_gain_two,
        own_router,
        own_shared_gate,
        own_shared_up,
        own_shared_down,
        own_expert_gate,
        own_expert_up,
        own_expert_down,
    ) = owned
    dense = (
        lax.psum(own_gain_one.astype(jnp.bfloat16), "ctx").astype(jnp.float32),
        lax.psum(own_wquery.astype(jnp.bfloat16), "ctx").astype(jnp.float32),
        lax.psum(own_wkey.astype(jnp.bfloat16), "ctx").astype(jnp.float32),
        lax.psum(own_wvalue.astype(jnp.bfloat16), "ctx").astype(jnp.float32),
        lax.psum(own_output.astype(jnp.bfloat16), "ctx").astype(jnp.float32),
        lax.psum(own_gain_two.astype(jnp.bfloat16), "ctx").astype(jnp.float32),
        lax.psum(own_router.astype(jnp.bfloat16), "ctx").astype(jnp.float32),
        lax.psum(own_shared_gate.astype(jnp.bfloat16), "ctx").astype(jnp.float32),
        lax.psum(own_shared_up.astype(jnp.bfloat16), "ctx").astype(jnp.float32),
        lax.psum(own_shared_down.astype(jnp.bfloat16), "ctx").astype(jnp.float32),
    )
    return (
        output_rows[None],
        grad_inputs.astype(jnp.bfloat16)[None],
        dense[0],
        dense[1],
        dense[2],
        dense[3],
        dense[4],
        dense[5],
        dense[6],
        dense[7],
        dense[8],
        dense[9],
        own_expert_gate,
        own_expert_up,
        own_expert_down,
    )


def solution(mesh):
    fast = mesh.shape['ctx'] == 8 and mesh.shape['fsdp'] == NZ
    body = per_device_fast if fast else per_device
    return jax.shard_map(
        body,
        mesh=mesh,
        in_specs=(
            P("fsdp", "ctx", None),
            P("fsdp", "ctx"),
            P("fsdp", "ctx", None),
            P("fsdp", "ctx", None),
            P("fsdp"),
            P("fsdp", None),
            P("fsdp", None),
            P("fsdp", None),
            P("fsdp", None),
            P("fsdp"),
            P("fsdp", None),
            P("fsdp", None),
            P("fsdp", None),
            P("fsdp", None),
            P("ctx", "fsdp", None),
            P("ctx", "fsdp", None),
            P("ctx", "fsdp", None),
            P("fsdp", "ctx", None),
        ),
        out_specs=(
            P("fsdp", "ctx", None),
            P("fsdp", "ctx", None),
            P("fsdp"),
            P("fsdp", None),
            P("fsdp", None),
            P("fsdp", None),
            P("fsdp", None),
            P("fsdp"),
            P("fsdp", None),
            P("fsdp", None),
            P("fsdp", None),
            P("fsdp", None),
            P("ctx", "fsdp", None),
            P("ctx", "fsdp", None),
            P("ctx", "fsdp", None),
        ),
        check_vma=False,
    )
```
